32 devices in a mesh: expert: 16 (over z, x, core), dp: 2 (over y).
Axes of the slice: x: 2, y: 2, z: 4, core: 2. Of those that a mesh axis runs over, the one named last changes fastest.
Arguments:
- tokens: bfloat16 [1792, 2048], P(('expert', 'dp')), may hold values from -6 to 6
- cotangent: bfloat16 [1792, 2048], P(('expert', 'dp')), may hold values from -6 to 6
- expert_ids: int32 [1792, 8], P(('expert', 'dp')), may hold values from 0 to 15, all different within a row; in each aligned block of 56 rows (0 to 55, 56 to 111, ...) at most 35 rows name the same one
- combine: bfloat16 [1792, 8], P(('expert', 'dp')), may hold values from 0.019897461 to 0.5
- gate_up: bfloat16 [16, 2048, 1536], P('expert'), may hold values from -0.125 to 0.125
- down_proj: bfloat16 [16, 2048, 768], P('expert'), may hold values from -0.21875 to 0.21875
Outputs:
- grad_tokens: bfloat16 [1792, 2048], P(('expert', 'dp'))
- grad_combine: bfloat16 [1792, 8], P(('expert', 'dp'))
- grad_gate_up: bfloat16 [16, 2048, 1536], P('expert', 'dp')
- grad_down: bfloat16 [16, 2048, 768], P('expert', 'dp')
The draws below stay inside these ranges and needn't reach their ends.
Inputs may be any that keep to these rules, and one draw needn't show every extreme that they name: `expert_ids`: each token names 8 different experts. Among the 56 tokens of one device (aligned blocks of rows) no expert is named more than 35 times, and in every draw some device names some expert exactly 35 times.
All inputs are finite; a program needn't handle non-finite values.
Results may differ from the reference program's by a relative error of at most 0.015.
Values may be sent and summed in bfloat16 or wider, within the bound.
No kernel may reach another device: no remote copies, remote signals or barrier semaphores. Data moves between devices by JAX's collectives and lax.ppermute only.
A program may use at most 128 MiB of HBM per device.

```python
import math
import jax
import jax.numpy as jnp
import numpy as np
from jax import lax

D = 2048
H = 768
TOP = 8
TOK_DEV = 56
EXPERTS = 16
CAP = 35
TOKENS = 1792
N_EXPERT = 16
N_DP = 2


def levels(stream_key, dims, cuts, low, high):
    gain = 1.0
    for position, blocks in cuts:
        steps = jax.random.uniform(jax.random.fold_in(jax.random.fold_in(stream_key, 6), position), (blocks,), jnp.float32, low / len(cuts), high / len(cuts))
        gain = gain * jnp.repeat(jnp.exp(steps), dims[position] // blocks).reshape((-1,) + (1,) * (len(dims) - 1 - position))
    return gain


def shared_out(stream_key, own, number, rows, amount, top, bound, skew):
    ranking = jax.random.permutation(stream_key, amount)
    crowded, usual = load_shares(amount, rows * top, bound, skew, True), load_shares(amount, rows * top, bound, skew, False)
    places = jnp.arange(amount)

    def named(lengths, offset_by):
        used = int((lengths > 0).sum())
        fixed = max(1, used // 4)
        passed = fixed + (places - fixed + offset_by * (used - fixed)) % max(1, amount - fixed)
        return jnp.zeros((amount,), jnp.int32).at[ranking[jnp.where(places < fixed, places, passed)]].set(jnp.asarray(lengths, jnp.int32))

    lengths = jnp.where(number % 4 == 0, named(crowded, number // 4), named(usual, number - number // 4 - 1))
    mixed = jax.random.permutation(jax.random.fold_in(own, 3), amount)
    donor, taker = mixed[0:amount // 2 * 2:2], mixed[1:amount // 2 * 2:2]
    slack = jnp.minimum(lengths[donor] - 1, bound - lengths[taker]) // 2
    slack = jnp.where((donor == ranking[0]) | (taker == ranking[0]) | (lengths[taker] == 0), 0, jnp.maximum(slack, 0))
    passed = jax.random.randint(jax.random.fold_in(own, 4), (amount // 2,), 0, 1 << 20) % (slack + 1)
    lengths = lengths.at[donor].add(-passed).at[taker].add(passed)
    labels = jnp.searchsorted(jnp.cumsum(lengths), jnp.arange(rows * top), side="right").astype(jnp.int32)
    listing = labels.reshape(top, rows).T
    listing = listing[jax.random.permutation(jax.random.fold_in(own, 1), rows)]
    offset_by = jax.random.randint(jax.random.fold_in(own, 2), (rows, 1), 0, top)
    return jnp.take_along_axis(listing, (jnp.arange(top)[None, :] + offset_by) % top, axis=1)


def load_shares(number_of, total, most, skew, full):
    weights = [(1 << 20) // math.isqrt(rank ** skew) + 1 for rank in range(1, number_of + 1)]
    largest = most if full else min(most, max(-(-total // number_of), total * weights[0] // sum(weights)))
    least = 1 if total - largest >= number_of - 1 else 0
    given, surplus = [largest] + [least] * (number_of - 1), total - largest - least * (number_of - 1)
    while surplus > 0:
        free = [i for i in range(1, number_of) if given[i] < largest] or [i for i in range(1, number_of) if given[i] < most]
        mass, budget = sum([weights[i] for i in free]), surplus
        for i in free:
            more = min(most - given[i], max(1, budget * weights[i] // mass), surplus)
            given[i] = given[i] + more
            surplus = surplus - more
    return np.array(given)


def noise(own_key, extent, width, most, cuts=(), kind=jnp.bfloat16):
    array = jax.random.normal(own_key, extent, jnp.float32) * width
    if len(cuts) > 0:
        array = levels(own_key, extent, cuts, -0.22, 0.18) * array
    return jnp.clip(array, min=-most, max=most).astype(kind)


def setup_inputs(seed: int = 0) -> dict:
    key_of = jax.random.split(jax.random.key(seed), 7)
    tokens = noise(key_of[0], (TOKENS, D), 1.0, 6.0, ((0, 32),))
    cotangent = noise(key_of[1], (TOKENS, D), 1.0, 6.0, ((0, 32),))
    expert_ids_keys = jax.random.split(jax.random.fold_in(key_of[2], 1), TOKENS // TOK_DEV)
    expert_ids_turns = jax.random.permutation(jax.random.fold_in(key_of[2], 3), TOKENS // TOK_DEV)
    expert_ids = jax.vmap(lambda own, number: shared_out(jax.random.fold_in(key_of[2], 2), own, number, TOK_DEV, EXPERTS, TOP, CAP, 2))(expert_ids_keys, expert_ids_turns).reshape((TOKENS, TOP))
    combine = jnp.clip(jnp.exp(math.log(0.5) - 3.224016 * jax.random.uniform(key_of[3], (TOKENS, TOP), jnp.float32) ** levels(key_of[3], (TOKENS, TOP), ((0, 32),), -0.2, 0.2)), 0.019897461, 0.5).astype(jnp.bfloat16)
    gate_up = noise(key_of[4], (EXPERTS, D, 2 * H), D ** -0.5, 0.125, ((0, 16),))
    down_proj = noise(key_of[5], (EXPERTS, D, H), H ** -0.5, 0.21875, ((0, 16),))
    return dict(tokens=tokens, cotangent=cotangent, expert_ids=expert_ids, combine=combine, gate_up=gate_up, down_proj=down_proj)


def expert_pass(in_rows, cot_rows, weight_rows, w_in, w_out):
    hidden = w_out.shape[1]
    both = jnp.dot(in_rows, w_in, preferred_element_type=jnp.float32)
    gate = both[:, :hidden]
    upper = both[:, hidden:]
    sigma = jax.nn.sigmoid(gate)
    swish = gate * sigma
    activ = (swish * upper).astype(jnp.bfloat16)
    expert_out = lax.dot_general(activ, w_out, (((1,), (1,)), ((), ())), preferred_element_type=jnp.float32).astype(jnp.bfloat16)
    inner = jnp.sum(cot_rows.astype(jnp.float32) * expert_out.astype(jnp.float32), axis=1).astype(jnp.bfloat16)
    grad_rows = (weight_rows[:, None].astype(jnp.float32) * cot_rows.astype(jnp.float32)).astype(jnp.bfloat16)
    grad_act = jnp.dot(grad_rows, w_out, preferred_element_type=jnp.float32)
    grad_gate = grad_act * upper * sigma * (1.0 + gate * (1.0 - sigma))
    grad_upper = grad_act * swish
    grad_both = jnp.concatenate([grad_gate, grad_upper], axis=1).astype(jnp.bfloat16)
    row_grad = lax.dot_general(grad_both, w_in, (((1,), (1,)), ((), ())), preferred_element_type=jnp.float32).astype(jnp.bfloat16)
    grad_in_w = lax.dot_general(in_rows, grad_both, (((0,), (0,)), ((), ())), preferred_element_type=jnp.float32)
    grad_out_w = lax.dot_general(grad_rows, activ, (((0,), (0,)), ((), ())), preferred_element_type=jnp.float32)
    return row_grad, inner, grad_in_w, grad_out_w


def reference(tokens, cotangent, expert_ids, combine, gate_up, down_proj):
    pair_count = TOKENS * TOP
    most_rows = N_EXPERT * N_DP * CAP
    flat_ids = expert_ids.reshape(-1).astype(jnp.int32)
    order = jnp.argsort(flat_ids, stable=True).astype(jnp.int32)
    counts = jnp.bincount(flat_ids, length=EXPERTS).astype(jnp.int32)
    offsets = (jnp.cumsum(counts) - counts).astype(jnp.int32)
    padded = jnp.concatenate([order, jnp.zeros((most_rows,), jnp.int32)])
    flat_comb = combine.reshape(-1)

    def one_expert(carry, inputs):
        grad_acc, inner_acc = carry
        expert, w_in, w_out = inputs
        first_row = offsets[expert]
        picked = lax.dynamic_slice_in_dim(padded, first_row, most_rows)
        valid = jnp.arange(most_rows, dtype=jnp.int32) < counts[expert]
        pair_idx = jnp.where(valid, picked, 0).astype(jnp.int32)
        token_idx = (pair_idx // TOP).astype(jnp.int32)
        in_rows = jnp.where(valid[:, None], tokens[token_idx], jnp.zeros((), jnp.bfloat16))
        cot_rows = jnp.where(valid[:, None], cotangent[token_idx], jnp.zeros((), jnp.bfloat16))
        weight_rows = jnp.where(valid, flat_comb[pair_idx], jnp.zeros((), jnp.bfloat16))
        row_grad, inner, grad_in_w, grad_out_w = expert_pass(in_rows, cot_rows, weight_rows, w_in, w_out)
        grad_acc = grad_acc.at[token_idx].add(jnp.where(valid[:, None], row_grad.astype(jnp.float32), jnp.zeros((), jnp.float32)))
        target = jnp.where(valid, pair_idx, pair_count).astype(jnp.int32)
        inner_acc = inner_acc.at[target].set(inner.astype(jnp.float32))
        return (grad_acc, inner_acc), (grad_in_w.astype(jnp.bfloat16), grad_out_w.astype(jnp.bfloat16))

    start = (jnp.zeros((TOKENS, D), jnp.float32), jnp.zeros((pair_count + 1,), jnp.float32))
    (grad_acc, inner_acc), (grad_gate_up, grad_down) = lax.scan(one_expert, start, (jnp.arange(EXPERTS, dtype=jnp.int32), gate_up, down_proj))
    grad_tokens = grad_acc.astype(jnp.bfloat16)
    grad_combine = inner_acc[:pair_count].reshape(TOKENS, TOP).astype(jnp.bfloat16)
    return (grad_tokens, grad_combine, grad_gate_up, grad_down)
```

```python
import jax
import jax.numpy as jnp
from jax import lax
from jax.sharding import PartitionSpec as P

LANES = 128
GATHER_BYTES = 16 << 20


def shards(tokens, cotangent, expert_ids, combine, gate_up, down_proj):
    tok_rows, width = tokens.shape
    experts = lax.axis_size("expert")
    groups = lax.axis_size("dp")
    hidden = down_proj.shape[2]
    me = lax.axis_index("expert")
    mine = lax.axis_index("dp")
    w_in = gate_up[0]
    w_out = down_proj[0]
    extra = -(-experts // LANES) * LANES
    lanes = jnp.arange(extra, dtype=jnp.int32)

    picks = expert_ids[:, :, None] == lanes
    table = jnp.sum(
        jnp.where(picks, combine.astype(jnp.float32)[:, :, None], 0.0), axis=1
    ).astype(jnp.bfloat16)
    wide = jnp.concatenate([tokens, table], axis=1)

    whole = experts * groups * tok_rows * width * 2 <= GATHER_BYTES
    axes = ("expert", "dp") if whole else ("expert",)
    all_wide = lax.all_gather(wide, axes, axis=0, tiled=True)
    all_cot = lax.all_gather(cotangent, axes, axis=0, tiled=True)
    all_tok = all_wide[:, :width]
    weight = jnp.sum(
        jnp.where(lanes[None, :] == me, all_wide[:, width:].astype(jnp.float32), 0.0),
        axis=1,
        keepdims=True,
    )

    both = jnp.dot(all_tok, w_in, preferred_element_type=jnp.float32)
    gate, upper = both[:, :hidden], both[:, hidden:]
    sigma = jax.nn.sigmoid(gate)
    swish = gate * sigma
    activ = swish * upper
    cot_down = jnp.dot(all_cot, w_out, preferred_element_type=jnp.float32)
    inner = jnp.sum(activ * cot_down, axis=1)
    grad_act = weight * cot_down
    grad_gate = grad_act * upper * sigma * (1.0 + gate * (1.0 - sigma))
    grad_both = jnp.concatenate([grad_gate, grad_act * swish], axis=1).astype(jnp.bfloat16)
    scaled = (weight * activ).astype(jnp.bfloat16)

    def own_rows(array):
        if not whole:
            return array
        parts = array.reshape(experts, groups, tok_rows, -1)
        return lax.dynamic_index_in_dim(parts, mine, 1, False).reshape(experts * tok_rows, -1)

    row_grad = lax.dot_general(
        own_rows(grad_both), w_in, (((1,), (1,)), ((), ())), preferred_element_type=jnp.float32
    ).astype(jnp.bfloat16)
    inner_table = jnp.where(lanes[None, :] == me, own_rows(inner[:, None]), 0.0)
    returned = lax.psum_scatter(
        jnp.concatenate([row_grad, inner_table.astype(jnp.bfloat16)], axis=1),
        "expert",
        scatter_dimension=0,
        tiled=True,
    )
    grad_tokens = returned[:, :width]
    inner_back = returned[:, width:]
    grad_combine = jnp.sum(
        jnp.where(picks, inner_back.astype(jnp.float32)[:, None, :], 0.0), axis=2
    ).astype(jnp.bfloat16)

    part = width // groups

    def own_columns(array):
        return lax.dynamic_slice_in_dim(array, mine * part, part, axis=1)

    def outer(rows, columns):
        return lax.dot_general(
            rows, columns, (((0,), (0,)), ((), ())), preferred_element_type=jnp.float32
        ).astype(jnp.bfloat16)[None]

    if whole:
        grad_gate_up = outer(own_columns(all_tok), grad_both)
        grad_down = outer(own_columns(all_cot), scaled)
    else:
        grad_gate_up = lax.psum_scatter(
            outer(all_tok, grad_both), "dp", scatter_dimension=1, tiled=True
        )
        grad_down = lax.psum_scatter(
            outer(all_cot, scaled), "dp", scatter_dimension=1, tiled=True
        )
    return (grad_tokens, grad_combine, grad_gate_up, grad_down)


def solution(mesh):
    in_specs = (
        P(("expert", "dp"), None),
        P(("expert", "dp"), None),
        P(("expert", "dp"), None),
        P(("expert", "dp"), None),
        P("expert", None, None),
        P("expert", None, None),
    )
    out_specs = (
        P(("expert", "dp"), None),
        P(("expert", "dp"), None),
        P("expert", "dp", None),
        P("expert", "dp", None),
    )
    return jax.shard_map(shards, mesh=mesh, in_specs=in_specs, out_specs=out_specs, check_vma=False)
```

```python
import jax
import jax.numpy as jnp
from jax import lax
from jax.sharding import PartitionSpec as P

LANES = 128
CORES = 2
GATHER_BYTES = 16 << 20


def weight_table(expert_ids, combine, experts):
    lanes = jnp.arange(-(-experts // LANES) * LANES, dtype=jnp.int32)
    picks = expert_ids[:, :, None] == lanes
    table = jnp.sum(jnp.where(picks, combine.astype(jnp.float32)[:, :, None], 0.0), axis=1)
    return table.astype(jnp.bfloat16), picks, lanes


def rows_pass(rows, w_in, w_out, me, lanes, with_grad):
    width, hidden = w_out.shape
    tok, cot = rows[:, :width], rows[:, width : 2 * width]
    weight = jnp.sum(
        jnp.where(lanes[None, :] == me, rows[:, 2 * width :].astype(jnp.float32), 0.0),
        axis=1,
        keepdims=True,
    )
    both = jnp.dot(tok, w_in, preferred_element_type=jnp.float32)
    gate, upper = both[:, :hidden], both[:, hidden:]
    sigma = jax.nn.sigmoid(gate)
    swish = gate * sigma
    activ = swish * upper
    cot_down = jnp.dot(cot, w_out, preferred_element_type=jnp.float32)
    grad_act = weight * cot_down
    grad_gate = grad_act * upper * sigma * (1.0 + gate * (1.0 - sigma))
    grad_both = jnp.concatenate([grad_gate, grad_act * swish], axis=1).astype(jnp.bfloat16)
    scaled = (weight * activ).astype(jnp.bfloat16)
    if not with_grad:
        return grad_both, scaled, None
    inner = jnp.sum(activ * cot_down, axis=1, keepdims=True)
    row_grad = lax.dot_general(
        grad_both, w_in, (((1,), (1,)), ((), ())), preferred_element_type=jnp.float32
    ).astype(jnp.bfloat16)
    inner_table = jnp.where(lanes[None, :] == me, inner, 0.0).astype(jnp.bfloat16)
    return grad_both, scaled, jnp.concatenate([row_grad, inner_table], axis=1)


def outer(rows, columns):
    return lax.dot_general(
        rows, columns, (((0,), (0,)), ((), ())), preferred_element_type=jnp.float32
    ).astype(jnp.bfloat16)


def pick_inner(back, picks):
    return jnp.sum(jnp.where(picks, back.astype(jnp.float32)[:, None, :], 0.0), axis=2).astype(
        jnp.bfloat16
    )


def grouped(tokens, cotangent, expert_ids, combine, gate_up, down_proj):
    width = tokens.shape[1]
    me = lax.axis_index("expert")
    table, picks, lanes = weight_table(expert_ids, combine, lax.axis_size("expert"))
    rows = lax.all_gather(
        jnp.concatenate([tokens, cotangent, table], axis=1), "expert", axis=0, tiled=True
    )
    grad_both, scaled, back = rows_pass(rows, gate_up[0], down_proj[0], me, lanes, True)
    back = lax.psum_scatter(back, "expert", scatter_dimension=0, tiled=True)

    def share(term):
        return lax.psum_scatter(term, "dp", scatter_dimension=0, tiled=True)[None]

    return (
        back[:, :width],
        pick_inner(back[:, width:], picks),
        share(outer(rows[:, :width], grad_both)),
        share(outer(rows[:, width : 2 * width], scaled)),
    )


def streamed(tokens, cotangent, expert_ids, combine, gate_up, down_proj):
    width = tokens.shape[1]
    experts = lax.axis_size("expert")
    me = lax.axis_index("expert")
    mine = lax.axis_index("dp")
    w_in, w_out = gate_up[0], down_proj[0]
    table, picks, lanes = weight_table(expert_ids, combine, experts)

    chips = experts // CORES
    n_x = 1
    while 4 * n_x * n_x <= chips:
        n_x *= 2
    n_z = chips // n_x
    assert n_x == 2 and lax.axis_size("dp") == 2

    def place(z, x, core):
        return (z * n_x + x) * CORES + core

    spots = [(z, x, c) for z in range(n_z) for x in range(n_x) for c in range(CORES)]
    up_z = [(place(z, x, c), place((z + 1) % n_z, x, c)) for z, x, c in spots]
    over_x = [(place(z, x, c), place(z, 1 - x, c)) for z, x, c in spots]
    over_core = [(place(z, x, c), place(z, x, 1 - c)) for z, x, c in spots]

    def z_hop(a):
        return lax.ppermute(a, "expert", up_z)

    def x_hop(a):
        return lax.ppermute(a, "expert", over_x)

    def core_hop(a):
        return lax.ppermute(a, "expert", over_core)

    def y_hop(a):
        return lax.ppermute(a, "dp", [(0, 1), (1, 0)])

    column = [jnp.concatenate([tokens, cotangent, table], axis=1)]
    for s in range(1, n_z):
        column.append(z_hop(column[-1]))
    side = [x_hop(a) for a in column]
    across = [y_hop(a) for a in column]
    far = [x_hop(a) if s < n_z // 2 else y_hop(b) for s, (a, b) in enumerate(zip(across, side))]

    tok_rows = tokens.shape[0]
    all_rows, all_both, all_scaled, backs = [], [], [], []
    for s in range(n_z):
        own = [column[s], side[s]]
        rows = jnp.concatenate(own + [core_hop(a) for a in own], axis=0)
        grad_both, scaled, back = rows_pass(rows, w_in, w_out, me, lanes, True)
        all_rows.append(rows)
        all_both.append(grad_both)
        all_scaled.append(scaled)
        backs.append(back)
    for s in range(n_z):
        other = [across[s], far[s]]
        rows = jnp.concatenate(other + [core_hop(a) for a in other], axis=0)
        grad_both, scaled, _ = rows_pass(rows, w_in, w_out, me, lanes, False)
        all_rows.append(rows)
        all_both.append(grad_both)
        all_scaled.append(scaled)

    def add(a, b):
        return (a.astype(jnp.float32) + b.astype(jnp.float32)).astype(jnp.bfloat16)

    def chip_sum(s):
        kept, sent = backs[s][: 2 * tok_rows], backs[s][2 * tok_rows :]
        pair = add(kept, core_hop(sent))
        return add(pair[:tok_rows], x_hop(pair[tok_rows:]))

    total = chip_sum(1)
    for s in range(2, n_z):
        total = add(chip_sum(s), z_hop(total))
    total = add(chip_sum(0), z_hop(total))

    part = width // 2
    rows = jnp.concatenate(all_rows, axis=0)
    own_tok = lax.dynamic_slice_in_dim(rows, mine * part, part, axis=1)
    own_cot = lax.dynamic_slice_in_dim(rows, width + mine * part, part, axis=1)
    return (
        total[:, :width],
        pick_inner(total[:, width:], picks),
        outer(own_tok, jnp.concatenate(all_both, axis=0))[None],
        outer(own_cot, jnp.concatenate(all_scaled, axis=0))[None],
    )


def solution(mesh):
    in_specs = (
        P(("expert", "dp"), None),
        P(("expert", "dp"), None),
        P(("expert", "dp"), None),
        P(("expert", "dp"), None),
        P("expert", None, None),
        P("expert", None, None),
    )
    out_specs = (
        P(("expert", "dp"), None),
        P(("expert", "dp"), None),
        P("expert", "dp", None),
        P("expert", "dp", None),
    )

    def run(tokens, *rest):
        small = tokens.size * 2 <= GATHER_BYTES and mesh.shape["dp"] == 2
        shards = streamed if small and mesh.shape["expert"] == 16 else grouped
        return jax.shard_map(
            shards, mesh=mesh, in_specs=in_specs, out_specs=out_specs, check_vma=False
        )(tokens, *rest)

    return run
```

```python
import functools

import jax
import jax.numpy as jnp
from jax import lax
from jax.experimental import pallas as pl
from jax.experimental.pallas import tpu as pltpu
from jax.sharding import PartitionSpec as P

LANES = 128
CORES = 2
GATHER_BYTES = 16 << 20


def weight_table(expert_ids, combine, experts):
    lanes = jnp.arange(-(-experts // LANES) * LANES, dtype=jnp.int32)
    picks = expert_ids[:, :, None] == lanes
    table = jnp.sum(jnp.where(picks, combine.astype(jnp.float32)[:, :, None], 0.0), axis=1)
    return table.astype(jnp.bfloat16), picks, lanes


def rows_pass(rows, w_in, w_out, me, lanes, with_grad):
    width, hidden = w_out.shape
    tok, cot = rows[:, :width], rows[:, width : 2 * width]
    weight = jnp.sum(
        jnp.where(lanes[None, :] == me, rows[:, 2 * width :].astype(jnp.float32), 0.0),
        axis=1,
        keepdims=True,
    )
    both = jnp.dot(tok, w_in, preferred_element_type=jnp.float32)
    gate, upper = both[:, :hidden], both[:, hidden:]
    sigma = jax.nn.sigmoid(gate)
    swish = gate * sigma
    activ = swish * upper
    cot_down = jnp.dot(cot, w_out, preferred_element_type=jnp.float32)
    grad_act = weight * cot_down
    grad_gate = grad_act * upper * sigma * (1.0 + gate * (1.0 - sigma))
    grad_both = jnp.concatenate([grad_gate, grad_act * swish], axis=1).astype(jnp.bfloat16)
    scaled = (weight * activ).astype(jnp.bfloat16)
    if not with_grad:
        return grad_both, scaled, None
    inner = jnp.sum(activ * cot_down, axis=1, keepdims=True)
    row_grad = lax.dot_general(
        grad_both, w_in, (((1,), (1,)), ((), ())), preferred_element_type=jnp.float32
    ).astype(jnp.bfloat16)
    inner_table = jnp.where(lanes[None, :] == me, inner, 0.0).astype(jnp.bfloat16)
    return grad_both, scaled, jnp.concatenate([row_grad, inner_table], axis=1)


def outer(rows, columns):
    return lax.dot_general(
        rows, columns, (((0,), (0,)), ((), ())), preferred_element_type=jnp.float32
    ).astype(jnp.bfloat16)


def pick_inner(back, picks):
    return jnp.sum(jnp.where(picks, back.astype(jnp.float32)[:, None, :], 0.0), axis=2).astype(
        jnp.bfloat16
    )


def grouped(tokens, cotangent, expert_ids, combine, gate_up, down_proj):
    width = tokens.shape[1]
    me = lax.axis_index("expert")
    table, picks, lanes = weight_table(expert_ids, combine, lax.axis_size("expert"))
    rows = lax.all_gather(
        jnp.concatenate([tokens, cotangent, table], axis=1), "expert", axis=0, tiled=True
    )
    grad_both, scaled, back = rows_pass(rows, gate_up[0], down_proj[0], me, lanes, True)
    back = lax.psum_scatter(back, "expert", scatter_dimension=0, tiled=True)

    def share(term):
        return lax.psum_scatter(term, "dp", scatter_dimension=0, tiled=True)[None]

    return (
        back[:, :width],
        pick_inner(back[:, width:], picks),
        share(outer(rows[:, :width], grad_both)),
        share(outer(rows[:, width : 2 * width], scaled)),
    )


def gate(passed, extra, groups):
    arrays = list(passed) + list(extra)
    count = len(passed)
    places = [(g, j, k) for g, members in enumerate(groups) for j, k in enumerate(members)]

    def kernel(*refs):
        ins, outs = refs[: len(arrays)], refs[len(arrays) : -1]
        copies = [
            pltpu.make_async_copy(ins[k], outs[count + g].at[j], refs[-1].at[i])
            for i, (g, j, k) in enumerate(places)
        ]
        for copy in copies:
            copy.start()
        for copy in copies:
            copy.wait()

    anywhere = pl.BlockSpec(memory_space=pl.ANY)
    shapes = [jax.ShapeDtypeStruct(p.shape, p.dtype) for p in passed]
    shapes += [jax.ShapeDtypeStruct((len(g),) + arrays[0].shape, arrays[0].dtype) for g in groups]
    out = pl.pallas_call(
        kernel,
        out_shape=shapes,
        in_specs=[anywhere] * len(arrays),
        out_specs=[anywhere] * len(shapes),
        scratch_shapes=[pltpu.SemaphoreType.DMA((max(1, len(places)),))],
        input_output_aliases={i: i for i in range(count)},
    )(*arrays)
    return out[:count], out[count:]


def slot_kernel(with_grad, started, where, own, near, w_in, w_out, *refs):
    refs = refs[4:] if started else refs
    out_tok, out_cot, out_both, out_scaled = refs[:4]
    kept, sent = refs[4:6] if with_grad else (None, None)
    tok, cot, win, wout, sems = refs[-5:]
    width, hidden = w_out.shape
    units, tok_rows, _ = own.shape
    part = out_tok.shape[1]
    step = 256 if hidden % 256 == 0 else hidden
    copies = []
    for j in range(hidden // step):
        gates, uppers = pl.ds(j * step, step), pl.ds(hidden + j * step, step)
        copies.append(
            [
                pltpu.make_async_copy(w_in.at[:, gates], win.at[:, gates], sems.at[j, 0]),
                pltpu.make_async_copy(w_in.at[:, uppers], win.at[:, uppers], sems.at[j, 1]),
                pltpu.make_async_copy(w_out.at[:, gates], wout.at[:, gates], sems.at[j, 2]),
            ]
        )
        for copy in copies[-1]:
            copy.start()

    me, mine = where[0], where[1]
    blocks = [own.at[i] for i in range(units)] + [near.at[i] for i in range(units)]
    weights = []
    for i in range(0, 2 * units, 2):
        pair = blocks[i : i + 2]
        rows = pl.ds(i * tok_rows, 2 * tok_rows)
        for target, first in ((tok, 0), (cot, width)):
            joined = [b[:, pl.ds(first, width)].astype(jnp.float32) for b in pair]
            target[rows, :] = jnp.concatenate(joined, axis=0).astype(jnp.bfloat16)
        for b in pair:
            table = b[:, pl.ds(2 * width, b.shape[1] - 2 * width)].astype(jnp.float32)
            lane = lax.broadcasted_iota(jnp.int32, table.shape, 1)
            weights.append(jnp.sum(jnp.where(lane == me, table, 0.0), axis=1, keepdims=True))
    weight = jnp.concatenate(weights, axis=0)
    columns = pl.ds(pl.multiple_of(mine * part, part), part)
    out_tok[...] = tok[:, columns]
    out_cot[...] = cot[:, columns]

    inner = jnp.zeros_like(weight)
    for j in range(hidden // step):
        for copy in copies[j]:
            copy.wait()
        gates, uppers = pl.ds(j * step, step), pl.ds(hidden + j * step, step)
        gate_x = jnp.dot(tok[...], win[:, gates], preferred_element_type=jnp.float32)
        upper = jnp.dot(tok[...], win[:, uppers], preferred_element_type=jnp.float32)
        cot_down = jnp.dot(cot[...], wout[:, gates], preferred_element_type=jnp.float32)
        sigma = 1.0 / (1.0 + jnp.exp(-gate_x))
        swish = gate_x * sigma
        activ = swish * upper
        grad_act = weight * cot_down
        out_both[:, gates] = (
            grad_act * upper * sigma * (1.0 + gate_x * (1.0 - sigma))
        ).astype(jnp.bfloat16)
        out_both[:, uppers] = (grad_act * swish).astype(jnp.bfloat16)
        out_scaled[:, gates] = (weight * activ).astype(jnp.bfloat16)
        if with_grad:
            inner += jnp.sum(activ * cot_down, axis=1, keepdims=True)
    if not with_grad:
        return

    def give(columns, value):
        for i in range(2 * units):
            target = kept if i < units else sent
            target[i % units, :, columns] = value[i * tok_rows : (i + 1) * tok_rows].astype(
                jnp.bfloat16
            )

    wide = 512 if width % 512 == 0 else width
    for j in range(width // wide):
        span = pl.ds(j * wide, wide)
        give(
            span,
            lax.dot_general(
                out_both[...],
                win[span, :],
                (((1,), (1,)), ((), ())),
                preferred_element_type=jnp.float32,
            ),
        )
    extra = own.shape[2] - 2 * width
    lane = lax.broadcasted_iota(jnp.int32, (inner.shape[0], extra), 1)
    give(pl.ds(width, extra), jnp.where(lane == me, inner, 0.0))


def slot_pass(index, slots, where, own, near, w_in, w_out, shared, with_grad):
    width, hidden = w_out.shape
    units, tok_rows, wide = own.shape
    rows = 2 * units * tok_rows
    part = width // 2
    columns = (part, part, 2 * hidden, hidden)
    started = shared is not None
    whole = pl.BlockSpec((units, tok_rows, wide), lambda i: (0, 0, 0))
    anywhere = pl.BlockSpec(memory_space=pl.ANY)
    shapes = [jax.ShapeDtypeStruct((slots * rows, c), jnp.bfloat16) for c in columns]
    specs = [pl.BlockSpec((rows, c), lambda i: (index, 0)) for c in columns]
    if with_grad:
        back = (units, tok_rows, wide - width)
        shapes += [jax.ShapeDtypeStruct(back, jnp.bfloat16)] * 2
        specs += [pl.BlockSpec(back, lambda i: (0, 0, 0))] * 2
    flops = 2 * rows * width * hidden * (5 if with_grad else 3)
    out = pl.pallas_call(
        functools.partial(slot_kernel, with_grad, started),
        grid=(1,),
        out_shape=shapes,
        in_specs=[pl.BlockSpec(memory_space=pltpu.SMEM), whole, whole, anywhere, anywhere]
        + [anywhere] * (4 if started else 0),
        out_specs=specs,
        scratch_shapes=[
            pltpu.VMEM((rows, width), jnp.bfloat16),
            pltpu.VMEM((rows, width), jnp.bfloat16),
            pltpu.VMEM(w_in.shape, jnp.bfloat16),
            pltpu.VMEM(w_out.shape, jnp.bfloat16),
            pltpu.SemaphoreType.DMA((hidden // 256 if hidden % 256 == 0 else 1, 3)),
        ],
        input_output_aliases={5 + i: i for i in range(4)} if started else {},
        compiler_params=pltpu.CompilerParams(vmem_limit_bytes=40 << 20),
        cost_estimate=pl.CostEstimate(
            flops=flops, bytes_accessed=3 * width * hidden * 2, transcendentals=rows * hidden
        ),
    )(where, own, near, w_in, w_out, *(shared or ()))
    return out[:4], out[4:]


def streamed(tokens, cotangent, expert_ids, combine, gate_up, down_proj):
    width = tokens.shape[1]
    experts = lax.axis_size("expert")
    me = lax.axis_index("expert")
    w_in, w_out = gate_up[0], down_proj[0]
    where = jnp.stack([me, lax.axis_index("dp")]).astype(jnp.int32)
    table, picks, lanes = weight_table(expert_ids, combine, experts)

    n_x, n_z = 2, experts // CORES // 2

    def place(z, x, core):
        return (z * n_x + x) * CORES + core

    spots = [(z, x, c) for z in range(n_z) for x in range(n_x) for c in range(CORES)]
    up_z = [(place(z, x, c), place((z + 1) % n_z, x, c)) for z, x, c in spots]
    over_x = [(place(z, x, c), place(z, 1 - x, c)) for z, x, c in spots]
    over_core = [(place(z, x, c), place(z, x, 1 - c)) for z, x, c in spots]

    def z_hop(a):
        return lax.ppermute(a, "expert", up_z)

    def x_hop(a):
        return lax.ppermute(a, "expert", over_x)

    def core_hop(a):
        return lax.ppermute(a, "expert", over_core)

    def y_hop(a):
        return lax.ppermute(a, "dp", [(0, 1), (1, 0)])

    shared = None
    backs = []

    def run(index, rows, with_grad):
        nonlocal shared
        shared, back = slot_pass(
            index, 2 * n_z, where, rows, core_hop(rows), w_in, w_out, shared, with_grad
        )
        if with_grad:
            backs.append(back)

    z0 = jnp.concatenate([tokens, cotangent, table], axis=1)
    z1, x0, y0 = z_hop(z0), x_hop(z0), y_hop(z0)
    (z1, x0, y0), (m0,) = gate([z1, x0, y0], [z0], [[3, 1]])
    z2, x1, y1 = z_hop(z1), x_hop(z1), y_hop(z1)
    run(0, m0, True)
    (z2, x1, y1), (m1,) = gate([z2, x1, y1], [z1], [[3, 1]])
    z3, x2, y2 = z_hop(z2), x_hop(z2), y_hop(z2)
    run(1, m1, True)
    (z3, x2, y2), (m2,) = gate([z3, x2, y2], [z2], [[3, 1]])
    x3, y3, d0 = x_hop(z3), z_hop(y2), y_hop(x0)
    run(2, m2, True)
    (x3, y3, d0), (m3, n0) = gate([x3, y3, d0], [z3, y0], [[3, 0], [4, 2]])
    d1, d2 = z_hop(d0), y_hop(x2)
    run(3, m3, True)
    run(4, n0, False)
    (d1, d2), (n1, n2) = gate([d1, d2], [y1, y2], [[2, 0], [3, 1]])
    d3 = y_hop(x3)
    run(5, n1, False)
    run(6, n2, False)
    _, (n3,) = gate([], [y3, d3], [[0, 1]])
    run(7, n3, False)

    def add(a, b):
        return (a.astype(jnp.float32) + b.astype(jnp.float32)).astype(jnp.bfloat16)

    def chip_sum(s):
        kept, sent = backs[s]
        pair = add(kept, core_hop(sent))
        return add(pair[0], x_hop(pair[1]))

    total = chip_sum(1)
    for s in range(2, n_z):
        total = add(chip_sum(s), z_hop(total))
    total = add(chip_sum(0), z_hop(total))

    own_tok, own_cot, all_both, all_scaled = shared
    return (
        total[:, :width],
        pick_inner(total[:, width:], picks),
        outer(own_tok, all_both)[None],
        outer(own_cot, all_scaled)[None],
    )


def solution(mesh):
    in_specs = (
        P(("expert", "dp"), None),
        P(("expert", "dp"), None),
        P(("expert", "dp"), None),
        P(("expert", "dp"), None),
        P("expert", None, None),
        P("expert", None, None),
    )
    out_specs = (
        P(("expert", "dp"), None),
        P(("expert", "dp"), None),
        P("expert", "dp", None),
        P("expert", "dp", None),
    )

    def run(tokens, *rest):
        small = tokens.size * 2 <= GATHER_BYTES and mesh.shape["dp"] == 2
        shards = streamed if small and mesh.shape["expert"] == 16 else grouped
        return jax.shard_map(
            shards, mesh=mesh, in_specs=in_specs, out_specs=out_specs, check_vma=False
        )(tokens, *rest)

    return run
```

```python
import functools

import jax
import jax.numpy as jnp
from jax import lax
from jax.experimental import pallas as pl
from jax.experimental.pallas import tpu as pltpu
from jax.sharding import PartitionSpec as P

LANES = 128
CORES = 2
GATHER_BYTES = 16 << 20


def weight_table(expert_ids, combine, experts):
    lanes = jnp.arange(-(-experts // LANES) * LANES, dtype=jnp.int32)
    picks = expert_ids[:, :, None] == lanes
    table = jnp.sum(jnp.where(picks, combine.astype(jnp.float32)[:, :, None], 0.0), axis=1)
    return table.astype(jnp.bfloat16), picks, lanes


def rows_pass(rows, w_in, w_out, me, lanes, with_grad):
    width, hidden = w_out.shape
    tok, cot = rows[:, :width], rows[:, width : 2 * width]
    weight = jnp.sum(
        jnp.where(lanes[None, :] == me, rows[:, 2 * width :].astype(jnp.float32), 0.0),
        axis=1,
        keepdims=True,
    )
    both = jnp.dot(tok, w_in, preferred_element_type=jnp.float32)
    gate, upper = both[:, :hidden], both[:, hidden:]
    sigma = jax.nn.sigmoid(gate)
    swish = gate * sigma
    activ = swish * upper
    cot_down = jnp.dot(cot, w_out, preferred_element_type=jnp.float32)
    grad_act = weight * cot_down
    grad_gate = grad_act * upper * sigma * (1.0 + gate * (1.0 - sigma))
    grad_both = jnp.concatenate([grad_gate, grad_act * swish], axis=1).astype(jnp.bfloat16)
    scaled = (weight * activ).astype(jnp.bfloat16)
    if not with_grad:
        return grad_both, scaled, None
    inner = jnp.sum(activ * cot_down, axis=1, keepdims=True)
    row_grad = lax.dot_general(
        grad_both, w_in, (((1,), (1,)), ((), ())), preferred_element_type=jnp.float32
    ).astype(jnp.bfloat16)
    inner_table = jnp.where(lanes[None, :] == me, inner, 0.0).astype(jnp.bfloat16)
    return grad_both, scaled, jnp.concatenate([row_grad, inner_table], axis=1)


def outer(rows, columns):
    return lax.dot_general(
        rows, columns, (((0,), (0,)), ((), ())), preferred_element_type=jnp.float32
    ).astype(jnp.bfloat16)


def pick_inner(back, picks):
    return jnp.sum(jnp.where(picks, back.astype(jnp.float32)[:, None, :], 0.0), axis=2).astype(
        jnp.bfloat16
    )


def grouped(tokens, cotangent, expert_ids, combine, gate_up, down_proj):
    width = tokens.shape[1]
    me = lax.axis_index("expert")
    table, picks, lanes = weight_table(expert_ids, combine, lax.axis_size("expert"))
    rows = lax.all_gather(
        jnp.concatenate([tokens, cotangent, table], axis=1), "expert", axis=0, tiled=True
    )
    grad_both, scaled, back = rows_pass(rows, gate_up[0], down_proj[0], me, lanes, True)
    back = lax.psum_scatter(back, "expert", scatter_dimension=0, tiled=True)

    def share(term):
        return lax.psum_scatter(term, "dp", scatter_dimension=0, tiled=True)[None]

    return (
        back[:, :width],
        pick_inner(back[:, width:], picks),
        share(outer(rows[:, :width], grad_both)),
        share(outer(rows[:, width : 2 * width], scaled)),
    )


def gate(*arrays):
    if len(arrays) == 1:
        return arrays
    anywhere = pl.BlockSpec(memory_space=pl.ANY)
    return pl.pallas_call(
        lambda *refs: None,
        out_shape=[jax.ShapeDtypeStruct(a.shape, a.dtype) for a in arrays],
        in_specs=[anywhere] * len(arrays),
        out_specs=[anywhere] * len(arrays),
        input_output_aliases={i: i for i in range(len(arrays))},
        compiler_params=pltpu.CompilerParams(vmem_limit_bytes=1 << 20),
    )(*arrays)


def keep_near(*arrays):
    def kernel(*refs):
        count = len(arrays)
        copies = [
            pltpu.make_async_copy(refs[i], refs[count + i], refs[-1].at[i]) for i in range(count)
        ]
        for copy in copies:
            copy.start()
        for copy in copies:
            copy.wait()

    return pl.pallas_call(
        kernel,
        out_shape=[pltpu.VMEM(a.shape, a.dtype) for a in arrays],
        in_specs=[pl.BlockSpec(memory_space=pltpu.HBM)] * len(arrays),
        out_specs=[pl.BlockSpec(memory_space=pltpu.VMEM)] * len(arrays),
        scratch_shapes=[pltpu.SemaphoreType.DMA((len(arrays),))],
        compiler_params=pltpu.CompilerParams(vmem_limit_bytes=1 << 20),
    )(*arrays)


def slot_kernel(with_grad, first, last, *refs):
    where, units, (win, wout) = refs[0], refs[1:5], refs[5:7]
    refs = refs[7:]
    if not first:
        old_up, old_down = refs[:2]
        refs = refs[2:]
    new_up, new_down = refs[:2]
    refs = refs[2:]
    if with_grad:
        kept, sent = refs[:2]
        refs = refs[2:]
    tok, cot, both, scaled, tok_t, cot_t, sems = refs[:7]
    refs = refs[7:]
    if last:
        done_up, done_down = refs[:2]

    width, hidden = wout.shape
    tok_rows, wide = units[0].shape
    rows = 4 * tok_rows
    spare = tok.shape[0] - rows
    part = tok_t.shape[0]
    me, mine = where[0], where[1]
    for padded in (tok, cot, both, scaled) if spare else ():
        padded[pl.ds(rows, spare), :] = jnp.zeros((spare, padded.shape[1]), jnp.bfloat16)

    weights = []
    for i in (0, 2):
        span = pl.ds(i * tok_rows, 2 * tok_rows)
        for target, start in ((tok, 0), (cot, width)):
            joined = [units[j][:, pl.ds(start, width)].astype(jnp.float32) for j in (i, i + 1)]
            target[span, :] = jnp.concatenate(joined, axis=0).astype(jnp.bfloat16)
        for j in (i, i + 1):
            table = units[j][:, pl.ds(2 * width, wide - 2 * width)].astype(jnp.float32)
            lane = lax.broadcasted_iota(jnp.int32, table.shape, 1)
            weights.append(jnp.sum(jnp.where(lane == me, table, 0.0), axis=1, keepdims=True))
    weight = jnp.concatenate(weights, axis=0)

    real = pl.ds(0, rows)
    step = 256 if hidden % 256 == 0 else hidden
    inner = jnp.zeros_like(weight)
    for j in range(hidden // step):
        gates, uppers = pl.ds(j * step, step), pl.ds(hidden + j * step, step)
        gate_x = jnp.dot(tok[real, :], win[:, gates], preferred_element_type=jnp.float32)
        upper = jnp.dot(tok[real, :], win[:, uppers], preferred_element_type=jnp.float32)
        cot_down = jnp.dot(cot[real, :], wout[:, gates], preferred_element_type=jnp.float32)
        sigma = 1.0 / (1.0 + jnp.exp(-gate_x))
        swish = gate_x * sigma
        activ = swish * upper
        grad_act = weight * cot_down
        both[real, gates] = (grad_act * upper * sigma * (1.0 + gate_x * (1.0 - sigma))).astype(
            jnp.bfloat16
        )
        both[real, uppers] = (grad_act * swish).astype(jnp.bfloat16)
        scaled[real, gates] = (weight * activ).astype(jnp.bfloat16)
        if with_grad:
            inner += jnp.sum(activ * cot_down, axis=1, keepdims=True)

    leave = []
    if with_grad:

        def back(columns, value):
            for i in range(4):
                target = (sent if i % 2 else kept).at[i // 2]
                target[:, columns] = value[i * tok_rows : (i + 1) * tok_rows].astype(jnp.bfloat16)

        for start in range(0, width, 512):
            span = pl.ds(start, min(512, width - start))
            term = lax.dot_general(
                both[real, :],
                win[span, :],
                (((1,), (1,)), ((), ())),
                preferred_element_type=jnp.float32,
            )
            back(span, term)
        lane = lax.broadcasted_iota(jnp.int32, (rows, wide - 2 * width), 1)
        back(pl.ds(width, wide - 2 * width), jnp.where(lane == me, inner, 0.0))

    columns = pl.ds(pl.multiple_of(mine * part, part), part)
    tok_t[...] = tok[:, columns].T
    cot_t[...] = cot[:, columns].T
    sides = [
        (tok_t, both, None if first else old_up, new_up, done_up if last else None),
        (cot_t, scaled, None if first else old_down, new_down, done_down if last else None),
    ]
    place = 0
    for left, right, old, new, done in sides:
        for start in range(0, right.shape[1], step):
            span = pl.ds(start, step)
            term = jnp.dot(left[...], right[:, span], preferred_element_type=jnp.float32)
            if not first:
                term += old[:, span]
            if not last:
                new[:, span] = term
                continue
            done[:, span] = term.astype(jnp.bfloat16)
            leave.append(
                pltpu.make_async_copy(done.at[:, span], new.at[:, span], sems.at[place])
            )
            leave[-1].start()
            place += 1
    for copy in leave:
        copy.wait()


def slot_pass(where, units, win, wout, sums, with_grad, last):
    width, hidden = wout.shape
    tok_rows, wide = units[0].shape
    rows = 4 * tok_rows
    padded = -(-rows // LANES) * LANES
    part = width // 2
    first = sums is None
    near, far = pl.BlockSpec(memory_space=pltpu.VMEM), pl.BlockSpec(memory_space=pltpu.HBM)
    grads = [(part, 2 * hidden), (part, hidden)]
    if last:
        shapes, specs = [pltpu.HBM(g, jnp.bfloat16) for g in grads], [far, far]
    else:
        shapes, specs = [pltpu.VMEM(g, jnp.float32) for g in grads], [near, near]
    back = (2, tok_rows, wide - width)
    scratch = [
        pltpu.VMEM((padded, width), jnp.bfloat16),
        pltpu.VMEM((padded, width), jnp.bfloat16),
        pltpu.VMEM((padded, 2 * hidden), jnp.bfloat16),
        pltpu.VMEM((padded, hidden), jnp.bfloat16),
        pltpu.VMEM((part, padded), jnp.bfloat16),
        pltpu.VMEM((part, padded), jnp.bfloat16),
        pltpu.SemaphoreType.DMA((3 * hidden // (256 if hidden % 256 == 0 else hidden),)),
    ]
    if with_grad:
        shapes += [pltpu.VMEM(back, jnp.bfloat16)] * 2
        specs += [near, near]
    if last:
        scratch += [pltpu.VMEM(g, jnp.bfloat16) for g in grads]
    flops = 2 * rows * width * hidden * (6.5 if with_grad else 4.5)
    out = pl.pallas_call(
        functools.partial(slot_kernel, with_grad, first, last),
        out_shape=shapes,
        in_specs=[pl.BlockSpec(memory_space=pltpu.SMEM)]
        + [near] * (6 if first else 8),
        out_specs=specs,
        scratch_shapes=scratch,
        input_output_aliases={} if first or last else {7: 0, 8: 1},
        compiler_params=pltpu.CompilerParams(vmem_limit_bytes=(18 if last else 14) << 20),
        cost_estimate=pl.CostEstimate(
            flops=int(flops), bytes_accessed=4 * tok_rows * wide * 2, transcendentals=rows * hidden
        ),
    )(where, *units, win, wout, *(sums or ()))
    return out[:2], out[2:]


def streamed(tokens, cotangent, expert_ids, combine, gate_up, down_proj):
    width = tokens.shape[1]
    experts = lax.axis_size("expert")
    me = lax.axis_index("expert")
    where = jnp.stack([me, lax.axis_index("dp")]).astype(jnp.int32)
    table, picks, lanes = weight_table(expert_ids, combine, experts)

    n_x, n_z = 2, experts // CORES // 2

    def place(z, x, core):
        return (z * n_x + x) * CORES + core

    spots = [(z, x, c) for z in range(n_z) for x in range(n_x) for c in range(CORES)]
    up_z = [(place(z, x, c), place((z + 1) % n_z, x, c)) for z, x, c in spots]
    over_x = [(place(z, x, c), place(z, 1 - x, c)) for z, x, c in spots]
    over_core = [(place(z, x, c), place(z, x, 1 - c)) for z, x, c in spots]

    def z_hop(a):
        return lax.ppermute(a, "expert", up_z)

    def x_hop(a):
        return lax.ppermute(a, "expert", over_x)

    def core_hop(a):
        return lax.ppermute(a, "expert", over_core)

    def y_hop(a):
        return lax.ppermute(a, "dp", [(0, 1), (1, 0)])

    sums, backs = None, []
    win, wout = keep_near(gate_up[0], down_proj[0])

    def run(units, with_grad=False, last=False):
        nonlocal sums
        sums, back = slot_pass(where, units, win, wout, sums, with_grad, last)
        if with_grad:
            backs.append(back)

    z0 = jnp.concatenate([tokens, cotangent, table], axis=1)
    z1, x0, y0, z0c = gate(z_hop(z0), x_hop(z0), y_hop(z0), core_hop(z0))
    x0c, z1c = core_hop(x0), core_hop(z1)
    run((z0, z0c, x0, x0c), with_grad=True)
    z2, x1, y1, z1c = gate(z_hop(z1), x_hop(z1), y_hop(z1), z1c)
    x1c, z2c = core_hop(x1), core_hop(z2)
    run((z1, z1c, x1, x1c), with_grad=True)
    z3, x2, y2, z2c = gate(z_hop(z2), x_hop(z2), y_hop(z2), z2c)
    x2c, z3c = core_hop(x2), core_hop(z3)
    run((z2, z2c, x2, x2c), with_grad=True)
    x3, y3, d0, z3c = gate(x_hop(z3), z_hop(y2), y_hop(x0), z3c)
    x3c, y0c, d0c = core_hop(x3), core_hop(y0), core_hop(d0)
    run((z3, z3c, x3, x3c), with_grad=True)
    run((y0, y0c, d0, d0c))
    d1, d2 = gate(z_hop(d0), y_hop(x2))
    y1c, y2c, y3c, d1c, d2c = (core_hop(a) for a in (y1, y2, y3, d1, d2))
    run((y1, y1c, d1, d1c))
    run((y2, y2c, d2, d2c))
    d3 = y_hop(x3)
    run((y3, y3c, d3, core_hop(d3)), last=True)

    def add(a, b):
        return (a.astype(jnp.float32) + b.astype(jnp.float32)).astype(jnp.bfloat16)

    def chip_sum(s):
        kept, sent = backs[s]
        pair = add(kept, core_hop(sent))
        return add(pair[0], x_hop(pair[1]))

    total = chip_sum(1)
    for s in range(2, n_z):
        total = add(chip_sum(s), z_hop(total))
    total = add(chip_sum(0), z_hop(total))

    return (
        total[:, :width],
        pick_inner(total[:, width:], picks),
        sums[0][None],
        sums[1][None],
    )


def solution(mesh):
    in_specs = (
        P(("expert", "dp"), None),
        P(("expert", "dp"), None),
        P(("expert", "dp"), None),
        P(("expert", "dp"), None),
        P("expert", None, None),
        P("expert", None, None),
    )
    out_specs = (
        P(("expert", "dp"), None),
        P(("expert", "dp"), None),
        P("expert", "dp", None),
        P("expert", "dp", None),
    )

    def run(tokens, *rest):
        small = tokens.size * 2 <= GATHER_BYTES and mesh.shape["dp"] == 2
        shards = streamed if small and mesh.shape["expert"] == 16 else grouped
        return jax.shard_map(
            shards, mesh=mesh, in_specs=in_specs, out_specs=out_specs, check_vma=False
        )(tokens, *rest)

    return run
```

```python
import functools

import jax
import jax.numpy as jnp
from jax import lax
from jax.experimental import pallas as pl
from jax.experimental.pallas import tpu as pltpu
from jax.sharding import PartitionSpec as P

LANES = 128
CORES = 2
GATHER_BYTES = 16 << 20


def weight_table(expert_ids, combine, experts):
    lanes = jnp.arange(-(-experts // LANES) * LANES, dtype=jnp.int32)
    picks = expert_ids[:, :, None] == lanes
    table = jnp.sum(jnp.where(picks, combine.astype(jnp.float32)[:, :, None], 0.0), axis=1)
    return table.astype(jnp.bfloat16), picks, lanes


def rows_pass(rows, w_in, w_out, me, lanes, with_grad):
    width, hidden = w_out.shape
    tok, cot = rows[:, :width], rows[:, width : 2 * width]
    weight = jnp.sum(
        jnp.where(lanes[None, :] == me, rows[:, 2 * width :].astype(jnp.float32), 0.0),
        axis=1,
        keepdims=True,
    )
    both = jnp.dot(tok, w_in, preferred_element_type=jnp.float32)
    gate, upper = both[:, :hidden], both[:, hidden:]
    sigma = jax.nn.sigmoid(gate)
    swish = gate * sigma
    activ = swish * upper
    cot_down = jnp.dot(cot, w_out, preferred_element_type=jnp.float32)
    grad_act = weight * cot_down
    grad_gate = grad_act * upper * sigma * (1.0 + gate * (1.0 - sigma))
    grad_both = jnp.concatenate([grad_gate, grad_act * swish], axis=1).astype(jnp.bfloat16)
    scaled = (weight * activ).astype(jnp.bfloat16)
    if not with_grad:
        return grad_both, scaled, None
    inner = jnp.sum(activ * cot_down, axis=1, keepdims=True)
    row_grad = lax.dot_general(
        grad_both, w_in, (((1,), (1,)), ((), ())), preferred_element_type=jnp.float32
    ).astype(jnp.bfloat16)
    inner_table = jnp.where(lanes[None, :] == me, inner, 0.0).astype(jnp.bfloat16)
    return grad_both, scaled, jnp.concatenate([row_grad, inner_table], axis=1)


def outer(rows, columns):
    return lax.dot_general(
        rows, columns, (((0,), (0,)), ((), ())), preferred_element_type=jnp.float32
    ).astype(jnp.bfloat16)


def pick_inner(back, picks):
    return jnp.sum(jnp.where(picks, back.astype(jnp.float32)[:, None, :], 0.0), axis=2).astype(
        jnp.bfloat16
    )


def grouped(tokens, cotangent, expert_ids, combine, gate_up, down_proj):
    width = tokens.shape[1]
    me = lax.axis_index("expert")
    table, picks, lanes = weight_table(expert_ids, combine, lax.axis_size("expert"))
    rows = lax.all_gather(
        jnp.concatenate([tokens, cotangent, table], axis=1), "expert", axis=0, tiled=True
    )
    grad_both, scaled, back = rows_pass(rows, gate_up[0], down_proj[0], me, lanes, True)
    back = lax.psum_scatter(back, "expert", scatter_dimension=0, tiled=True)

    def share(term):
        return lax.psum_scatter(term, "dp", scatter_dimension=0, tiled=True)[None]

    return (
        back[:, :width],
        pick_inner(back[:, width:], picks),
        share(outer(rows[:, :width], grad_both)),
        share(outer(rows[:, width : 2 * width], scaled)),
    )


def gate(passed, stacked=(), after=()):
    count = len(passed)
    arrays = list(passed) + list(after)
    stacked = [next(i for i, p in enumerate(passed) if p is a) for a in stacked]

    def kernel(*refs):
        if not stacked:
            return
        out = refs[len(arrays) + count]
        copies = [
            pltpu.make_async_copy(refs[i], out.at[j], refs[-1].at[j]) for j, i in enumerate(stacked)
        ]
        for copy in copies:
            copy.start()
        for copy in copies:
            copy.wait()

    anywhere = pl.BlockSpec(memory_space=pl.ANY)
    shapes = [jax.ShapeDtypeStruct(a.shape, a.dtype) for a in passed]
    specs = [anywhere] * count
    if stacked:
        first = arrays[stacked[0]]
        shapes.append(jax.ShapeDtypeStruct((len(stacked),) + first.shape, first.dtype))
        specs.append(pl.BlockSpec(memory_space=pltpu.VMEM))
    out = pl.pallas_call(
        kernel,
        out_shape=shapes,
        in_specs=[anywhere] * len(arrays),
        out_specs=specs,
        scratch_shapes=[pltpu.SemaphoreType.DMA((max(1, len(stacked)),))],
        input_output_aliases={i: i for i in range(count)},
        compiler_params=pltpu.CompilerParams(vmem_limit_bytes=4 << 20),
    )(*arrays)
    return out


def add(terms, after=()):
    arrays, picks = zip(*terms)
    anywhere = pl.BlockSpec(memory_space=pl.ANY)
    near = pl.BlockSpec(memory_space=pltpu.VMEM)

    def kernel(*refs):
        parts = [ref if k is None else ref.at[k] for ref, k in zip(refs, picks)]
        total = parts[0][...].astype(jnp.float32)
        for part in parts[1:]:
            total += part[...].astype(jnp.float32)
        refs[-1][...] = total.astype(jnp.bfloat16)

    return pl.pallas_call(
        kernel,
        out_shape=jax.ShapeDtypeStruct(arrays[0].shape[-2:], jnp.bfloat16),
        in_specs=[near] * len(arrays) + [anywhere] * len(after),
        compiler_params=pltpu.CompilerParams(vmem_limit_bytes=6 << 20),
    )(*arrays, *after)


def finish(terms, expert_ids, width, after):
    arrays, picks = zip(*terms)
    tok_rows, top = expert_ids.shape
    anywhere = pl.BlockSpec(memory_space=pl.ANY)
    near = pl.BlockSpec(memory_space=pltpu.VMEM)

    def kernel(ids, *refs):
        parts = [ref if k is None else ref.at[k] for ref, k in zip(refs, picks)]
        out, chosen = refs[-2:]
        total = parts[0][...].astype(jnp.float32)
        for part in parts[1:]:
            total += part[...].astype(jnp.float32)
        out[...] = total[:, :width].astype(jnp.bfloat16)
        table = total[:, width:]
        lane = lax.broadcasted_iota(jnp.int32, table.shape, 1)
        kept = [
            jnp.sum(jnp.where(lane == ids[:, k : k + 1], table, 0.0), axis=1, keepdims=True)
            for k in range(top)
        ]
        chosen[...] = jnp.concatenate(kept, axis=1).astype(jnp.bfloat16)

    return pl.pallas_call(
        kernel,
        out_shape=[
            jax.ShapeDtypeStruct((tok_rows, width), jnp.bfloat16),
            jax.ShapeDtypeStruct((tok_rows, top), jnp.bfloat16),
        ],
        in_specs=[near] * (1 + len(arrays)) + [anywhere] * len(after),
        compiler_params=pltpu.CompilerParams(vmem_limit_bytes=6 << 20),
    )(expert_ids, *arrays, *after)


def keep_near(*arrays):
    def kernel(*refs):
        count = len(arrays)
        copies = [
            pltpu.make_async_copy(refs[i], refs[count + i], refs[-1].at[i]) for i in range(count)
        ]
        for copy in copies:
            copy.start()
        for copy in copies:
            copy.wait()

    return pl.pallas_call(
        kernel,
        out_shape=[pltpu.VMEM(a.shape, a.dtype) for a in arrays],
        in_specs=[pl.BlockSpec(memory_space=pltpu.HBM)] * len(arrays),
        out_specs=[pl.BlockSpec(memory_space=pltpu.VMEM)] * len(arrays),
        scratch_shapes=[pltpu.SemaphoreType.DMA((len(arrays),))],
        compiler_params=pltpu.CompilerParams(vmem_limit_bytes=1 << 20),
    )(*arrays)


def slot_kernel(picks, waits, with_grad, first, last, *refs):
    where, (win, wout) = refs[0], refs[5:7]
    units = [ref if k is None else ref.at[k] for ref, k in zip(refs[1:5], picks)]
    refs = refs[7:]
    if not first:
        old_up, old_down = refs[:2]
        refs = refs[2:]
    refs = refs[waits:]
    new_up, new_down = refs[:2]
    refs = refs[2:]
    if with_grad:
        kept, sent = refs[:2]
        refs = refs[2:]
    else:
        refs[0][...] = jnp.zeros_like(refs[0])
        refs = refs[1:]
    tok, cot, both, scaled, tok_t, cot_t, sems = refs[:7]
    refs = refs[7:]
    if last:
        done_up, done_down = refs[:2]

    width, hidden = wout.shape
    tok_rows, wide = units[0].shape
    rows = 4 * tok_rows
    spare = tok.shape[0] - rows
    part = tok_t.shape[0]
    me, mine = where[0], where[1]
    for padded in (tok, cot, both, scaled) if spare else ():
        padded[pl.ds(rows, spare), :] = jnp.zeros((spare, padded.shape[1]), jnp.bfloat16)

    weights = []
    for i in (0, 2):
        span = pl.ds(i * tok_rows, 2 * tok_rows)
        for target, start in ((tok, 0), (cot, width)):
            joined = [units[j][:, pl.ds(start, width)].astype(jnp.float32) for j in (i, i + 1)]
            target[span, :] = jnp.concatenate(joined, axis=0).astype(jnp.bfloat16)
        for j in (i, i + 1):
            table = units[j][:, pl.ds(2 * width, wide - 2 * width)].astype(jnp.float32)
            lane = lax.broadcasted_iota(jnp.int32, table.shape, 1)
            weights.append(jnp.sum(jnp.where(lane == me, table, 0.0), axis=1, keepdims=True))
    weight = jnp.concatenate(weights, axis=0)

    real = pl.ds(0, rows)
    step = 256 if hidden % 256 == 0 else hidden
    inner = jnp.zeros_like(weight)
    for j in range(hidden // step):
        gates, uppers = pl.ds(j * step, step), pl.ds(hidden + j * step, step)
        gate_x = jnp.dot(tok[real, :], win[:, gates], preferred_element_type=jnp.float32)
        upper = jnp.dot(tok[real, :], win[:, uppers], preferred_element_type=jnp.float32)
        cot_down = jnp.dot(cot[real, :], wout[:, gates], preferred_element_type=jnp.float32)
        sigma = 1.0 / (1.0 + jnp.exp(-gate_x))
        swish = gate_x * sigma
        activ = swish * upper
        grad_act = weight * cot_down
        both[real, gates] = (grad_act * upper * sigma * (1.0 + gate_x * (1.0 - sigma))).astype(
            jnp.bfloat16
        )
        both[real, uppers] = (grad_act * swish).astype(jnp.bfloat16)
        scaled[real, gates] = (weight * activ).astype(jnp.bfloat16)
        if with_grad:
            inner += jnp.sum(activ * cot_down, axis=1, keepdims=True)

    leave = []
    if with_grad:

        def back(columns, value):
            for i in range(4):
                target = (sent if i % 2 else kept).at[i // 2]
                target[:, columns] = value[i * tok_rows : (i + 1) * tok_rows].astype(jnp.bfloat16)

        for start in range(0, width, 512):
            span = pl.ds(start, min(512, width - start))
            term = lax.dot_general(
                both[real, :],
                win[span, :],
                (((1,), (1,)), ((), ())),
                preferred_element_type=jnp.float32,
            )
            back(span, term)
        lane = lax.broadcasted_iota(jnp.int32, (rows, wide - 2 * width), 1)
        back(pl.ds(width, wide - 2 * width), jnp.where(lane == me, inner, 0.0))

    columns = pl.ds(pl.multiple_of(mine * part, part), part)
    tok_t[...] = tok[:, columns].T
    cot_t[...] = cot[:, columns].T
    sides = [
        (tok_t, both, None if first else old_up, new_up, done_up if last else None),
        (cot_t, scaled, None if first else old_down, new_down, done_down if last else None),
    ]
    place = 0
    for left, right, old, new, done in sides:
        for start in range(0, right.shape[1], step):
            span = pl.ds(start, step)
            term = jnp.dot(left[...], right[:, span], preferred_element_type=jnp.float32)
            if not first:
                term += old[:, span]
            if not last:
                new[:, span] = term
                continue
            done[:, span] = term.astype(jnp.bfloat16)
            leave.append(
                pltpu.make_async_copy(done.at[:, span], new.at[:, span], sems.at[place])
            )
            leave[-1].start()
            place += 1
    for copy in leave:
        copy.wait()


def slot_pass(where, units, win, wout, sums, with_grad, last, after):
    width, hidden = wout.shape
    arrays, picks = zip(*units)
    tok_rows, wide = arrays[0].shape[-2:]
    rows = 4 * tok_rows
    padded = -(-rows // LANES) * LANES
    part = width // 2
    first = sums is None
    near, far = pl.BlockSpec(memory_space=pltpu.VMEM), pl.BlockSpec(memory_space=pltpu.HBM)
    grads = [(part, 2 * hidden), (part, hidden)]
    if last:
        shapes, specs = [pltpu.HBM(g, jnp.bfloat16) for g in grads], [far, far]
    else:
        shapes, specs = [pltpu.VMEM(g, jnp.float32) for g in grads], [near, near]
    back = (2, tok_rows, wide - width)
    scratch = [
        pltpu.VMEM((padded, width), jnp.bfloat16),
        pltpu.VMEM((padded, width), jnp.bfloat16),
        pltpu.VMEM((padded, 2 * hidden), jnp.bfloat16),
        pltpu.VMEM((padded, hidden), jnp.bfloat16),
        pltpu.VMEM((part, padded), jnp.bfloat16),
        pltpu.VMEM((part, padded), jnp.bfloat16),
        pltpu.SemaphoreType.DMA((3 * hidden // (256 if hidden % 256 == 0 else hidden),)),
    ]
    if with_grad:
        shapes += [pltpu.VMEM(back, jnp.bfloat16)] * 2
        specs += [near, near]
    else:
        shapes.append(pltpu.VMEM((8, LANES), jnp.float32))
        specs.append(near)
    if last:
        scratch += [pltpu.VMEM(g, jnp.bfloat16) for g in grads]
    flops = 2 * rows * width * hidden * (6.5 if with_grad else 4.5)
    out = pl.pallas_call(
        functools.partial(slot_kernel, picks, len(after), with_grad, first, last),
        out_shape=shapes,
        in_specs=[pl.BlockSpec(memory_space=pltpu.SMEM)]
        + [near] * (6 if first else 8)
        + [pl.BlockSpec(memory_space=pl.ANY)] * len(after),
        out_specs=specs,
        scratch_shapes=scratch,
        input_output_aliases={} if first or last else {7: 0, 8: 1},
        compiler_params=pltpu.CompilerParams(vmem_limit_bytes=(14 if last else 10) << 20),
        cost_estimate=pl.CostEstimate(
            flops=int(flops), bytes_accessed=4 * tok_rows * wide * 2, transcendentals=rows * hidden
        ),
    )(where, *arrays, win, wout, *(sums or ()), *after)
    return out[:2], out[2:]


def streamed(tokens, cotangent, expert_ids, combine, gate_up, down_proj):
    width = tokens.shape[1]
    experts = lax.axis_size("expert")
    me = lax.axis_index("expert")
    where = jnp.stack([me, lax.axis_index("dp")]).astype(jnp.int32)
    table, picks, lanes = weight_table(expert_ids, combine, experts)

    n_x, n_z = 2, experts // CORES // 2

    def place(z, x, core):
        return (z * n_x + x) * CORES + core

    spots = [(z, x, c) for z in range(n_z) for x in range(n_x) for c in range(CORES)]
    up_z = [(place(z, x, c), place((z + 1) % n_z, x, c)) for z, x, c in spots]
    over_x = [(place(z, x, c), place(z, 1 - x, c)) for z, x, c in spots]
    over_core = [(place(z, x, c), place(z, x, 1 - c)) for z, x, c in spots]

    def z_hop(a):
        return lax.ppermute(a, "expert", up_z)

    def x_hop(a):
        return lax.ppermute(a, "expert", over_x)

    def core_hop(a):
        return lax.ppermute(a, "expert", over_core)

    def y_hop(a):
        return lax.ppermute(a, "dp", [(0, 1), (1, 0)])

    sums = None
    win, wout = keep_near(gate_up[0], down_proj[0])

    def run(units, with_grad=False, last=False, after=()):
        nonlocal sums
        sums, rest = slot_pass(where, units, win, wout, sums, with_grad, last, after)
        return rest

    z0 = jnp.concatenate([tokens, cotangent, table], axis=1)
    z1, x0, y0, z0c = z_hop(z0), x_hop(z0), y_hop(z0), core_hop(z0)
    z1, x0, y0, z0c, pile = gate((z1, x0, y0, z0c), stacked=(x0, z1, y0), after=(win, wout))

    z2, x1, y1, c1 = z_hop(z1), x_hop(z1), y_hop(z1), core_hop(pile)
    kept0, sent0 = run([(z0, None), (z0c, None), (x0, None), (c1, 0)], with_grad=True)
    z2, x1, y1, sent0, pile = gate((z2, x1, y1, sent0), stacked=(x1, z2, y1))

    z3, x2, y2, c2 = z_hop(z2), x_hop(z2), y_hop(z2), core_hop(pile)
    came0 = core_hop(sent0)
    kept1, sent1 = run([(z1, None), (c1, 1), (x1, None), (c2, 0)], with_grad=True)
    z3, x2, y2, sent1, pile = gate((z3, x2, y2, sent1), stacked=(x2, z3, y2))

    x3, y3, d0, c3 = x_hop(z3), z_hop(y2), y_hop(x0), core_hop(pile)
    came1 = core_hop(sent1)
    kept2, sent2 = run([(z2, None), (c2, 1), (x2, None), (c3, 0)], with_grad=True)
    part1 = add([(kept1, 1), (came1, 1)], after=(kept2,))
    part0 = add([(kept0, 1), (came0, 1)], after=(part1,))
    (mark,) = run([(y0, None), (c1, 2), (y1, None), (c2, 2)], after=(part0,))
    x3, y3, d0, sent2, part1, pile = gate(
        (x3, y3, d0, sent2, part1), stacked=(x3, y3, d0), after=(mark,)
    )

    d1, d2, c4 = z_hop(d0), y_hop(x2), core_hop(pile)
    side1, came2 = x_hop(part1), core_hop(sent2)
    kept3, sent3 = run([(z3, None), (c3, 1), (x3, None), (c4, 0)], with_grad=True)
    part2 = add([(kept2, 1), (came2, 1)], after=(kept3,))
    (mark,) = run([(y2, None), (c3, 2), (y3, None), (c4, 1)], after=(part2,))
    total = add([(kept1, 0), (came1, 0), (side1, None)], after=(mark,))
    d1, d2, sent3, part2, part0, total, pile = gate(
        (d1, d2, sent3, part2, part0, total), stacked=(d1, d2)
    )

    d3, c5, came3 = y_hop(x3), core_hop(pile), core_hop(sent3)
    side2, total, side0 = x_hop(part2), z_hop(total), x_hop(part0)
    (mark,) = run([(d0, None), (c4, 2), (d1, None), (c5, 0)])
    part3 = add([(kept3, 1), (came3, 1)], after=(mark,))
    total = add([(kept2, 0), (came2, 0), (side2, None), (total, None)], after=(part3,))
    (d3,) = gate((d3,), after=(total,))

    c6, side3, total = core_hop(d3), x_hop(part3), z_hop(total)
    total = add([(kept3, 0), (came3, 0), (side3, None), (total, None)], after=(d3,))
    (mark,) = run([(d2, None), (c5, 1), (d3, None), (c6, None)], last=True, after=(total,))
    grad_tokens, grad_combine = finish(
        [(kept0, 0), (came0, 0), (side0, None), (z_hop(total), None)],
        expert_ids,
        width,
        after=(mark,),
    )
    return grad_tokens, grad_combine, sums[0][None], sums[1][None]


def solution(mesh):
    in_specs = (
        P(("expert", "dp"), None),
        P(("expert", "dp"), None),
        P(("expert", "dp"), None),
        P(("expert", "dp"), None),
        P("expert", None, None),
        P("expert", None, None),
    )
    out_specs = (
        P(("expert", "dp"), None),
        P(("expert", "dp"), None),
        P("expert", "dp", None),
        P("expert", "dp", None),
    )

    def run(tokens, *rest):
        small = tokens.size * 2 <= GATHER_BYTES and mesh.shape["dp"] == 2
        shards = streamed if small and mesh.shape["expert"] == 16 else grouped
        return jax.shard_map(
            shards, mesh=mesh, in_specs=in_specs, out_specs=out_specs, check_vma=False
        )(tokens, *rest)

    return run
```

```python
import functools

import jax
import jax.numpy as jnp
from jax import lax
from jax.experimental import pallas as pl
from jax.experimental.pallas import tpu as pltpu
from jax.sharding import PartitionSpec as P

LANES = 128
CORES = 2
GATHER_BYTES = 16 << 20


def weight_table(expert_ids, combine, experts):
    lanes = jnp.arange(-(-experts // LANES) * LANES, dtype=jnp.int32)
    picks = expert_ids[:, :, None] == lanes
    table = jnp.sum(jnp.where(picks, combine.astype(jnp.float32)[:, :, None], 0.0), axis=1)
    return table.astype(jnp.bfloat16), picks, lanes


def rows_pass(rows, w_in, w_out, me, lanes, with_grad):
    width, hidden = w_out.shape
    tok, cot = rows[:, :width], rows[:, width : 2 * width]
    weight = jnp.sum(
        jnp.where(lanes[None, :] == me, rows[:, 2 * width :].astype(jnp.float32), 0.0),
        axis=1,
        keepdims=True,
    )
    both = jnp.dot(tok, w_in, preferred_element_type=jnp.float32)
    gate, upper = both[:, :hidden], both[:, hidden:]
    sigma = jax.nn.sigmoid(gate)
    swish = gate * sigma
    activ = swish * upper
    cot_down = jnp.dot(cot, w_out, preferred_element_type=jnp.float32)
    grad_act = weight * cot_down
    grad_gate = grad_act * upper * sigma * (1.0 + gate * (1.0 - sigma))
    grad_both = jnp.concatenate([grad_gate, grad_act * swish], axis=1).astype(jnp.bfloat16)
    scaled = (weight * activ).astype(jnp.bfloat16)
    if not with_grad:
        return grad_both, scaled, None
    inner = jnp.sum(activ * cot_down, axis=1, keepdims=True)
    row_grad = lax.dot_general(
        grad_both, w_in, (((1,), (1,)), ((), ())), preferred_element_type=jnp.float32
    ).astype(jnp.bfloat16)
    inner_table = jnp.where(lanes[None, :] == me, inner, 0.0).astype(jnp.bfloat16)
    return grad_both, scaled, jnp.concatenate([row_grad, inner_table], axis=1)


def outer(rows, columns):
    return lax.dot_general(
        rows, columns, (((0,), (0,)), ((), ())), preferred_element_type=jnp.float32
    ).astype(jnp.bfloat16)


def pick_inner(back, picks):
    return jnp.sum(jnp.where(picks, back.astype(jnp.float32)[:, None, :], 0.0), axis=2).astype(
        jnp.bfloat16
    )


def grouped(tokens, cotangent, expert_ids, combine, gate_up, down_proj):
    width = tokens.shape[1]
    me = lax.axis_index("expert")
    table, picks, lanes = weight_table(expert_ids, combine, lax.axis_size("expert"))
    rows = lax.all_gather(
        jnp.concatenate([tokens, cotangent, table], axis=1), "expert", axis=0, tiled=True
    )
    grad_both, scaled, back = rows_pass(rows, gate_up[0], down_proj[0], me, lanes, True)
    back = lax.psum_scatter(back, "expert", scatter_dimension=0, tiled=True)

    def share(term):
        return lax.psum_scatter(term, "dp", scatter_dimension=0, tiled=True)[None]

    return (
        back[:, :width],
        pick_inner(back[:, width:], picks),
        share(outer(rows[:, :width], grad_both)),
        share(outer(rows[:, width : 2 * width], scaled)),
    )


def gate(passed, stacked=(), after=()):
    count = len(passed)
    arrays = list(passed) + list(after)
    stacked = [next(i for i, p in enumerate(passed) if p is a) for a in stacked]

    def kernel(*refs):
        if not stacked:
            return
        out = refs[len(arrays) + count]
        copies = [
            pltpu.make_async_copy(refs[i], out.at[j], refs[-1].at[j]) for j, i in enumerate(stacked)
        ]
        for copy in copies:
            copy.start()
        for copy in copies:
            copy.wait()

    anywhere = pl.BlockSpec(memory_space=pl.ANY)
    shapes = [jax.ShapeDtypeStruct(a.shape, a.dtype) for a in passed]
    specs = [anywhere] * count
    if stacked:
        first = arrays[stacked[0]]
        shapes.append(jax.ShapeDtypeStruct((len(stacked),) + first.shape, first.dtype))
        specs.append(pl.BlockSpec(memory_space=pltpu.VMEM))
    out = pl.pallas_call(
        kernel,
        out_shape=shapes,
        in_specs=[anywhere] * len(arrays),
        out_specs=specs,
        scratch_shapes=[pltpu.SemaphoreType.DMA((max(1, len(stacked)),))],
        input_output_aliases={i: i for i in range(count)},
        compiler_params=pltpu.CompilerParams(vmem_limit_bytes=4 << 20),
    )(*arrays)
    return out


def add(terms, after=()):
    arrays, picks = zip(*terms)
    anywhere = pl.BlockSpec(memory_space=pl.ANY)
    near = pl.BlockSpec(memory_space=pltpu.VMEM)

    def kernel(*refs):
        parts = [ref if k is None else ref.at[k] for ref, k in zip(refs, picks)]
        total = parts[0][...].astype(jnp.float32)
        for part in parts[1:]:
            total += part[...].astype(jnp.float32)
        refs[-1][...] = total.astype(jnp.bfloat16)

    return pl.pallas_call(
        kernel,
        out_shape=jax.ShapeDtypeStruct(arrays[0].shape[-2:], jnp.bfloat16),
        in_specs=[near] * len(arrays) + [anywhere] * len(after),
        compiler_params=pltpu.CompilerParams(vmem_limit_bytes=6 << 20),
    )(*arrays, *after)


def finish(terms, ids, width, after):
    arrays, picks = zip(*terms)
    top, tok_rows = ids.shape
    anywhere = pl.BlockSpec(memory_space=pl.ANY)
    near = pl.BlockSpec(memory_space=pltpu.VMEM)

    def kernel(ids, *refs):
        parts = [ref if k is None else ref.at[k] for ref, k in zip(refs, picks)]
        out, chosen, rows = refs[-3:]
        total = parts[0][...].astype(jnp.float32)
        for part in parts[1:]:
            total += part[...].astype(jnp.float32)
        out[...] = total[:, :width].astype(jnp.bfloat16)
        table = total[:, width:].T
        line = lax.broadcasted_iota(jnp.int32, table.shape, 0)
        for k in range(top):
            picked = jnp.where(line == ids[k : k + 1, :], table, 0.0)
            rows[k : k + 1, :] = jnp.sum(picked, axis=0, keepdims=True)
        chosen[...] = rows[...].astype(jnp.bfloat16)

    return pl.pallas_call(
        kernel,
        out_shape=[
            jax.ShapeDtypeStruct((tok_rows, width), jnp.bfloat16),
            jax.ShapeDtypeStruct((top, tok_rows), jnp.bfloat16),
        ],
        scratch_shapes=[pltpu.VMEM((top, tok_rows), jnp.float32)],
        in_specs=[near] * (1 + len(arrays)) + [anywhere] * len(after),
        compiler_params=pltpu.CompilerParams(vmem_limit_bytes=6 << 20),
    )(ids, *arrays, *after)


def first_rows(tokens, cotangent, ids, combine, experts):
    top, tok_rows = ids.shape
    width = tokens.shape[1]
    extra = -(-experts // LANES) * LANES

    def kernel(tok, cot, ids, combine, out):
        out[:, :width] = tok[...]
        out[:, width : 2 * width] = cot[...]
        line = lax.broadcasted_iota(jnp.int32, (extra, tok_rows), 0)
        share = combine[...].astype(jnp.float32)
        table = jnp.zeros((extra, tok_rows), jnp.float32)
        for k in range(top):
            table += jnp.where(line == ids[k : k + 1, :], share[k : k + 1, :], 0.0)
        out[:, 2 * width :] = table.T.astype(jnp.bfloat16)

    return pl.pallas_call(
        kernel,
        out_shape=jax.ShapeDtypeStruct((tok_rows, 2 * width + extra), jnp.bfloat16),
        compiler_params=pltpu.CompilerParams(vmem_limit_bytes=4 << 20),
    )(tokens, cotangent, ids, combine)


def keep_near(*arrays):
    def kernel(*refs):
        count = len(arrays)
        copies = [
            pltpu.make_async_copy(refs[i], refs[count + i], refs[-1].at[i]) for i in range(count)
        ]
        for copy in copies:
            copy.start()
        for copy in copies:
            copy.wait()

    return pl.pallas_call(
        kernel,
        out_shape=[pltpu.VMEM(a.shape, a.dtype) for a in arrays],
        in_specs=[pl.BlockSpec(memory_space=pltpu.HBM)] * len(arrays),
        out_specs=[pl.BlockSpec(memory_space=pltpu.VMEM)] * len(arrays),
        scratch_shapes=[pltpu.SemaphoreType.DMA((len(arrays),))],
        compiler_params=pltpu.CompilerParams(vmem_limit_bytes=44 << 20),
    )(*arrays)


def slot_kernel(picks, waits, with_grad, first, last, *refs):
    units = [ref if k is None else ref.at[k] for ref, k in zip(refs[:4], picks)]
    win, wout = refs[4:6]
    refs = refs[6:]
    if not first:
        old_up, old_down = refs[:2]
        refs = refs[2:]
    refs = refs[waits:]
    new_up, new_down = refs[:2]
    refs = refs[2:]
    if with_grad:
        kept, sent = refs[:2]
        refs = refs[2:]
    else:
        refs[0][...] = jnp.zeros_like(refs[0])
        refs = refs[1:]
    tok, cot, both, scaled, tok_t, cot_t, sems = refs[:7]
    refs = refs[7:]
    if last:
        done_up, done_down = refs[:2]

    width, hidden = wout.shape
    tok_rows, wide = units[0].shape
    rows = 4 * tok_rows
    spare = tok.shape[0] - rows
    part = tok_t.shape[0]
    me, mine = lax.axis_index("expert"), lax.axis_index("dp")
    for padded in (tok, cot, both, scaled) if spare else ():
        padded[pl.ds(rows, spare), :] = jnp.zeros((spare, padded.shape[1]), jnp.bfloat16)

    weights = []
    for i in (0, 2):
        span = pl.ds(i * tok_rows, 2 * tok_rows)
        for target, start in ((tok, 0), (cot, width)):
            joined = [units[j][:, pl.ds(start, width)].astype(jnp.float32) for j in (i, i + 1)]
            target[span, :] = jnp.concatenate(joined, axis=0).astype(jnp.bfloat16)
        for j in (i, i + 1):
            table = units[j][:, pl.ds(2 * width, wide - 2 * width)].astype(jnp.float32)
            lane = lax.broadcasted_iota(jnp.int32, table.shape, 1)
            weights.append(jnp.sum(jnp.where(lane == me, table, 0.0), axis=1, keepdims=True))
    weight = jnp.concatenate(weights, axis=0)

    real = pl.ds(0, rows)
    step = 256 if hidden % 256 == 0 else hidden
    inner = jnp.zeros_like(weight)
    for j in range(hidden // step):
        gates, uppers = pl.ds(j * step, step), pl.ds(hidden + j * step, step)
        gate_x = jnp.dot(tok[real, :], win[:, gates], preferred_element_type=jnp.float32)
        upper = jnp.dot(tok[real, :], win[:, uppers], preferred_element_type=jnp.float32)
        cot_down = jnp.dot(cot[real, :], wout[:, gates], preferred_element_type=jnp.float32)
        sigma = 1.0 / (1.0 + jnp.exp(-gate_x))
        swish = gate_x * sigma
        activ = swish * upper
        grad_act = weight * cot_down
        both[real, gates] = (grad_act * upper * sigma * (1.0 + gate_x * (1.0 - sigma))).astype(
            jnp.bfloat16
        )
        both[real, uppers] = (grad_act * swish).astype(jnp.bfloat16)
        scaled[real, gates] = (weight * activ).astype(jnp.bfloat16)
        if with_grad:
            inner += jnp.sum(activ * cot_down, axis=1, keepdims=True)

    leave = []
    if with_grad:

        def back(columns, value):
            for i in range(4):
                target = (sent if i % 2 else kept).at[i // 2]
                target[:, columns] = value[i * tok_rows : (i + 1) * tok_rows].astype(jnp.bfloat16)

        for start in range(0, width, 512):
            span = pl.ds(start, min(512, width - start))
            term = lax.dot_general(
                both[real, :],
                win[span, :],
                (((1,), (1,)), ((), ())),
                preferred_element_type=jnp.float32,
            )
            back(span, term)
        lane = lax.broadcasted_iota(jnp.int32, (rows, wide - 2 * width), 1)
        back(pl.ds(width, wide - 2 * width), jnp.where(lane == me, inner, 0.0))

    columns = pl.ds(pl.multiple_of(mine * part, part), part)
    tok_t[...] = tok[:, columns].T
    cot_t[...] = cot[:, columns].T
    sides = [
        (tok_t, both, None if first else old_up, new_up, done_up if last else None),
        (cot_t, scaled, None if first else old_down, new_down, done_down if last else None),
    ]
    place = 0
    for left, right, old, new, done in sides:
        for start in range(0, right.shape[1], step):
            span = pl.ds(start, step)
            term = jnp.dot(left[...], right[:, span], preferred_element_type=jnp.float32)
            if not first:
                term += old[:, span]
            if not last:
                new[:, span] = term
                continue
            done[:, span] = term.astype(jnp.bfloat16)
            leave.append(
                pltpu.make_async_copy(done.at[:, span], new.at[:, span], sems.at[place])
            )
            leave[-1].start()
            place += 1
    for copy in leave:
        copy.wait()


def slot_pass(units, win, wout, sums, with_grad, last, after):
    width, hidden = wout.shape
    arrays, picks = zip(*units)
    tok_rows, wide = arrays[0].shape[-2:]
    rows = 4 * tok_rows
    padded = -(-rows // LANES) * LANES
    part = width // 2
    first = sums is None
    near, far = pl.BlockSpec(memory_space=pltpu.VMEM), pl.BlockSpec(memory_space=pltpu.HBM)
    grads = [(part, 2 * hidden), (part, hidden)]
    if last:
        shapes, specs = [pltpu.HBM(g, jnp.bfloat16) for g in grads], [far, far]
    else:
        shapes, specs = [pltpu.VMEM(g, jnp.float32) for g in grads], [near, near]
    back = (2, tok_rows, wide - width)
    scratch = [
        pltpu.VMEM((padded, width), jnp.bfloat16),
        pltpu.VMEM((padded, width), jnp.bfloat16),
        pltpu.VMEM((padded, 2 * hidden), jnp.bfloat16),
        pltpu.VMEM((padded, hidden), jnp.bfloat16),
        pltpu.VMEM((part, padded), jnp.bfloat16),
        pltpu.VMEM((part, padded), jnp.bfloat16),
        pltpu.SemaphoreType.DMA((3 * hidden // (256 if hidden % 256 == 0 else hidden),)),
    ]
    if with_grad:
        shapes += [pltpu.VMEM(back, jnp.bfloat16)] * 2
        specs += [near, near]
    else:
        shapes.append(pltpu.VMEM((8, LANES), jnp.float32))
        specs.append(near)
    if last:
        scratch += [pltpu.VMEM(g, jnp.bfloat16) for g in grads]
    flops = 2 * rows * width * hidden * (6.5 if with_grad else 4.5)
    out = pl.pallas_call(
        functools.partial(slot_kernel, picks, len(after), with_grad, first, last),
        out_shape=shapes,
        in_specs=[near] * (6 if first else 8)
        + [pl.BlockSpec(memory_space=pl.ANY)] * len(after),
        out_specs=specs,
        scratch_shapes=scratch,
        input_output_aliases={} if first or last else {6: 0, 7: 1},
        compiler_params=pltpu.CompilerParams(vmem_limit_bytes=(14 if last else 10) << 20),
        cost_estimate=pl.CostEstimate(
            flops=int(flops), bytes_accessed=4 * tok_rows * wide * 2, transcendentals=rows * hidden
        ),
    )(*arrays, win, wout, *(sums or ()), *after)
    return out[:2], out[2:]


def streamed(tokens, cotangent, expert_ids, combine, gate_up, down_proj):
    width = tokens.shape[1]
    experts = lax.axis_size("expert")
    ids = expert_ids.T

    n_x, n_z = 2, experts // CORES // 2

    def place(z, x, core):
        return (z * n_x + x) * CORES + core

    spots = [(z, x, c) for z in range(n_z) for x in range(n_x) for c in range(CORES)]
    up_z = [(place(z, x, c), place((z + 1) % n_z, x, c)) for z, x, c in spots]
    over_x = [(place(z, x, c), place(z, 1 - x, c)) for z, x, c in spots]
    over_core = [(place(z, x, c), place(z, x, 1 - c)) for z, x, c in spots]

    def z_hop(a):
        return lax.ppermute(a, "expert", up_z)

    def x_hop(a):
        return lax.ppermute(a, "expert", over_x)

    def core_hop(a):
        return lax.ppermute(a, "expert", over_core)

    def y_hop(a):
        return lax.ppermute(a, "dp", [(0, 1), (1, 0)])

    sums = None
    win, wout = keep_near(gate_up[0], down_proj[0])

    def run(units, with_grad=False, last=False, after=()):
        nonlocal sums
        sums, rest = slot_pass(units, win, wout, sums, with_grad, last, after)
        return rest

    z0 = first_rows(tokens, cotangent, ids, combine.T, experts)
    z1, x0, y0, z0c = z_hop(z0), x_hop(z0), y_hop(z0), core_hop(z0)
    z1, x0, y0, z0c, pile = gate((z1, x0, y0, z0c), stacked=(x0, z1, y0), after=(win, wout))

    z2, x1, y1, c1 = z_hop(z1), x_hop(z1), y_hop(z1), core_hop(pile)
    kept0, sent0 = run([(z0, None), (z0c, None), (x0, None), (c1, 0)], with_grad=True)
    z2, x1, y1, sent0, pile = gate((z2, x1, y1, sent0), stacked=(x1, z2, y1))

    z3, x2, y2, c2 = z_hop(z2), x_hop(z2), y_hop(z2), core_hop(pile)
    came0 = core_hop(sent0)
    kept1, sent1 = run([(z1, None), (c1, 1), (x1, None), (c2, 0)], with_grad=True)
    z3, x2, y2, sent1, pile = gate((z3, x2, y2, sent1), stacked=(x2, z3, y2))

    x3, y3, d0, c3 = x_hop(z3), z_hop(y2), y_hop(x0), core_hop(pile)
    came1 = core_hop(sent1)
    kept2, sent2 = run([(z2, None), (c2, 1), (x2, None), (c3, 0)], with_grad=True)
    part1 = add([(kept1, 1), (came1, 1)], after=(kept2,))
    part0 = add([(kept0, 1), (came0, 1)], after=(part1,))
    x3, y3, d0, sent2, part1, pile = gate(
        (x3, y3, d0, sent2, part1), stacked=(x3, y3, d0), after=(part0,)
    )

    d1, d2, c4 = z_hop(d0), y_hop(x2), core_hop(pile)
    side1, came2 = x_hop(part1), core_hop(sent2)
    kept3, sent3 = run([(z3, None), (c3, 1), (x3, None), (c4, 0)], with_grad=True)
    part2 = add([(kept2, 1), (came2, 1)], after=(kept3,))
    total = add([(kept1, 0), (came1, 0), (side1, None)], after=(part2,))
    (mark,) = run([(y0, None), (c1, 2), (y1, None), (c2, 2)], after=(total,))
    d1, d2, sent3, part2, part0, total, pile = gate(
        (d1, d2, sent3, part2, part0, total), stacked=(d1, d2), after=(mark,)
    )

    d3, c5, came3 = y_hop(x3), core_hop(pile), core_hop(sent3)
    side2, total, side0 = x_hop(part2), z_hop(total), x_hop(part0)
    (mark,) = run([(y2, None), (c3, 2), (y3, None), (c4, 1)], after=(pile,))
    part3 = add([(kept3, 1), (came3, 1)], after=(mark,))
    done2 = add([(kept2, 0), (came2, 0), (side2, None), (total, None)], after=(part3,))
    side3, total = x_hop(part3), z_hop(done2)
    (d3,) = gate((d3,), after=(done2,))

    c6 = core_hop(d3)
    (mark,) = run([(d0, None), (c4, 2), (d1, None), (c5, 0)], after=(d3,))
    total = add([(kept3, 0), (came3, 0), (side3, None), (total, None)], after=(mark,))
    (mark,) = run([(d2, None), (c5, 1), (d3, None), (c6, None)], last=True, after=(total,))
    grad_tokens, grad_combine = finish(
        [(kept0, 0), (came0, 0), (side0, None), (z_hop(total), None)],
        ids,
        width,
        after=(mark,),
    )
    return grad_tokens, grad_combine.T, sums[0][None], sums[1][None]


def solution(mesh):
    in_specs = (
        P(("expert", "dp"), None),
        P(("expert", "dp"), None),
        P(("expert", "dp"), None),
        P(("expert", "dp"), None),
        P("expert", None, None),
        P("expert", None, None),
    )
    out_specs = (
        P(("expert", "dp"), None),
        P(("expert", "dp"), None),
        P("expert", "dp", None),
        P("expert", "dp", None),
    )

    def run(tokens, *rest):
        small = tokens.size * 2 <= GATHER_BYTES and mesh.shape["dp"] == 2
        shards = streamed if small and mesh.shape["expert"] == 16 else grouped
        return jax.shard_map(
            shards, mesh=mesh, in_specs=in_specs, out_specs=out_specs, check_vma=False
        )(tokens, *rest)

    return run
```

```python
import functools

import jax
import jax.numpy as jnp
from jax import lax
from jax.experimental import pallas as pl
from jax.experimental.pallas import tpu as pltpu
from jax.sharding import PartitionSpec as P

LANES = 128
CORES = 2
GATHER_BYTES = 16 << 20


def weight_table(expert_ids, combine, experts):
    lanes = jnp.arange(-(-experts // LANES) * LANES, dtype=jnp.int32)
    picks = expert_ids[:, :, None] == lanes
    table = jnp.sum(jnp.where(picks, combine.astype(jnp.float32)[:, :, None], 0.0), axis=1)
    return table.astype(jnp.bfloat16), picks, lanes


def rows_pass(rows, w_in, w_out, me, lanes, with_grad):
    width, hidden = w_out.shape
    tok, cot = rows[:, :width], rows[:, width : 2 * width]
    weight = jnp.sum(
        jnp.where(lanes[None, :] == me, rows[:, 2 * width :].astype(jnp.float32), 0.0),
        axis=1,
        keepdims=True,
    )
    both = jnp.dot(tok, w_in, preferred_element_type=jnp.float32)
    gate, upper = both[:, :hidden], both[:, hidden:]
    sigma = jax.nn.sigmoid(gate)
    swish = gate * sigma
    activ = swish * upper
    cot_down = jnp.dot(cot, w_out, preferred_element_type=jnp.float32)
    grad_act = weight * cot_down
    grad_gate = grad_act * upper * sigma * (1.0 + gate * (1.0 - sigma))
    grad_both = jnp.concatenate([grad_gate, grad_act * swish], axis=1).astype(jnp.bfloat16)
    scaled = (weight * activ).astype(jnp.bfloat16)
    if not with_grad:
        return grad_both, scaled, None
    inner = jnp.sum(activ * cot_down, axis=1, keepdims=True)
    row_grad = lax.dot_general(
        grad_both, w_in, (((1,), (1,)), ((), ())), preferred_element_type=jnp.float32
    ).astype(jnp.bfloat16)
    inner_table = jnp.where(lanes[None, :] == me, inner, 0.0).astype(jnp.bfloat16)
    return grad_both, scaled, jnp.concatenate([row_grad, inner_table], axis=1)


def outer(rows, columns):
    return lax.dot_general(
        rows, columns, (((0,), (0,)), ((), ())), preferred_element_type=jnp.float32
    ).astype(jnp.bfloat16)


def pick_inner(back, picks):
    return jnp.sum(jnp.where(picks, back.astype(jnp.float32)[:, None, :], 0.0), axis=2).astype(
        jnp.bfloat16
    )


def grouped(tokens, cotangent, expert_ids, combine, gate_up, down_proj):
    width = tokens.shape[1]
    me = lax.axis_index("expert")
    table, picks, lanes = weight_table(expert_ids, combine, lax.axis_size("expert"))
    rows = lax.all_gather(
        jnp.concatenate([tokens, cotangent, table], axis=1), "expert", axis=0, tiled=True
    )
    grad_both, scaled, back = rows_pass(rows, gate_up[0], down_proj[0], me, lanes, True)
    back = lax.psum_scatter(back, "expert", scatter_dimension=0, tiled=True)

    def share(term):
        return lax.psum_scatter(term, "dp", scatter_dimension=0, tiled=True)[None]

    return (
        back[:, :width],
        pick_inner(back[:, width:], picks),
        share(outer(rows[:, :width], grad_both)),
        share(outer(rows[:, width : 2 * width], scaled)),
    )


def gate(passed, stacks=(), after=()):
    count = len(passed)
    arrays = list(passed) + list(after)
    places = [
        (g, j, next(i for i, a in enumerate(arrays) if a is member))
        for g, members in enumerate(stacks)
        for j, member in enumerate(members)
    ]

    def kernel(*refs):
        out = refs[len(arrays) + count :]
        copies = [
            pltpu.make_async_copy(refs[i], out[g].at[j], refs[-1].at[n])
            for n, (g, j, i) in enumerate(places)
        ]
        for copy in copies:
            copy.start()
        for copy in copies:
            copy.wait()

    anywhere = pl.BlockSpec(memory_space=pl.ANY)
    shapes = [jax.ShapeDtypeStruct(a.shape, a.dtype) for a in passed]
    shapes += [jax.ShapeDtypeStruct((len(g),) + g[0].shape, g[0].dtype) for g in stacks]
    return pl.pallas_call(
        kernel,
        out_shape=shapes,
        in_specs=[anywhere] * len(arrays),
        out_specs=[anywhere] * count + [pl.BlockSpec(memory_space=pltpu.VMEM)] * len(stacks),
        scratch_shapes=[pltpu.SemaphoreType.DMA((max(1, len(places)),))],
        input_output_aliases={i: i for i in range(count)},
        compiler_params=pltpu.CompilerParams(vmem_limit_bytes=4 << 20),
    )(*arrays)


def add(terms, after=(), dtype=jnp.bfloat16):
    arrays, picks = zip(*terms)
    anywhere = pl.BlockSpec(memory_space=pl.ANY)
    near = pl.BlockSpec(memory_space=pltpu.VMEM)

    def kernel(*refs):
        parts = [ref if k is None else ref.at[k] for ref, k in zip(refs, picks)]
        total = parts[0][...].astype(jnp.float32)
        for part in parts[1:]:
            total += part[...].astype(jnp.float32)
        refs[-1][...] = total.astype(dtype)

    return pl.pallas_call(
        kernel,
        out_shape=jax.ShapeDtypeStruct(arrays[0].shape[-2:], dtype),
        in_specs=[near] * len(arrays) + [anywhere] * len(after),
        compiler_params=pltpu.CompilerParams(vmem_limit_bytes=6 << 20),
    )(*arrays, *after)


def finish(terms, ids, width, after):
    arrays, picks = zip(*terms)
    top, tok_rows = ids.shape
    anywhere = pl.BlockSpec(memory_space=pl.ANY)
    near = pl.BlockSpec(memory_space=pltpu.VMEM)

    def kernel(ids, *refs):
        parts = [ref if k is None else ref.at[k] for ref, k in zip(refs, picks)]
        out, chosen, rows = refs[-3:]
        total = parts[0][...].astype(jnp.float32)
        for part in parts[1:]:
            total += part[...].astype(jnp.float32)
        out[...] = total[:, :width].astype(jnp.bfloat16)
        table = total[:, width:].T
        line = lax.broadcasted_iota(jnp.int32, table.shape, 0)
        for k in range(top):
            picked = jnp.where(line == ids[k : k + 1, :], table, 0.0)
            rows[k : k + 1, :] = jnp.sum(picked, axis=0, keepdims=True)
        chosen[...] = rows[...].astype(jnp.bfloat16)

    return pl.pallas_call(
        kernel,
        out_shape=[
            jax.ShapeDtypeStruct((tok_rows, width), jnp.bfloat16),
            jax.ShapeDtypeStruct((top, tok_rows), jnp.bfloat16),
        ],
        scratch_shapes=[pltpu.VMEM((top, tok_rows), jnp.float32)],
        in_specs=[near] * (1 + len(arrays)) + [anywhere] * len(after),
        compiler_params=pltpu.CompilerParams(vmem_limit_bytes=6 << 20),
    )(ids, *arrays, *after)


def first_rows(tokens, cotangent, ids, combine, experts):
    top, tok_rows = ids.shape
    width = tokens.shape[1]
    extra = -(-experts // LANES) * LANES

    def kernel(tok, cot, ids, combine, out):
        out[:, :width] = tok[...]
        out[:, width : 2 * width] = cot[...]
        line = lax.broadcasted_iota(jnp.int32, (extra, tok_rows), 0)
        share = combine[...].astype(jnp.float32)
        table = jnp.zeros((extra, tok_rows), jnp.float32)
        for k in range(top):
            table += jnp.where(line == ids[k : k + 1, :], share[k : k + 1, :], 0.0)
        out[:, 2 * width :] = table.T.astype(jnp.bfloat16)

    return pl.pallas_call(
        kernel,
        out_shape=jax.ShapeDtypeStruct((tok_rows, 2 * width + extra), jnp.bfloat16),
        compiler_params=pltpu.CompilerParams(vmem_limit_bytes=4 << 20),
    )(tokens, cotangent, ids, combine)


def keep_near(*arrays):
    def kernel(*refs):
        count = len(arrays)
        copies = [
            pltpu.make_async_copy(refs[i], refs[count + i], refs[-1].at[i]) for i in range(count)
        ]
        for copy in copies:
            copy.start()
        for copy in copies:
            copy.wait()

    return pl.pallas_call(
        kernel,
        out_shape=[pltpu.VMEM(a.shape, a.dtype) for a in arrays],
        in_specs=[pl.BlockSpec(memory_space=pltpu.HBM)] * len(arrays),
        out_specs=[pl.BlockSpec(memory_space=pltpu.VMEM)] * len(arrays),
        scratch_shapes=[pltpu.SemaphoreType.DMA((len(arrays),))],
        compiler_params=pltpu.CompilerParams(vmem_limit_bytes=44 << 20),
    )(*arrays)


def slot_kernel(picks, waits, with_grad, first, last, *refs):
    units = [ref if k is None else ref.at[k] for ref, k in zip(refs[:4], picks)]
    win, wout = refs[4:6]
    refs = refs[6:]
    if not first:
        old_up, old_down = refs[:2]
        refs = refs[2:]
    refs = refs[waits:]
    new_up, new_down = refs[:2]
    refs = refs[2:]
    if with_grad:
        kept, sent = refs[:2]
        refs = refs[2:]
    else:
        refs[0][...] = jnp.zeros_like(refs[0])
        refs = refs[1:]
    tok, cot, both, scaled, tok_t, cot_t, sems = refs[:7]
    refs = refs[7:]
    if last:
        done_up, done_down = refs[:2]

    width, hidden = wout.shape
    tok_rows, wide = units[0].shape
    rows = 4 * tok_rows
    spare = tok.shape[0] - rows
    part = tok_t.shape[0]
    me, mine = lax.axis_index("expert"), lax.axis_index("dp")
    for padded in (tok, cot, both, scaled) if spare else ():
        padded[pl.ds(rows, spare), :] = jnp.zeros((spare, padded.shape[1]), jnp.bfloat16)

    weights = []
    for i in (0, 2):
        span = pl.ds(i * tok_rows, 2 * tok_rows)
        for target, start in ((tok, 0), (cot, width)):
            joined = [units[j][:, pl.ds(start, width)].astype(jnp.float32) for j in (i, i + 1)]
            target[span, :] = jnp.concatenate(joined, axis=0).astype(jnp.bfloat16)
        for j in (i, i + 1):
            table = units[j][:, pl.ds(2 * width, wide - 2 * width)].astype(jnp.float32)
            lane = lax.broadcasted_iota(jnp.int32, table.shape, 1)
            weights.append(jnp.sum(jnp.where(lane == me, table, 0.0), axis=1, keepdims=True))
    weight = jnp.concatenate(weights, axis=0)

    real = pl.ds(0, rows)
    step = 256 if hidden % 256 == 0 else hidden
    inner = jnp.zeros_like(weight)
    for j in range(hidden // step):
        gates, uppers = pl.ds(j * step, step), pl.ds(hidden + j * step, step)
        gate_x = jnp.dot(tok[real, :], win[:, gates], preferred_element_type=jnp.float32)
        upper = jnp.dot(tok[real, :], win[:, uppers], preferred_element_type=jnp.float32)
        cot_down = jnp.dot(cot[real, :], wout[:, gates], preferred_element_type=jnp.float32)
        sigma = 1.0 / (1.0 + jnp.exp(-gate_x))
        swish = gate_x * sigma
        activ = swish * upper
        grad_act = weight * cot_down
        both[real, gates] = (grad_act * upper * sigma * (1.0 + gate_x * (1.0 - sigma))).astype(
            jnp.bfloat16
        )
        both[real, uppers] = (grad_act * swish).astype(jnp.bfloat16)
        scaled[real, gates] = (weight * activ).astype(jnp.bfloat16)
        if with_grad:
            inner += jnp.sum(activ * cot_down, axis=1, keepdims=True)

    leave = []
    if with_grad:

        def back(columns, value):
            for i in range(4):
                target = (sent if i % 2 else kept).at[i // 2]
                target[:, columns] = value[i * tok_rows : (i + 1) * tok_rows].astype(jnp.bfloat16)

        for start in range(0, width, 512):
            span = pl.ds(start, min(512, width - start))
            term = lax.dot_general(
                both[real, :],
                win[span, :],
                (((1,), (1,)), ((), ())),
                preferred_element_type=jnp.float32,
            )
            back(span, term)
        lane = lax.broadcasted_iota(jnp.int32, (rows, wide - 2 * width), 1)
        back(pl.ds(width, wide - 2 * width), jnp.where(lane == me, inner, 0.0))

    columns = pl.ds(pl.multiple_of(mine * part, part), part)
    tok_t[...] = tok[:, columns].T
    cot_t[...] = cot[:, columns].T
    sides = [
        (tok_t, both, None if first else old_up, new_up, done_up if last else None),
        (cot_t, scaled, None if first else old_down, new_down, done_down if last else None),
    ]
    place = 0
    for left, right, old, new, done in sides:
        for start in range(0, right.shape[1], step):
            span = pl.ds(start, step)
            term = jnp.dot(left[...], right[:, span], preferred_element_type=jnp.float32)
            if not first:
                term += old[:, span]
            if not last:
                new[:, span] = term
                continue
            done[:, span] = term.astype(jnp.bfloat16)
            leave.append(
                pltpu.make_async_copy(done.at[:, span], new.at[:, span], sems.at[place])
            )
            leave[-1].start()
            place += 1
    for copy in leave:
        copy.wait()


def slot_pass(units, win, wout, sums, with_grad, last, after):
    width, hidden = wout.shape
    arrays, picks = zip(*units)
    tok_rows, wide = arrays[0].shape[-2:]
    rows = 4 * tok_rows
    padded = -(-rows // LANES) * LANES
    part = width // 2
    first = sums is None
    near, far = pl.BlockSpec(memory_space=pltpu.VMEM), pl.BlockSpec(memory_space=pltpu.HBM)
    grads = [(part, 2 * hidden), (part, hidden)]
    if last:
        shapes, specs = [pltpu.HBM(g, jnp.bfloat16) for g in grads], [far, far]
    else:
        shapes, specs = [pltpu.VMEM(g, jnp.float32) for g in grads], [near, near]
    back = (2, tok_rows, wide - width)
    scratch = [
        pltpu.VMEM((padded, width), jnp.bfloat16),
        pltpu.VMEM((padded, width), jnp.bfloat16),
        pltpu.VMEM((padded, 2 * hidden), jnp.bfloat16),
        pltpu.VMEM((padded, hidden), jnp.bfloat16),
        pltpu.VMEM((part, padded), jnp.bfloat16),
        pltpu.VMEM((part, padded), jnp.bfloat16),
        pltpu.SemaphoreType.DMA((3 * hidden // (256 if hidden % 256 == 0 else hidden),)),
    ]
    if with_grad:
        shapes += [pltpu.VMEM(back, jnp.bfloat16)] * 2
        specs += [near, near]
    else:
        shapes.append(pltpu.VMEM((8, LANES), jnp.float32))
        specs.append(near)
    if last:
        scratch += [pltpu.VMEM(g, jnp.bfloat16) for g in grads]
    out = pl.pallas_call(
        functools.partial(slot_kernel, picks, len(after), with_grad, first, last),
        out_shape=shapes,
        in_specs=[near] * (6 if first else 8)
        + [pl.BlockSpec(memory_space=pl.ANY)] * len(after),
        out_specs=specs,
        scratch_shapes=scratch,
        input_output_aliases={} if first or last else {6: 0, 7: 1},
        compiler_params=pltpu.CompilerParams(vmem_limit_bytes=(14 if last else 10) << 20),
        cost_estimate=pl.CostEstimate(flops=0, bytes_accessed=0, transcendentals=0),
    )(*arrays, win, wout, *(sums or ()), *after)
    return out[:2], out[2:]


def streamed(tokens, cotangent, expert_ids, combine, gate_up, down_proj):
    width = tokens.shape[1]
    experts = lax.axis_size("expert")
    ids = expert_ids.T

    n_x, n_z = 2, experts // CORES // 2

    def place(z, x, core):
        return (z * n_x + x) * CORES + core

    spots = [(z, x, c) for z in range(n_z) for x in range(n_x) for c in range(CORES)]
    by_z = [
        [(place(z, x, c), place((z + far) % n_z, x, c)) for z, x, c in spots] for far in range(n_z)
    ]
    over_x = [(place(z, x, c), place(z, 1 - x, c)) for z, x, c in spots]
    over_core = [(place(z, x, c), place(z, x, 1 - c)) for z, x, c in spots]

    def z_hop(a, far=1):
        return lax.ppermute(a, "expert", by_z[far % n_z])

    def x_hop(a):
        return lax.ppermute(a, "expert", over_x)

    def core_hop(a):
        return lax.ppermute(a, "expert", over_core)

    def y_hop(a):
        return lax.ppermute(a, "dp", [(0, 1), (1, 0)])

    sums = None
    win, wout = keep_near(gate_up[0], down_proj[0])

    def run(units, with_grad=False, last=False, after=()):
        nonlocal sums
        sums, rest = slot_pass(units, win, wout, sums, with_grad, last, after)
        return rest

    z0 = first_rows(tokens, cotangent, ids, combine.T, experts)
    z1, x0, y0, z0c = z_hop(z0), x_hop(z0), y_hop(z0), core_hop(z0)
    z1, x0, y0, z0c, pile = gate((z1, x0, y0, z0c), stacks=((x0, z1, y0),), after=(win, wout))

    c1, z2, x1, y1 = core_hop(pile), z_hop(z1), x_hop(z1), y_hop(z1)
    kept0, sent0 = run([(z0, None), (z0c, None), (x0, None), (c1, 0)], with_grad=True)
    z2, x1, y1, sent0, pile = gate((z2, x1, y1, sent0), stacks=((x1, z2, y1),))

    c2, z3, x2, y2, d0 = core_hop(pile), z_hop(z2), x_hop(z2), y_hop(z2), y_hop(x0)
    kept1, sent1 = run([(z1, None), (c1, 1), (x1, None), (c2, 0)], with_grad=True)
    (mark,) = run([(y0, None), (c1, 2), (y1, None), (c2, 2)], after=(kept1,))
    z3, x2, y2, d0, sent0, sent1, pile = gate(
        (z3, x2, y2, d0, sent0, sent1), stacks=((x2, z3, y2, d0),), after=(mark,)
    )

    c3, x3, y3, d1 = core_hop(pile), z_hop(x2), y_hop(z3), x_hop(y1)
    came1, came0 = core_hop(sent1), core_hop(sent0)
    kept2, sent2 = run([(z2, None), (c2, 1), (x2, None), (c3, 0)], with_grad=True)
    part1 = add([(kept1, 1), (came1, 1)], after=(kept2,))
    part0 = add([(kept0, 1), (came0, 1)], after=(part1,))
    sum1 = add([(kept1, 0), (came1, 0), (x_hop(part1), None)], after=(part0,))
    x3, y3, d1, sent2, part0, sum1, pile, pair = gate(
        (x3, y3, d1, sent2, part0, sum1), stacks=((x3, y3, d1), (x2, x3)), after=(x2,)
    )

    c4, came2, d23 = core_hop(pile), core_hop(sent2), y_hop(pair)
    back1, side0 = z_hop(sum1, -1), x_hop(part0)
    part2 = add([(kept2, 1), (came2, 1)], after=(pile,))
    kept3, sent3 = run([(z3, None), (c3, 1), (x3, None), (c4, 0)], with_grad=True, after=(part2,))
    (mark,) = run([(y2, None), (c3, 2), (y3, None), (c4, 1)], after=(kept3,))
    came3 = core_hop(sent3)
    part3 = add([(kept3, 1), (came3, 1)], after=(mark,))
    sum2 = add([(kept2, 0), (came2, 0), (x_hop(part2), None)], after=(part3,))
    home = add(
        [(kept0, 0), (came0, 0), (side0, None), (back1, None)], after=(sum2,), dtype=jnp.float32
    )
    (mark,) = run([(d0, None), (c3, 3), (d1, None), (c4, 2)], after=(home,))
    sum3 = add([(kept3, 0), (came3, 0), (x_hop(part3), None)], after=(mark,))
    home = add([(home, None), (z_hop(sum2, -2), None)], after=(sum3,), dtype=jnp.float32)
    (d23,) = gate((d23,), after=(home,))

    c5, back3 = core_hop(d23), z_hop(sum3, -3)
    (mark,) = run([(d23, 0), (c5, 0), (d23, 1), (c5, 1)], last=True)
    grad_tokens, grad_combine = finish([(home, None), (back3, None)], ids, width, after=(mark,))
    return grad_tokens, grad_combine.T, sums[0][None], sums[1][None]


def solution(mesh):
    in_specs = (
        P(("expert", "dp"), None),
        P(("expert", "dp"), None),
        P(("expert", "dp"), None),
        P(("expert", "dp"), None),
        P("expert", None, None),
        P("expert", None, None),
    )
    out_specs = (
        P(("expert", "dp"), None),
        P(("expert", "dp"), None),
        P("expert", "dp", None),
        P("expert", "dp", None),
    )

    def run(tokens, *rest):
        small = tokens.size * 2 <= GATHER_BYTES and mesh.shape["dp"] == 2
        shards = streamed if small and mesh.shape["expert"] == 16 else grouped
        return jax.shard_map(
            shards, mesh=mesh, in_specs=in_specs, out_specs=out_specs, check_vma=False
        )(tokens, *rest)

    return run
```

```python
import functools

import jax
import jax.numpy as jnp
from jax import lax
from jax.experimental import pallas as pl
from jax.experimental.pallas import tpu as pltpu
from jax.sharding import PartitionSpec as P

LANES = 128
CORES = 2
GATHER_BYTES = 16 << 20


def weight_table(expert_ids, combine, experts):
    lanes = jnp.arange(-(-experts // LANES) * LANES, dtype=jnp.int32)
    picks = expert_ids[:, :, None] == lanes
    table = jnp.sum(jnp.where(picks, combine.astype(jnp.float32)[:, :, None], 0.0), axis=1)
    return table.astype(jnp.bfloat16), picks, lanes


def rows_pass(rows, w_in, w_out, me, lanes, with_grad):
    width, hidden = w_out.shape
    tok, cot = rows[:, :width], rows[:, width : 2 * width]
    weight = jnp.sum(
        jnp.where(lanes[None, :] == me, rows[:, 2 * width :].astype(jnp.float32), 0.0),
        axis=1,
        keepdims=True,
    )
    both = jnp.dot(tok, w_in, preferred_element_type=jnp.float32)
    gate, upper = both[:, :hidden], both[:, hidden:]
    sigma = jax.nn.sigmoid(gate)
    swish = gate * sigma
    activ = swish * upper
    cot_down = jnp.dot(cot, w_out, preferred_element_type=jnp.float32)
    grad_act = weight * cot_down
    grad_gate = grad_act * upper * sigma * (1.0 + gate * (1.0 - sigma))
    grad_both = jnp.concatenate([grad_gate, grad_act * swish], axis=1).astype(jnp.bfloat16)
    scaled = (weight * activ).astype(jnp.bfloat16)
    if not with_grad:
        return grad_both, scaled, None
    inner = jnp.sum(activ * cot_down, axis=1, keepdims=True)
    row_grad = lax.dot_general(
        grad_both, w_in, (((1,), (1,)), ((), ())), preferred_element_type=jnp.float32
    ).astype(jnp.bfloat16)
    inner_table = jnp.where(lanes[None, :] == me, inner, 0.0).astype(jnp.bfloat16)
    return grad_both, scaled, jnp.concatenate([row_grad, inner_table], axis=1)


def outer(rows, columns):
    return lax.dot_general(
        rows, columns, (((0,), (0,)), ((), ())), preferred_element_type=jnp.float32
    ).astype(jnp.bfloat16)


def pick_inner(back, picks):
    return jnp.sum(jnp.where(picks, back.astype(jnp.float32)[:, None, :], 0.0), axis=2).astype(
        jnp.bfloat16
    )


def grouped(tokens, cotangent, expert_ids, combine, gate_up, down_proj):
    width = tokens.shape[1]
    me = lax.axis_index("expert")
    table, picks, lanes = weight_table(expert_ids, combine, lax.axis_size("expert"))
    rows = lax.all_gather(
        jnp.concatenate([tokens, cotangent, table], axis=1), "expert", axis=0, tiled=True
    )
    grad_both, scaled, back = rows_pass(rows, gate_up[0], down_proj[0], me, lanes, True)
    back = lax.psum_scatter(back, "expert", scatter_dimension=0, tiled=True)

    def share(term):
        return lax.psum_scatter(term, "dp", scatter_dimension=0, tiled=True)[None]

    return (
        back[:, :width],
        pick_inner(back[:, width:], picks),
        share(outer(rows[:, :width], grad_both)),
        share(outer(rows[:, width : 2 * width], scaled)),
    )


def gate(passed, stacks=(), after=()):
    count = len(passed)
    arrays = list(passed) + list(after)
    places = [
        (g, j, next(i for i, a in enumerate(arrays) if a is member))
        for g, members in enumerate(stacks)
        for j, member in enumerate(members)
    ]

    def kernel(*refs):
        out = refs[len(arrays) + count :]
        copies = [
            pltpu.make_async_copy(refs[i], out[g].at[j], refs[-1].at[n])
            for n, (g, j, i) in enumerate(places)
        ]
        for copy in copies:
            copy.start()
        for copy in copies:
            copy.wait()

    anywhere = pl.BlockSpec(memory_space=pl.ANY)
    shapes = [jax.ShapeDtypeStruct(a.shape, a.dtype) for a in passed]
    shapes += [jax.ShapeDtypeStruct((len(g),) + g[0].shape, g[0].dtype) for g in stacks]
    return pl.pallas_call(
        kernel,
        out_shape=shapes,
        in_specs=[anywhere] * len(arrays),
        out_specs=[anywhere] * count + [pl.BlockSpec(memory_space=pltpu.VMEM)] * len(stacks),
        scratch_shapes=[pltpu.SemaphoreType.DMA((max(1, len(places)),))],
        input_output_aliases={i: i for i in range(count)},
        compiler_params=pltpu.CompilerParams(vmem_limit_bytes=4 << 20),
    )(*arrays)


def add(terms, after=(), dtype=jnp.bfloat16):
    arrays, picks = zip(*terms)
    anywhere = pl.BlockSpec(memory_space=pl.ANY)
    near = pl.BlockSpec(memory_space=pltpu.VMEM)

    def kernel(*refs):
        parts = [ref if k is None else ref.at[k] for ref, k in zip(refs, picks)]
        total = parts[0][...].astype(jnp.float32)
        for part in parts[1:]:
            total += part[...].astype(jnp.float32)
        refs[-1][...] = total.astype(dtype)

    return pl.pallas_call(
        kernel,
        out_shape=jax.ShapeDtypeStruct(arrays[0].shape[-2:], dtype),
        in_specs=[near] * len(arrays) + [anywhere] * len(after),
        compiler_params=pltpu.CompilerParams(vmem_limit_bytes=6 << 20),
    )(*arrays, *after)


def finish(terms, ids, width, after):
    arrays, picks = zip(*terms)
    top, tok_rows = ids.shape
    anywhere = pl.BlockSpec(memory_space=pl.ANY)
    near = pl.BlockSpec(memory_space=pltpu.VMEM)

    def kernel(ids, *refs):
        parts = [ref if k is None else ref.at[k] for ref, k in zip(refs, picks)]
        out, chosen, rows = refs[-3:]
        total = parts[0][...].astype(jnp.float32)
        for part in parts[1:]:
            total += part[...].astype(jnp.float32)
        out[...] = total[:, :width].astype(jnp.bfloat16)
        table = total[:, width:].T
        line = lax.broadcasted_iota(jnp.int32, table.shape, 0)
        for k in range(top):
            picked = jnp.where(line == ids[k : k + 1, :], table, 0.0)
            rows[k : k + 1, :] = jnp.sum(picked, axis=0, keepdims=True)
        chosen[...] = rows[...].astype(jnp.bfloat16)

    return pl.pallas_call(
        kernel,
        out_shape=[
            jax.ShapeDtypeStruct((tok_rows, width), jnp.bfloat16),
            jax.ShapeDtypeStruct((top, tok_rows), jnp.bfloat16),
        ],
        scratch_shapes=[pltpu.VMEM((top, tok_rows), jnp.float32)],
        in_specs=[near] * (1 + len(arrays)) + [anywhere] * len(after),
        compiler_params=pltpu.CompilerParams(vmem_limit_bytes=6 << 20),
    )(ids, *arrays, *after)


def first_rows(tokens, cotangent, ids, combine, experts):
    top, tok_rows = ids.shape
    width = tokens.shape[1]
    extra = -(-experts // LANES) * LANES

    def kernel(tok, cot, ids, combine, out):
        out[:, :width] = tok[...]
        out[:, width : 2 * width] = cot[...]
        line = lax.broadcasted_iota(jnp.int32, (extra, tok_rows), 0)
        share = combine[...].astype(jnp.float32)
        table = jnp.zeros((extra, tok_rows), jnp.float32)
        for k in range(top):
            table += jnp.where(line == ids[k : k + 1, :], share[k : k + 1, :], 0.0)
        out[:, 2 * width :] = table.T.astype(jnp.bfloat16)

    return pl.pallas_call(
        kernel,
        out_shape=jax.ShapeDtypeStruct((tok_rows, 2 * width + extra), jnp.bfloat16),
        compiler_params=pltpu.CompilerParams(vmem_limit_bytes=4 << 20),
    )(tokens, cotangent, ids, combine)


def keep_near(*arrays):
    def kernel(*refs):
        count = len(arrays)
        copies = [
            pltpu.make_async_copy(refs[i], refs[count + i], refs[-1].at[i]) for i in range(count)
        ]
        for copy in copies:
            copy.start()
        for copy in copies:
            copy.wait()

    return pl.pallas_call(
        kernel,
        out_shape=[pltpu.VMEM(a.shape, a.dtype) for a in arrays],
        in_specs=[pl.BlockSpec(memory_space=pltpu.HBM)] * len(arrays),
        out_specs=[pl.BlockSpec(memory_space=pltpu.VMEM)] * len(arrays),
        scratch_shapes=[pltpu.SemaphoreType.DMA((len(arrays),))],
        compiler_params=pltpu.CompilerParams(vmem_limit_bytes=44 << 20),
    )(*arrays)


def slot_kernel(picks, waits, with_grad, first, last, *refs):
    units = [ref if k is None else ref.at[k] for ref, k in zip(refs[:4], picks)]
    win, wout = refs[4:6]
    refs = refs[6:]
    if not first:
        old_up, old_down = refs[:2]
        refs = refs[2:]
    refs = refs[waits:]
    new_up, new_down = refs[:2]
    refs = refs[2:]
    if with_grad:
        kept, sent = refs[:2]
        refs = refs[2:]
    else:
        refs[0][...] = jnp.zeros_like(refs[0])
        refs = refs[1:]
    tok, cot, both, scaled, tok_t, cot_t, sems = refs[:7]
    refs = refs[7:]
    if last:
        done_up, done_down = refs[:2]

    width, hidden = wout.shape
    tok_rows, wide = units[0].shape
    rows = 4 * tok_rows
    spare = tok.shape[0] - rows
    part = tok_t.shape[0]
    me, mine = lax.axis_index("expert"), lax.axis_index("dp")
    for padded in (tok, cot, both, scaled) if spare else ():
        padded[pl.ds(rows, spare), :] = jnp.zeros((spare, padded.shape[1]), jnp.bfloat16)

    weights = []
    for i in (0, 2):
        span = pl.ds(i * tok_rows, 2 * tok_rows)
        for target, start in ((tok, 0), (cot, width)):
            joined = [units[j][:, pl.ds(start, width)].astype(jnp.float32) for j in (i, i + 1)]
            target[span, :] = jnp.concatenate(joined, axis=0).astype(jnp.bfloat16)
        for j in (i, i + 1):
            table = units[j][:, pl.ds(2 * width, wide - 2 * width)].astype(jnp.float32)
            lane = lax.broadcasted_iota(jnp.int32, table.shape, 1)
            weights.append(jnp.sum(jnp.where(lane == me, table, 0.0), axis=1, keepdims=True))
    weight = jnp.concatenate(weights, axis=0)

    real = pl.ds(0, rows)
    step = 256 if hidden % 256 == 0 else hidden
    inner = jnp.zeros_like(weight)
    for j in range(hidden // step):
        gates, uppers = pl.ds(j * step, step), pl.ds(hidden + j * step, step)
        gate_x = jnp.dot(tok[real, :], win[:, gates], preferred_element_type=jnp.float32)
        upper = jnp.dot(tok[real, :], win[:, uppers], preferred_element_type=jnp.float32)
        cot_down = jnp.dot(cot[real, :], wout[:, gates], preferred_element_type=jnp.float32)
        sigma = 1.0 / (1.0 + jnp.exp(-gate_x))
        swish = gate_x * sigma
        activ = swish * upper
        grad_act = weight * cot_down
        both[real, gates] = (grad_act * upper * sigma * (1.0 + gate_x * (1.0 - sigma))).astype(
            jnp.bfloat16
        )
        both[real, uppers] = (grad_act * swish).astype(jnp.bfloat16)
        scaled[real, gates] = (weight * activ).astype(jnp.bfloat16)
        if with_grad:
            inner += jnp.sum(activ * cot_down, axis=1, keepdims=True)

    leave = []
    if with_grad:

        def back(columns, value):
            for i in range(4):
                target = (sent if i % 2 else kept).at[i // 2]
                target[:, columns] = value[i * tok_rows : (i + 1) * tok_rows].astype(jnp.bfloat16)

        for start in range(0, width, 512):
            span = pl.ds(start, min(512, width - start))
            term = lax.dot_general(
                both[real, :],
                win[span, :],
                (((1,), (1,)), ((), ())),
                preferred_element_type=jnp.float32,
            )
            back(span, term)
        lane = lax.broadcasted_iota(jnp.int32, (rows, wide - 2 * width), 1)
        back(pl.ds(width, wide - 2 * width), jnp.where(lane == me, inner, 0.0))

    columns = pl.ds(pl.multiple_of(mine * part, part), part)
    tok_t[...] = tok[:, columns].T
    cot_t[...] = cot[:, columns].T
    sides = [
        (tok_t, both, None if first else old_up, new_up, done_up if last else None),
        (cot_t, scaled, None if first else old_down, new_down, done_down if last else None),
    ]
    place = 0
    for left, right, old, new, done in sides:
        for start in range(0, right.shape[1], step):
            span = pl.ds(start, step)
            term = jnp.dot(left[...], right[:, span], preferred_element_type=jnp.float32)
            if not first:
                term += old[:, span]
            if not last:
                new[:, span] = term
                continue
            done[:, span] = term.astype(jnp.bfloat16)
            leave.append(
                pltpu.make_async_copy(done.at[:, span], new.at[:, span], sems.at[place])
            )
            leave[-1].start()
            place += 1
    for copy in leave:
        copy.wait()


def slot_pass(units, win, wout, sums, with_grad, last, after):
    width, hidden = wout.shape
    arrays, picks = zip(*units)
    tok_rows, wide = arrays[0].shape[-2:]
    rows = 4 * tok_rows
    padded = -(-rows // LANES) * LANES
    part = width // 2
    first = sums is None
    near, far = pl.BlockSpec(memory_space=pltpu.VMEM), pl.BlockSpec(memory_space=pltpu.HBM)
    grads = [(part, 2 * hidden), (part, hidden)]
    if last:
        shapes, specs = [pltpu.HBM(g, jnp.bfloat16) for g in grads], [far, far]
    else:
        shapes, specs = [pltpu.VMEM(g, jnp.float32) for g in grads], [near, near]
    back = (2, tok_rows, wide - width)
    scratch = [
        pltpu.VMEM((padded, width), jnp.bfloat16),
        pltpu.VMEM((padded, width), jnp.bfloat16),
        pltpu.VMEM((padded, 2 * hidden), jnp.bfloat16),
        pltpu.VMEM((padded, hidden), jnp.bfloat16),
        pltpu.VMEM((part, padded), jnp.bfloat16),
        pltpu.VMEM((part, padded), jnp.bfloat16),
        pltpu.SemaphoreType.DMA((3 * hidden // (256 if hidden % 256 == 0 else hidden),)),
    ]
    if with_grad:
        shapes += [pltpu.VMEM(back, jnp.bfloat16)] * 2
        specs += [near, near]
    else:
        shapes.append(pltpu.VMEM((8, LANES), jnp.float32))
        specs.append(near)
    if last:
        scratch += [pltpu.VMEM(g, jnp.bfloat16) for g in grads]
    out = pl.pallas_call(
        functools.partial(slot_kernel, picks, len(after), with_grad, first, last),
        out_shape=shapes,
        in_specs=[near] * (6 if first else 8)
        + [pl.BlockSpec(memory_space=pl.ANY)] * len(after),
        out_specs=specs,
        scratch_shapes=scratch,
        input_output_aliases={} if first or last else {6: 0, 7: 1},
        compiler_params=pltpu.CompilerParams(vmem_limit_bytes=(14 if last else 10) << 20),
        cost_estimate=pl.CostEstimate(flops=0, bytes_accessed=0, transcendentals=0),
    )(*arrays, win, wout, *(sums or ()), *after)
    return out[:2], out[2:]


def streamed(tokens, cotangent, expert_ids, combine, gate_up, down_proj):
    width = tokens.shape[1]
    experts = lax.axis_size("expert")
    ids = expert_ids.T

    n_x, n_z = 2, experts // CORES // 2

    def place(z, x, core):
        return (z * n_x + x) * CORES + core

    spots = [(z, x, c) for z in range(n_z) for x in range(n_x) for c in range(CORES)]
    ring = [0] + list(range(1, n_z, 2)) + list(range(2, n_z, 2))[::-1]
    by_z = [
        [
            (place(ring[i], x, c), place(ring[(i + far) % n_z], x, c))
            for i in range(n_z)
            for x in range(n_x)
            for c in range(CORES)
        ]
        for far in range(n_z)
    ]
    over_x = [(place(z, x, c), place(z, 1 - x, c)) for z, x, c in spots]
    over_core = [(place(z, x, c), place(z, x, 1 - c)) for z, x, c in spots]

    def z_hop(a, far=1):
        return lax.ppermute(a, "expert", by_z[far % n_z])

    def x_hop(a):
        return lax.ppermute(a, "expert", over_x)

    def core_hop(a):
        return lax.ppermute(a, "expert", over_core)

    def y_hop(a):
        return lax.ppermute(a, "dp", [(0, 1), (1, 0)])

    sums = None
    win, wout = keep_near(gate_up[0], down_proj[0])

    def run(units, with_grad=False, last=False, after=()):
        nonlocal sums
        sums, rest = slot_pass(units, win, wout, sums, with_grad, last, after)
        return rest

    z0 = first_rows(tokens, cotangent, ids, combine.T, experts)
    z1, x0, y0, z0c = z_hop(z0), x_hop(z0), y_hop(z0), core_hop(z0)
    z1, x0, y0, z0c, pile = gate((z1, x0, y0, z0c), stacks=((x0, z1, y0),), after=(win, wout))

    c1, z2, x1, y1 = core_hop(pile), z_hop(z1), x_hop(z1), y_hop(z1)
    kept0, sent0 = run([(z0, None), (z0c, None), (x0, None), (c1, 0)], with_grad=True)
    z2, x1, y1, sent0, pile = gate((z2, x1, y1, sent0), stacks=((x1, z2, y1),))

    c2, z3, x2, y2, came0 = core_hop(pile), z_hop(z2), x_hop(z2), y_hop(z2), core_hop(sent0)
    part0 = add([(kept0, 1), (came0, 1)], after=(pile,))
    side0 = x_hop(part0)
    kept1, sent1 = run([(z1, None), (c1, 1), (x1, None), (c2, 0)], with_grad=True, after=(part0,))
    (mark,) = run([(y0, None), (c1, 2), (y1, None), (c2, 2)], after=(kept1,))
    home = add(
        [(kept0, 0), (came0, 0), (side0, None)], after=(mark,), dtype=jnp.float32
    )
    z3, x2, y2, sent1, pile = gate((z3, x2, y2, sent1), stacks=((x2, z3, y2),), after=(home,))

    c3, x3, d0, y3, came1 = core_hop(pile), z_hop(x2), x_hop(y0), y_hop(z3), core_hop(sent1)
    part1 = add([(kept1, 1), (came1, 1)], after=(pile,))
    side1 = x_hop(part1)
    kept2, sent2 = run([(z2, None), (c2, 1), (x2, None), (c3, 0)], with_grad=True, after=(part1,))
    sum1 = add([(kept1, 0), (came1, 0), (side1, None)], after=(kept2,))
    x3, d0, y3, sent2, sum1, pile = gate((x3, d0, y3, sent2, sum1), stacks=((x3, y3, d0),))

    c4, d1, d2, d3, came2 = core_hop(pile), z_hop(d0), y_hop(x2), x_hop(y3), core_hop(sent2)
    back1 = z_hop(sum1, -1)
    part2 = add([(kept2, 1), (came2, 1)], after=(pile,))
    side2 = x_hop(part2)
    kept3, sent3 = run([(z3, None), (c3, 1), (x3, None), (c4, 0)], with_grad=True, after=(part2,))
    (mark,) = run([(y2, None), (c3, 2), (y3, None), (c4, 1)], after=(kept3,))
    sum2 = add([(kept2, 0), (came2, 0), (side2, None)], after=(mark,))
    home = add([(home, None), (back1, None)], after=(sum2,), dtype=jnp.float32)
    d1, d2, d3, sent3, sum2, pile = gate(
        (d1, d2, d3, sent3, sum2), stacks=((d1, d2, d3),), after=(home,)
    )

    c5, came3, back2 = core_hop(pile), core_hop(sent3), z_hop(sum2, -2)
    part3 = add([(kept3, 1), (came3, 1)], after=(pile,))
    side3 = x_hop(part3)
    (mark,) = run([(d0, None), (c4, 2), (d1, None), (c5, 0)], after=(part3,))
    sum3 = add([(kept3, 0), (came3, 0), (side3, None)], after=(mark,))
    back3 = z_hop(sum3, -3)
    (mark,) = run([(d2, None), (c5, 1), (d3, None), (c5, 2)], last=True, after=(sum3,))
    grad_tokens, grad_combine = finish(
        [(home, None), (back2, None), (back3, None)], ids, width, after=(mark,)
    )
    return grad_tokens, grad_combine.T, sums[0][None], sums[1][None]


def solution(mesh):
    in_specs = (
        P(("expert", "dp"), None),
        P(("expert", "dp"), None),
        P(("expert", "dp"), None),
        P(("expert", "dp"), None),
        P("expert", None, None),
        P("expert", None, None),
    )
    out_specs = (
        P(("expert", "dp"), None),
        P(("expert", "dp"), None),
        P("expert", "dp", None),
        P("expert", "dp", None),
    )

    def run(tokens, *rest):
        small = tokens.size * 2 <= GATHER_BYTES and mesh.shape["dp"] == 2
        shards = streamed if small and mesh.shape["expert"] == 16 else grouped
        return jax.shard_map(
            shards, mesh=mesh, in_specs=in_specs, out_specs=out_specs, check_vma=False
        )(tokens, *rest)

    return run
```

```python
import functools

import jax
import jax.numpy as jnp
from jax import lax
from jax.experimental import pallas as pl
from jax.experimental.pallas import tpu as pltpu
from jax.sharding import PartitionSpec as P

LANES = 128
CORES = 2
GATHER_BYTES = 16 << 20


def weight_table(expert_ids, combine, experts):
    lanes = jnp.arange(-(-experts // LANES) * LANES, dtype=jnp.int32)
    picks = expert_ids[:, :, None] == lanes
    table = jnp.sum(jnp.where(picks, combine.astype(jnp.float32)[:, :, None], 0.0), axis=1)
    return table.astype(jnp.bfloat16), picks, lanes


def rows_pass(rows, w_in, w_out, me, lanes, with_grad):
    width, hidden = w_out.shape
    tok, cot = rows[:, :width], rows[:, width : 2 * width]
    weight = jnp.sum(
        jnp.where(lanes[None, :] == me, rows[:, 2 * width :].astype(jnp.float32), 0.0),
        axis=1,
        keepdims=True,
    )
    both = jnp.dot(tok, w_in, preferred_element_type=jnp.float32)
    gate, upper = both[:, :hidden], both[:, hidden:]
    sigma = jax.nn.sigmoid(gate)
    swish = gate * sigma
    activ = swish * upper
    cot_down = jnp.dot(cot, w_out, preferred_element_type=jnp.float32)
    grad_act = weight * cot_down
    grad_gate = grad_act * upper * sigma * (1.0 + gate * (1.0 - sigma))
    grad_both = jnp.concatenate([grad_gate, grad_act * swish], axis=1).astype(jnp.bfloat16)
    scaled = (weight * activ).astype(jnp.bfloat16)
    if not with_grad:
        return grad_both, scaled, None
    inner = jnp.sum(activ * cot_down, axis=1, keepdims=True)
    row_grad = lax.dot_general(
        grad_both, w_in, (((1,), (1,)), ((), ())), preferred_element_type=jnp.float32
    ).astype(jnp.bfloat16)
    inner_table = jnp.where(lanes[None, :] == me, inner, 0.0).astype(jnp.bfloat16)
    return grad_both, scaled, jnp.concatenate([row_grad, inner_table], axis=1)


def outer(rows, columns):
    return lax.dot_general(
        rows, columns, (((0,), (0,)), ((), ())), preferred_element_type=jnp.float32
    ).astype(jnp.bfloat16)


def pick_inner(back, picks):
    return jnp.sum(jnp.where(picks, back.astype(jnp.float32)[:, None, :], 0.0), axis=2).astype(
        jnp.bfloat16
    )


def grouped(tokens, cotangent, expert_ids, combine, gate_up, down_proj):
    width = tokens.shape[1]
    me = lax.axis_index("expert")
    table, picks, lanes = weight_table(expert_ids, combine, lax.axis_size("expert"))
    rows = lax.all_gather(
        jnp.concatenate([tokens, cotangent, table], axis=1), "expert", axis=0, tiled=True
    )
    grad_both, scaled, back = rows_pass(rows, gate_up[0], down_proj[0], me, lanes, True)
    back = lax.psum_scatter(back, "expert", scatter_dimension=0, tiled=True)

    def share(term):
        return lax.psum_scatter(term, "dp", scatter_dimension=0, tiled=True)[None]

    return (
        back[:, :width],
        pick_inner(back[:, width:], picks),
        share(outer(rows[:, :width], grad_both)),
        share(outer(rows[:, width : 2 * width], scaled)),
    )


def gate(passed, stacks=(), after=()):
    count = len(passed)
    arrays = list(passed) + list(after)
    places = [
        (g, j, next(i for i, a in enumerate(arrays) if a is member))
        for g, members in enumerate(stacks)
        for j, member in enumerate(members)
    ]

    def kernel(*refs):
        out = refs[len(arrays) + count :]
        copies = [
            pltpu.make_async_copy(refs[i], out[g].at[j], refs[-1].at[n])
            for n, (g, j, i) in enumerate(places)
        ]
        for copy in copies:
            copy.start()
        for copy in copies:
            copy.wait()

    anywhere = pl.BlockSpec(memory_space=pl.ANY)
    shapes = [jax.ShapeDtypeStruct(a.shape, a.dtype) for a in passed]
    shapes += [jax.ShapeDtypeStruct((len(g),) + g[0].shape, g[0].dtype) for g in stacks]
    return pl.pallas_call(
        kernel,
        out_shape=shapes,
        in_specs=[anywhere] * len(arrays),
        out_specs=[anywhere] * count + [pl.BlockSpec(memory_space=pltpu.VMEM)] * len(stacks),
        scratch_shapes=[pltpu.SemaphoreType.DMA((max(1, len(places)),))],
        input_output_aliases={i: i for i in range(count)},
        compiler_params=pltpu.CompilerParams(vmem_limit_bytes=4 << 20),
    )(*arrays)


def add(terms, after=(), dtype=jnp.bfloat16):
    arrays, picks = zip(*terms)
    anywhere = pl.BlockSpec(memory_space=pl.ANY)
    near = pl.BlockSpec(memory_space=pltpu.VMEM)

    def kernel(*refs):
        parts = [ref if k is None else ref.at[k] for ref, k in zip(refs, picks)]
        total = parts[0][...].astype(jnp.float32)
        for part in parts[1:]:
            total += part[...].astype(jnp.float32)
        refs[-1][...] = total.astype(dtype)

    return pl.pallas_call(
        kernel,
        out_shape=jax.ShapeDtypeStruct(arrays[0].shape[-2:], dtype),
        in_specs=[near] * len(arrays) + [anywhere] * len(after),
        compiler_params=pltpu.CompilerParams(vmem_limit_bytes=6 << 20),
    )(*arrays, *after)


def finish(terms, ids, width, after):
    arrays, picks = zip(*terms)
    top, tok_rows = ids.shape
    anywhere = pl.BlockSpec(memory_space=pl.ANY)
    near = pl.BlockSpec(memory_space=pltpu.VMEM)

    def kernel(ids, *refs):
        parts = [ref if k is None else ref.at[k] for ref, k in zip(refs, picks)]
        out, chosen, rows = refs[-3:]
        total = parts[0][...].astype(jnp.float32)
        for part in parts[1:]:
            total += part[...].astype(jnp.float32)
        out[...] = total[:, :width].astype(jnp.bfloat16)
        table = total[:, width:].T
        line = lax.broadcasted_iota(jnp.int32, table.shape, 0)
        for k in range(top):
            picked = jnp.where(line == ids[k : k + 1, :], table, 0.0)
            rows[k : k + 1, :] = jnp.sum(picked, axis=0, keepdims=True)
        chosen[...] = rows[...].astype(jnp.bfloat16)

    return pl.pallas_call(
        kernel,
        out_shape=[
            jax.ShapeDtypeStruct((tok_rows, width), jnp.bfloat16),
            jax.ShapeDtypeStruct((top, tok_rows), jnp.bfloat16),
        ],
        scratch_shapes=[pltpu.VMEM((top, tok_rows), jnp.float32)],
        in_specs=[near] * (1 + len(arrays)) + [anywhere] * len(after),
        compiler_params=pltpu.CompilerParams(vmem_limit_bytes=6 << 20),
    )(ids, *arrays, *after)


def first_rows(tokens, cotangent, ids, combine, experts):
    top, tok_rows = ids.shape
    width = tokens.shape[1]
    extra = -(-experts // LANES) * LANES

    def kernel(tok, cot, ids, combine, out):
        out[:, :width] = tok[...]
        out[:, width : 2 * width] = cot[...]
        line = lax.broadcasted_iota(jnp.int32, (extra, tok_rows), 0)
        share = combine[...].astype(jnp.float32)
        table = jnp.zeros((extra, tok_rows), jnp.float32)
        for k in range(top):
            table += jnp.where(line == ids[k : k + 1, :], share[k : k + 1, :], 0.0)
        out[:, 2 * width :] = table.T.astype(jnp.bfloat16)

    return pl.pallas_call(
        kernel,
        out_shape=jax.ShapeDtypeStruct((tok_rows, 2 * width + extra), jnp.bfloat16),
        compiler_params=pltpu.CompilerParams(vmem_limit_bytes=4 << 20),
    )(tokens, cotangent, ids, combine)


def keep_near(*arrays):
    def kernel(*refs):
        count = len(arrays)
        copies = [
            pltpu.make_async_copy(refs[i], refs[count + i], refs[-1].at[i]) for i in range(count)
        ]
        for copy in copies:
            copy.start()
        for copy in copies:
            copy.wait()

    return pl.pallas_call(
        kernel,
        out_shape=[pltpu.VMEM(a.shape, a.dtype) for a in arrays],
        in_specs=[pl.BlockSpec(memory_space=pltpu.HBM)] * len(arrays),
        out_specs=[pl.BlockSpec(memory_space=pltpu.VMEM)] * len(arrays),
        scratch_shapes=[pltpu.SemaphoreType.DMA((len(arrays),))],
        compiler_params=pltpu.CompilerParams(vmem_limit_bytes=44 << 20),
    )(*arrays)


def slot_kernel(picks, waits, with_grad, first, last, *refs):
    units = [ref if k is None else ref.at[k] for ref, k in zip(refs[:4], picks)]
    win, wout = refs[4:6]
    refs = refs[6:]
    if not first:
        old_up, old_down = refs[:2]
        refs = refs[2:]
    refs = refs[waits:]
    new_up, new_down = refs[:2]
    refs = refs[2:]
    if with_grad:
        kept, sent = refs[0], refs[1 : 1 + with_grad]
        sent = [sent[0].at[0], sent[0].at[1]] if with_grad == 1 else sent
        refs = refs[1 + with_grad :]
    else:
        refs[0][...] = jnp.zeros_like(refs[0])
        refs = refs[1:]
    tok, cot, both, scaled, tok_t, cot_t, sems = refs[:7]
    refs = refs[7:]
    if last:
        done_up, done_down = refs[:2]

    width, hidden = wout.shape
    tok_rows, wide = units[0].shape
    rows = 4 * tok_rows
    spare = tok.shape[0] - rows
    part = tok_t.shape[0]
    me, mine = lax.axis_index("expert"), lax.axis_index("dp")
    for padded in (tok, cot, both, scaled) if spare else ():
        padded[pl.ds(rows, spare), :] = jnp.zeros((spare, padded.shape[1]), jnp.bfloat16)

    weights = []
    for i in (0, 2):
        span = pl.ds(i * tok_rows, 2 * tok_rows)
        for target, start in ((tok, 0), (cot, width)):
            joined = [units[j][:, pl.ds(start, width)].astype(jnp.float32) for j in (i, i + 1)]
            target[span, :] = jnp.concatenate(joined, axis=0).astype(jnp.bfloat16)
        for j in (i, i + 1):
            table = units[j][:, pl.ds(2 * width, wide - 2 * width)].astype(jnp.float32)
            lane = lax.broadcasted_iota(jnp.int32, table.shape, 1)
            weights.append(jnp.sum(jnp.where(lane == me, table, 0.0), axis=1, keepdims=True))
    weight = jnp.concatenate(weights, axis=0)

    real = pl.ds(0, rows)
    step = 256 if hidden % 256 == 0 else hidden
    inner = jnp.zeros_like(weight)
    for j in range(hidden // step):
        gates, uppers = pl.ds(j * step, step), pl.ds(hidden + j * step, step)
        gate_x = jnp.dot(tok[real, :], win[:, gates], preferred_element_type=jnp.float32)
        upper = jnp.dot(tok[real, :], win[:, uppers], preferred_element_type=jnp.float32)
        cot_down = jnp.dot(cot[real, :], wout[:, gates], preferred_element_type=jnp.float32)
        sigma = 1.0 / (1.0 + jnp.exp(-gate_x))
        swish = gate_x * sigma
        activ = swish * upper
        grad_act = weight * cot_down
        both[real, gates] = (grad_act * upper * sigma * (1.0 + gate_x * (1.0 - sigma))).astype(
            jnp.bfloat16
        )
        both[real, uppers] = (grad_act * swish).astype(jnp.bfloat16)
        scaled[real, gates] = (weight * activ).astype(jnp.bfloat16)
        if with_grad:
            inner += jnp.sum(activ * cot_down, axis=1, keepdims=True)

    leave = []
    if with_grad:

        def back(columns, value):
            for i in range(4):
                target = sent[i // 2] if i % 2 else kept.at[i // 2]
                target[:, columns] = value[i * tok_rows : (i + 1) * tok_rows].astype(jnp.bfloat16)

        for start in range(0, width, 512):
            span = pl.ds(start, min(512, width - start))
            term = lax.dot_general(
                both[real, :],
                win[span, :],
                (((1,), (1,)), ((), ())),
                preferred_element_type=jnp.float32,
            )
            back(span, term)
        lane = lax.broadcasted_iota(jnp.int32, (rows, wide - 2 * width), 1)
        back(pl.ds(width, wide - 2 * width), jnp.where(lane == me, inner, 0.0))

    columns = pl.ds(pl.multiple_of(mine * part, part), part)
    tok_t[...] = tok[:, columns].T
    cot_t[...] = cot[:, columns].T
    sides = [
        (tok_t, both, None if first else old_up, new_up, done_up if last else None),
        (cot_t, scaled, None if first else old_down, new_down, done_down if last else None),
    ]
    place = 0
    for left, right, old, new, done in sides:
        for start in range(0, right.shape[1], step):
            span = pl.ds(start, step)
            term = jnp.dot(left[...], right[:, span], preferred_element_type=jnp.float32)
            if not first:
                term += old[:, span]
            if not last:
                new[:, span] = term
                continue
            done[:, span] = term.astype(jnp.bfloat16)
            leave.append(
                pltpu.make_async_copy(done.at[:, span], new.at[:, span], sems.at[place])
            )
            leave[-1].start()
            place += 1
    for copy in leave:
        copy.wait()


def slot_pass(units, win, wout, sums, with_grad, last, after):
    width, hidden = wout.shape
    arrays, picks = zip(*units)
    tok_rows, wide = arrays[0].shape[-2:]
    rows = 4 * tok_rows
    padded = -(-rows // LANES) * LANES
    part = width // 2
    first = sums is None
    near, far = pl.BlockSpec(memory_space=pltpu.VMEM), pl.BlockSpec(memory_space=pltpu.HBM)
    grads = [(part, 2 * hidden), (part, hidden)]
    if last:
        shapes, specs = [pltpu.HBM(g, jnp.bfloat16) for g in grads], [far, far]
    else:
        shapes, specs = [pltpu.VMEM(g, jnp.float32) for g in grads], [near, near]
    back = (2, tok_rows, wide - width)
    scratch = [
        pltpu.VMEM((padded, width), jnp.bfloat16),
        pltpu.VMEM((padded, width), jnp.bfloat16),
        pltpu.VMEM((padded, 2 * hidden), jnp.bfloat16),
        pltpu.VMEM((padded, hidden), jnp.bfloat16),
        pltpu.VMEM((part, padded), jnp.bfloat16),
        pltpu.VMEM((part, padded), jnp.bfloat16),
        pltpu.SemaphoreType.DMA((3 * hidden // (256 if hidden % 256 == 0 else hidden),)),
    ]
    if with_grad:
        shapes.append(pltpu.VMEM(back, jnp.bfloat16))
        shapes += [pltpu.VMEM(back[with_grad - 1 :], jnp.bfloat16)] * with_grad
        specs += [near] * (1 + with_grad)
    else:
        shapes.append(pltpu.VMEM((8, LANES), jnp.float32))
        specs.append(near)
    if last:
        scratch += [pltpu.VMEM(g, jnp.bfloat16) for g in grads]
    out = pl.pallas_call(
        functools.partial(slot_kernel, picks, len(after), with_grad, first, last),
        out_shape=shapes,
        in_specs=[near] * (6 if first else 8)
        + [pl.BlockSpec(memory_space=pl.ANY)] * len(after),
        out_specs=specs,
        scratch_shapes=scratch,
        input_output_aliases={} if first or last else {6: 0, 7: 1},
        compiler_params=pltpu.CompilerParams(vmem_limit_bytes=(14 if last else 10) << 20),
        cost_estimate=pl.CostEstimate(flops=0, bytes_accessed=0, transcendentals=0),
    )(*arrays, win, wout, *(sums or ()), *after)
    return out[:2], out[2:]


def streamed(tokens, cotangent, expert_ids, combine, gate_up, down_proj):
    width = tokens.shape[1]
    experts = lax.axis_size("expert")
    ids = expert_ids.T

    n_x, n_z = 2, experts // CORES // 2

    def place(z, x, core):
        return (z * n_x + x) * CORES + core

    spots = [(z, x, c) for z in range(n_z) for x in range(n_x) for c in range(CORES)]
    ring = [0] + list(range(1, n_z, 2)) + list(range(2, n_z, 2))[::-1]
    by_z = [
        [
            (place(ring[i], x, c), place(ring[(i + far) % n_z], x, c))
            for i in range(n_z)
            for x in range(n_x)
            for c in range(CORES)
        ]
        for far in range(n_z)
    ]
    over_x = [(place(z, x, c), place(z, 1 - x, c)) for z, x, c in spots]
    over_core = [(place(z, x, c), place(z, x, 1 - c)) for z, x, c in spots]

    def z_hop(a, far=1):
        return lax.ppermute(a, "expert", by_z[far % n_z])

    def x_hop(a):
        return lax.ppermute(a, "expert", over_x)

    def core_hop(a):
        return lax.ppermute(a, "expert", over_core)

    def y_hop(a):
        return lax.ppermute(a, "dp", [(0, 1), (1, 0)])

    sums = None
    win, wout = keep_near(gate_up[0], down_proj[0])

    def run(units, with_grad=False, last=False, after=()):
        nonlocal sums
        sums, rest = slot_pass(units, win, wout, sums, with_grad, last, after)
        return rest

    z0 = first_rows(tokens, cotangent, ids, combine.T, experts)
    z1, x0, y0, z0c = z_hop(z0), x_hop(z0), y_hop(z0), core_hop(z0)
    z1, x0, y0, z0c, pile = gate((z1, x0, y0, z0c), stacks=((x0, z1, y0),), after=(win, wout))

    c1, z2, x1, y1 = core_hop(pile), z_hop(z1), x_hop(z1), y_hop(z1)
    kept0, sent0 = run([(z0, None), (z0c, None), (x0, None), (c1, 0)], with_grad=1)
    z2, x1, y1, sent0, pile = gate((z2, x1, y1, sent0), stacks=((x1, z2, y1),))

    c2, z3, x2, y2, came0 = core_hop(pile), z_hop(z2), x_hop(z2), y_hop(z2), core_hop(sent0)
    part0 = add([(kept0, 1), (came0, 1)], after=(pile,))
    side0 = x_hop(part0)
    kept1, sent1 = run([(z1, None), (c1, 1), (x1, None), (c2, 0)], with_grad=1, after=(part0,))
    (mark,) = run([(y0, None), (c1, 2), (y1, None), (c2, 2)], after=(kept1,))
    home = add(
        [(kept0, 0), (came0, 0), (side0, None)], after=(mark,), dtype=jnp.float32
    )
    z3, x2, y2, sent1, pile = gate((z3, x2, y2, sent1), stacks=((x2, z3, y2),), after=(home,))

    c3, x3, d0, y3, came1 = core_hop(pile), z_hop(x2), x_hop(y0), y_hop(z3), core_hop(sent1)
    part1 = add([(kept1, 1), (came1, 1)], after=(pile,))
    kept2, sent2 = run([(z2, None), (c2, 1), (x2, None), (c3, 0)], with_grad=1, after=(part1,))
    x3, d0, y3, sent2, part1, pile, pair = gate(
        (x3, d0, y3, sent2, part1), stacks=((x3, y3, d0), (x2, x3)), after=(kept2, x2)
    )

    c4, d1, d23, came2 = core_hop(pile), z_hop(d0), y_hop(pair), core_hop(sent2)
    side1 = x_hop(part1)
    part2 = add([(kept2, 1), (came2, 1)], after=(pile,))
    side2 = x_hop(part2)
    kept3, sent3a, sent3b = run(
        [(z3, None), (c3, 1), (x3, None), (c4, 0)], with_grad=2, after=(part2,)
    )
    came3b, came3a = core_hop(sent3b), core_hop(sent3a)
    sum1 = add([(kept1, 0), (came1, 0), (side1, None)], after=(kept3,))
    (mark,) = run([(y2, None), (c3, 2), (y3, None), (c4, 1)], after=(sum1,))
    part3 = add([(kept3, 1), (came3b, None)], after=(mark,))
    sum2 = add([(kept2, 0), (came2, 0), (side2, None)], after=(part3,))
    home = add([(home, None), (z_hop(sum1, -1), None)], after=(sum2,), dtype=jnp.float32)
    d1, d23, sum2 = gate((d1, d23, sum2), after=(home,))

    c5, c6, side3 = core_hop(d1), core_hop(d23), x_hop(part3)
    back2 = z_hop(sum2, -2)
    (mark,) = run([(d0, None), (c4, 2), (d1, None), (c5, None)], after=(d1,))
    sum3 = add([(kept3, 0), (came3a, None), (side3, None)], after=(mark,))
    back3 = z_hop(sum3, -3)
    (mark,) = run([(d23, 0), (c6, 0), (d23, 1), (c6, 1)], last=True, after=(sum3,))
    grad_tokens, grad_combine = finish(
        [(home, None), (back2, None), (back3, None)], ids, width, after=(mark,)
    )
    return grad_tokens, grad_combine.T, sums[0][None], sums[1][None]


def solution(mesh):
    in_specs = (
        P(("expert", "dp"), None),
        P(("expert", "dp"), None),
        P(("expert", "dp"), None),
        P(("expert", "dp"), None),
        P("expert", None, None),
        P("expert", None, None),
    )
    out_specs = (
        P(("expert", "dp"), None),
        P(("expert", "dp"), None),
        P("expert", "dp", None),
        P("expert", "dp", None),
    )

    def run(tokens, *rest):
        small = tokens.size * 2 <= GATHER_BYTES and mesh.shape["dp"] == 2
        shards = streamed if small and mesh.shape["expert"] == 16 else grouped
        return jax.shard_map(
            shards, mesh=mesh, in_specs=in_specs, out_specs=out_specs, check_vma=False
        )(tokens, *rest)

    return run
```

```python
import functools

import jax
import jax.numpy as jnp
from jax import lax
from jax.experimental import pallas as pl
from jax.experimental.pallas import tpu as pltpu
from jax.sharding import PartitionSpec as P

LANES = 128
CORES = 2
GATHER_BYTES = 16 << 20


def weight_table(expert_ids, combine, experts):
    lanes = jnp.arange(-(-experts // LANES) * LANES, dtype=jnp.int32)
    picks = expert_ids[:, :, None] == lanes
    table = jnp.sum(jnp.where(picks, combine.astype(jnp.float32)[:, :, None], 0.0), axis=1)
    return table.astype(jnp.bfloat16), picks, lanes


def rows_pass(rows, w_in, w_out, me, lanes, with_grad):
    width, hidden = w_out.shape
    tok, cot = rows[:, :width], rows[:, width : 2 * width]
    weight = jnp.sum(
        jnp.where(lanes[None, :] == me, rows[:, 2 * width :].astype(jnp.float32), 0.0),
        axis=1,
        keepdims=True,
    )
    both = jnp.dot(tok, w_in, preferred_element_type=jnp.float32)
    gate, upper = both[:, :hidden], both[:, hidden:]
    sigma = jax.nn.sigmoid(gate)
    swish = gate * sigma
    activ = swish * upper
    cot_down = jnp.dot(cot, w_out, preferred_element_type=jnp.float32)
    grad_act = weight * cot_down
    grad_gate = grad_act * upper * sigma * (1.0 + gate * (1.0 - sigma))
    grad_both = jnp.concatenate([grad_gate, grad_act * swish], axis=1).astype(jnp.bfloat16)
    scaled = (weight * activ).astype(jnp.bfloat16)
    if not with_grad:
        return grad_both, scaled, None
    inner = jnp.sum(activ * cot_down, axis=1, keepdims=True)
    row_grad = lax.dot_general(
        grad_both, w_in, (((1,), (1,)), ((), ())), preferred_element_type=jnp.float32
    ).astype(jnp.bfloat16)
    inner_table = jnp.where(lanes[None, :] == me, inner, 0.0).astype(jnp.bfloat16)
    return grad_both, scaled, jnp.concatenate([row_grad, inner_table], axis=1)


def outer(rows, columns):
    return lax.dot_general(
        rows, columns, (((0,), (0,)), ((), ())), preferred_element_type=jnp.float32
    ).astype(jnp.bfloat16)


def pick_inner(back, picks):
    return jnp.sum(jnp.where(picks, back.astype(jnp.float32)[:, None, :], 0.0), axis=2).astype(
        jnp.bfloat16
    )


def grouped(tokens, cotangent, expert_ids, combine, gate_up, down_proj):
    width = tokens.shape[1]
    me = lax.axis_index("expert")
    table, picks, lanes = weight_table(expert_ids, combine, lax.axis_size("expert"))
    rows = lax.all_gather(
        jnp.concatenate([tokens, cotangent, table], axis=1), "expert", axis=0, tiled=True
    )
    grad_both, scaled, back = rows_pass(rows, gate_up[0], down_proj[0], me, lanes, True)
    back = lax.psum_scatter(back, "expert", scatter_dimension=0, tiled=True)

    def share(term):
        return lax.psum_scatter(term, "dp", scatter_dimension=0, tiled=True)[None]

    return (
        back[:, :width],
        pick_inner(back[:, width:], picks),
        share(outer(rows[:, :width], grad_both)),
        share(outer(rows[:, width : 2 * width], scaled)),
    )


def gate(passed, stacks=(), after=()):
    count = len(passed)
    arrays = list(passed) + list(after)
    places = [
        (g, j, next(i for i, a in enumerate(arrays) if a is member))
        for g, members in enumerate(stacks)
        for j, member in enumerate(members)
    ]

    def kernel(*refs):
        out = refs[len(arrays) + count :]
        copies = [
            pltpu.make_async_copy(refs[i], out[g].at[j], refs[-1].at[n])
            for n, (g, j, i) in enumerate(places)
        ]
        for copy in copies:
            copy.start()
        for copy in copies:
            copy.wait()

    anywhere = pl.BlockSpec(memory_space=pl.ANY)
    shapes = [jax.ShapeDtypeStruct(a.shape, a.dtype) for a in passed]
    shapes += [jax.ShapeDtypeStruct((len(g),) + g[0].shape, g[0].dtype) for g in stacks]
    return pl.pallas_call(
        kernel,
        out_shape=shapes,
        in_specs=[anywhere] * len(arrays),
        out_specs=[anywhere] * count + [pl.BlockSpec(memory_space=pltpu.VMEM)] * len(stacks),
        scratch_shapes=[pltpu.SemaphoreType.DMA((max(1, len(places)),))],
        input_output_aliases={i: i for i in range(count)},
        compiler_params=pltpu.CompilerParams(vmem_limit_bytes=4 << 20),
    )(*arrays)


def add(terms, after=(), dtype=jnp.bfloat16):
    arrays, picks = zip(*terms)
    anywhere = pl.BlockSpec(memory_space=pl.ANY)
    near = pl.BlockSpec(memory_space=pltpu.VMEM)

    def kernel(*refs):
        parts = [ref if k is None else ref.at[k] for ref, k in zip(refs, picks)]
        total = parts[0][...].astype(jnp.float32)
        for part in parts[1:]:
            total += part[...].astype(jnp.float32)
        refs[-1][...] = total.astype(dtype)

    return pl.pallas_call(
        kernel,
        out_shape=jax.ShapeDtypeStruct(arrays[0].shape[-2:], dtype),
        in_specs=[near] * len(arrays) + [anywhere] * len(after),
        compiler_params=pltpu.CompilerParams(vmem_limit_bytes=6 << 20),
    )(*arrays, *after)


def finish(terms, ids, width, after):
    arrays, picks = zip(*terms)
    top, tok_rows = ids.shape
    anywhere = pl.BlockSpec(memory_space=pl.ANY)
    near = pl.BlockSpec(memory_space=pltpu.VMEM)

    def kernel(ids, *refs):
        parts = [ref if k is None else ref.at[k] for ref, k in zip(refs, picks)]
        out, chosen, rows = refs[-3:]
        total = parts[0][...].astype(jnp.float32)
        for part in parts[1:]:
            total += part[...].astype(jnp.float32)
        out[...] = total[:, :width].astype(jnp.bfloat16)
        table = total[:, width:].T
        line = lax.broadcasted_iota(jnp.int32, table.shape, 0)
        for k in range(top):
            picked = jnp.where(line == ids[k : k + 1, :], table, 0.0)
            rows[k : k + 1, :] = jnp.sum(picked, axis=0, keepdims=True)
        chosen[...] = rows[...].astype(jnp.bfloat16)

    return pl.pallas_call(
        kernel,
        out_shape=[
            jax.ShapeDtypeStruct((tok_rows, width), jnp.bfloat16),
            jax.ShapeDtypeStruct((top, tok_rows), jnp.bfloat16),
        ],
        scratch_shapes=[pltpu.VMEM((top, tok_rows), jnp.float32)],
        in_specs=[near] * (1 + len(arrays)) + [anywhere] * len(after),
        compiler_params=pltpu.CompilerParams(vmem_limit_bytes=6 << 20),
    )(ids, *arrays, *after)


def first_rows(tokens, cotangent, ids, combine, experts):
    top, tok_rows = ids.shape
    width = tokens.shape[1]
    extra = -(-experts // LANES) * LANES

    def kernel(tok, cot, ids, combine, out):
        out[:, :width] = tok[...]
        out[:, width : 2 * width] = cot[...]
        line = lax.broadcasted_iota(jnp.int32, (extra, tok_rows), 0)
        share = combine[...].astype(jnp.float32)
        table = jnp.zeros((extra, tok_rows), jnp.float32)
        for k in range(top):
            table += jnp.where(line == ids[k : k + 1, :], share[k : k + 1, :], 0.0)
        out[:, 2 * width :] = table.T.astype(jnp.bfloat16)

    return pl.pallas_call(
        kernel,
        out_shape=jax.ShapeDtypeStruct((tok_rows, 2 * width + extra), jnp.bfloat16),
        compiler_params=pltpu.CompilerParams(vmem_limit_bytes=4 << 20),
    )(tokens, cotangent, ids, combine)


def keep_near(*arrays):
    def kernel(*refs):
        count = len(arrays)
        copies = [
            pltpu.make_async_copy(refs[i], refs[count + i], refs[-1].at[i]) for i in range(count)
        ]
        for copy in copies:
            copy.start()
        for copy in copies:
            copy.wait()

    return pl.pallas_call(
        kernel,
        out_shape=[pltpu.VMEM(a.shape, a.dtype) for a in arrays],
        in_specs=[pl.BlockSpec(memory_space=pltpu.HBM)] * len(arrays),
        out_specs=[pl.BlockSpec(memory_space=pltpu.VMEM)] * len(arrays),
        scratch_shapes=[pltpu.SemaphoreType.DMA((len(arrays),))],
        compiler_params=pltpu.CompilerParams(vmem_limit_bytes=44 << 20),
    )(*arrays)


def slot_kernel(picks, waits, with_grad, first, last, *refs):
    count = len(picks)
    units = [ref if k is None else ref.at[k] for ref, k in zip(refs[:count], picks)]
    win, wout = refs[count : count + 2]
    refs = refs[count + 2 :]
    if not first:
        old_up, old_down = refs[:2]
        refs = refs[2:]
    refs = refs[waits:]
    new_up, new_down = refs[:2]
    refs = refs[2:]
    if with_grad:
        kept, sent = refs[0], refs[1 : 1 + with_grad]
        sent = [sent[0].at[0], sent[0].at[1]] if with_grad == 1 else sent
        refs = refs[1 + with_grad :]
    else:
        refs[0][...] = jnp.zeros_like(refs[0])
        refs = refs[1:]
    tok, cot, both, scaled, tok_t, cot_t, sems = refs[:7]
    refs = refs[7:]
    if last:
        done_up, done_down = refs[:2]

    width, hidden = wout.shape
    tok_rows, wide = units[0].shape
    rows = count * tok_rows
    back_rows = 4 * tok_rows
    spare = tok.shape[0] - rows
    part = tok_t.shape[0]
    me, mine = lax.axis_index("expert"), lax.axis_index("dp")
    for padded in (tok, cot, both, scaled) if spare else ():
        padded[pl.ds(rows, spare), :] = jnp.zeros((spare, padded.shape[1]), jnp.bfloat16)

    weights = []
    for i in range(0, count, 2):
        span = pl.ds(i * tok_rows, 2 * tok_rows)
        for target, start in ((tok, 0), (cot, width)):
            joined = [units[j][:, pl.ds(start, width)].astype(jnp.float32) for j in (i, i + 1)]
            target[span, :] = jnp.concatenate(joined, axis=0).astype(jnp.bfloat16)
        for j in (i, i + 1):
            table = units[j][:, pl.ds(2 * width, wide - 2 * width)].astype(jnp.float32)
            lane = lax.broadcasted_iota(jnp.int32, table.shape, 1)
            weights.append(jnp.sum(jnp.where(lane == me, table, 0.0), axis=1, keepdims=True))
    weight = jnp.concatenate(weights, axis=0)

    real = pl.ds(0, rows)
    pair = jnp.dot(tok[real, :], win[...], preferred_element_type=jnp.float32)
    gate_x, upper = pair[:, :hidden], pair[:, hidden:]
    cot_down = jnp.dot(cot[real, :], wout[...], preferred_element_type=jnp.float32)
    sigma = 1.0 / (1.0 + jnp.exp(-gate_x))
    swish = gate_x * sigma
    activ = swish * upper
    grad_act = weight * cot_down
    both[real, :hidden] = (grad_act * upper * sigma * (1.0 + gate_x * (1.0 - sigma))).astype(
        jnp.bfloat16
    )
    both[real, hidden:] = (grad_act * swish).astype(jnp.bfloat16)
    scaled[real, :] = (weight * activ).astype(jnp.bfloat16)
    inner = jnp.sum((activ * cot_down)[:back_rows], axis=1, keepdims=True) if with_grad else None

    leave = []
    if with_grad:

        def back(columns, value):
            for i in range(4):
                target = sent[i // 2] if i % 2 else kept.at[i // 2]
                target[:, columns] = value[i * tok_rows : (i + 1) * tok_rows].astype(jnp.bfloat16)

        for start in range(0, width, 1024):
            span = pl.ds(start, min(1024, width - start))
            term = lax.dot_general(
                both[pl.ds(0, back_rows), :],
                win[span, :],
                (((1,), (1,)), ((), ())),
                preferred_element_type=jnp.float32,
            )
            back(span, term)
        lane = lax.broadcasted_iota(jnp.int32, (back_rows, wide - 2 * width), 1)
        back(pl.ds(width, wide - 2 * width), jnp.where(lane == me, inner, 0.0))

    columns = pl.ds(pl.multiple_of(mine * part, part), part)
    tok_t[...] = tok[:, columns].T
    cot_t[...] = cot[:, columns].T
    sides = [
        (tok_t, both, None if first else old_up, new_up, done_up if last else None),
        (cot_t, scaled, None if first else old_down, new_down, done_down if last else None),
    ]
    place = 0
    for left, right, old, new, done in sides:
        for start in range(0, right.shape[1], 512):
            span = pl.ds(start, min(512, right.shape[1] - start))
            term = jnp.dot(left[...], right[:, span], preferred_element_type=jnp.float32)
            if not first:
                term += old[:, span]
            if not last:
                new[:, span] = term
                continue
            done[:, span] = term.astype(jnp.bfloat16)
            leave.append(
                pltpu.make_async_copy(done.at[:, span], new.at[:, span], sems.at[place])
            )
            leave[-1].start()
            place += 1
    for copy in leave:
        copy.wait()


def slot_pass(units, win, wout, sums, with_grad, last, after):
    width, hidden = wout.shape
    arrays, picks = zip(*units)
    tok_rows, wide = arrays[0].shape[-2:]
    rows = len(units) * tok_rows
    padded = -(-rows // LANES) * LANES
    part = width // 2
    first = sums is None
    near, far = pl.BlockSpec(memory_space=pltpu.VMEM), pl.BlockSpec(memory_space=pltpu.HBM)
    grads = [(part, 2 * hidden), (part, hidden)]
    if last:
        shapes, specs = [pltpu.HBM(g, jnp.bfloat16) for g in grads], [far, far]
    else:
        shapes, specs = [pltpu.VMEM(g, jnp.float32) for g in grads], [near, near]
    back = (2, tok_rows, wide - width)
    scratch = [
        pltpu.VMEM((padded, width), jnp.bfloat16),
        pltpu.VMEM((padded, width), jnp.bfloat16),
        pltpu.VMEM((padded, 2 * hidden), jnp.bfloat16),
        pltpu.VMEM((padded, hidden), jnp.bfloat16),
        pltpu.VMEM((part, padded), jnp.bfloat16),
        pltpu.VMEM((part, padded), jnp.bfloat16),
        pltpu.SemaphoreType.DMA((-(-2 * hidden // 512) - (-hidden // 512),)),
    ]
    if with_grad:
        shapes.append(pltpu.VMEM(back, jnp.bfloat16))
        shapes += [pltpu.VMEM(back[with_grad - 1 :], jnp.bfloat16)] * with_grad
        specs += [near] * (1 + with_grad)
    else:
        shapes.append(pltpu.VMEM((8, LANES), jnp.float32))
        specs.append(near)
    if last:
        scratch += [pltpu.VMEM(g, jnp.bfloat16) for g in grads]
    out = pl.pallas_call(
        functools.partial(slot_kernel, picks, len(after), with_grad, first, last),
        out_shape=shapes,
        in_specs=[near] * (len(units) + (2 if first else 4))
        + [pl.BlockSpec(memory_space=pl.ANY)] * len(after),
        out_specs=specs,
        scratch_shapes=scratch,
        input_output_aliases={} if first or last else {len(units) + 2: 0, len(units) + 3: 1},
        compiler_params=pltpu.CompilerParams(vmem_limit_bytes=(22 if last else 20) << 20),
        cost_estimate=pl.CostEstimate(flops=0, bytes_accessed=0, transcendentals=0),
    )(*arrays, win, wout, *(sums or ()), *after)
    return out[:2], out[2:]


def streamed(tokens, cotangent, expert_ids, combine, gate_up, down_proj):
    width = tokens.shape[1]
    experts = lax.axis_size("expert")
    ids = expert_ids.T

    n_x, n_z = 2, experts // CORES // 2

    def place(z, x, core):
        return (z * n_x + x) * CORES + core

    spots = [(z, x, c) for z in range(n_z) for x in range(n_x) for c in range(CORES)]
    ring = [0] + list(range(1, n_z, 2)) + list(range(2, n_z, 2))[::-1]
    by_z = [
        [
            (place(ring[i], x, c), place(ring[(i + far) % n_z], x, c))
            for i in range(n_z)
            for x in range(n_x)
            for c in range(CORES)
        ]
        for far in range(n_z)
    ]
    over_x = [(place(z, x, c), place(z, 1 - x, c)) for z, x, c in spots]
    over_core = [(place(z, x, c), place(z, x, 1 - c)) for z, x, c in spots]

    def z_hop(a, far=1):
        return lax.ppermute(a, "expert", by_z[far % n_z])

    def x_hop(a):
        return lax.ppermute(a, "expert", over_x)

    def core_hop(a):
        return lax.ppermute(a, "expert", over_core)

    def y_hop(a):
        return lax.ppermute(a, "dp", [(0, 1), (1, 0)])

    sums = None
    win, wout = keep_near(gate_up[0], down_proj[0])

    def run(units, with_grad=False, last=False, after=()):
        nonlocal sums
        sums, rest = slot_pass(units, win, wout, sums, with_grad, last, after)
        return rest

    z0 = first_rows(tokens, cotangent, ids, combine.T, experts)
    z1, x0, y0, z0c = z_hop(z0), x_hop(z0), y_hop(z0), core_hop(z0)
    z1, x0, y0, z0c, pile = gate((z1, x0, y0, z0c), stacks=((x0, z1, y0),), after=(win, wout))

    c1, z2, x1, y1 = core_hop(pile), z_hop(z1), x_hop(z1), y_hop(z1)
    kept0, sent0 = run(
        [(z0, None), (z0c, None), (x0, None), (c1, 0), (y0, None), (c1, 2)], with_grad=1
    )
    z2, x1, y1, sent0, pile = gate((z2, x1, y1, sent0), stacks=((x1, z2, y1),))

    c2, z3, x2, y2, came0 = core_hop(pile), z_hop(z2), x_hop(z2), y_hop(z2), core_hop(sent0)
    part0 = add([(kept0, 1), (came0, 1)], after=(pile,))
    side0 = x_hop(part0)
    kept1, sent1 = run(
        [(z1, None), (c1, 1), (x1, None), (c2, 0), (y1, None), (c2, 2)],
        with_grad=1,
        after=(part0,),
    )
    home = add([(kept0, 0), (came0, 0), (side0, None)], after=(kept1,), dtype=jnp.float32)
    z3, x2, y2, sent1, pile = gate((z3, x2, y2, sent1), stacks=((x2, z3, y2),), after=(home,))

    c3, x3, d0, y3, came1 = core_hop(pile), z_hop(x2), x_hop(y0), y_hop(z3), core_hop(sent1)
    part1 = add([(kept1, 1), (came1, 1)], after=(pile,))
    kept2, sent2 = run(
        [(z2, None), (c2, 1), (x2, None), (c3, 0), (y2, None), (c3, 2)],
        with_grad=1,
        after=(part1,),
    )
    x3, d0, y3, sent2, part1, pile, pair = gate(
        (x3, d0, y3, sent2, part1), stacks=((x3, y3, d0), (x2, x3)), after=(kept2, x2)
    )

    c4, d1, d23, came2 = core_hop(pile), z_hop(d0), y_hop(pair), core_hop(sent2)
    side1 = x_hop(part1)
    part2 = add([(kept2, 1), (came2, 1)], after=(pile,))
    side2 = x_hop(part2)
    kept3, sent3a, sent3b = run(
        [(z3, None), (c3, 1), (x3, None), (c4, 0), (y3, None), (c4, 1)],
        with_grad=2,
        after=(part2,),
    )
    came3b, came3a = core_hop(sent3b), core_hop(sent3a)
    sum1 = add([(kept1, 0), (came1, 0), (side1, None)], after=(kept3,))
    sum2 = add([(kept2, 0), (came2, 0), (side2, None)], after=(sum1,))
    part3 = add([(kept3, 1), (came3b, None)], after=(sum2,))
    (d1,) = gate((d1,), after=(part3,))
    c5, side3 = core_hop(d1), x_hop(part3)
    home = add([(home, None), (z_hop(sum1, -1), None)], after=(d1,), dtype=jnp.float32)
    (mark,) = run([(d0, None), (c4, 2), (d1, None), (c5, None)], after=(home,))
    sum3 = add([(kept3, 0), (came3a, None), (side3, None)], after=(mark,))
    home = add([(home, None), (z_hop(sum2, -2), None)], after=(sum3,), dtype=jnp.float32)
    (d23,) = gate((d23,), after=(home,))

    c6, back3 = core_hop(d23), z_hop(sum3, -3)
    (mark,) = run([(d23, 0), (c6, 0), (d23, 1), (c6, 1)], last=True)
    grad_tokens, grad_combine = finish([(home, None), (back3, None)], ids, width, after=(mark,))
    return grad_tokens, grad_combine.T, sums[0][None], sums[1][None]


def solution(mesh):
    in_specs = (
        P(("expert", "dp"), None),
        P(("expert", "dp"), None),
        P(("expert", "dp"), None),
        P(("expert", "dp"), None),
        P("expert", None, None),
        P("expert", None, None),
    )
    out_specs = (
        P(("expert", "dp"), None),
        P(("expert", "dp"), None),
        P("expert", "dp", None),
        P("expert", "dp", None),
    )

    def run(tokens, *rest):
        small = tokens.size * 2 <= GATHER_BYTES and mesh.shape["dp"] == 2
        shards = streamed if small and mesh.shape["expert"] == 16 else grouped
        return jax.shard_map(
            shards, mesh=mesh, in_specs=in_specs, out_specs=out_specs, check_vma=False
        )(tokens, *rest)

    return run
```

```python
import functools

import jax
import jax.numpy as jnp
from jax import lax
from jax.experimental import pallas as pl
from jax.experimental.pallas import tpu as pltpu
from jax.sharding import PartitionSpec as P

LANES = 128
CORES = 2
GATHER_BYTES = 16 << 20


def weight_table(expert_ids, combine, experts):
    lanes = jnp.arange(-(-experts // LANES) * LANES, dtype=jnp.int32)
    picks = expert_ids[:, :, None] == lanes
    table = jnp.sum(jnp.where(picks, combine.astype(jnp.float32)[:, :, None], 0.0), axis=1)
    return table.astype(jnp.bfloat16), picks, lanes


def rows_pass(rows, w_in, w_out, me, lanes, with_grad):
    width, hidden = w_out.shape
    tok, cot = rows[:, :width], rows[:, width : 2 * width]
    weight = jnp.sum(
        jnp.where(lanes[None, :] == me, rows[:, 2 * width :].astype(jnp.float32), 0.0),
        axis=1,
        keepdims=True,
    )
    both = jnp.dot(tok, w_in, preferred_element_type=jnp.float32)
    gate, upper = both[:, :hidden], both[:, hidden:]
    sigma = jax.nn.sigmoid(gate)
    swish = gate * sigma
    activ = swish * upper
    cot_down = jnp.dot(cot, w_out, preferred_element_type=jnp.float32)
    grad_act = weight * cot_down
    grad_gate = grad_act * upper * sigma * (1.0 + gate * (1.0 - sigma))
    grad_both = jnp.concatenate([grad_gate, grad_act * swish], axis=1).astype(jnp.bfloat16)
    scaled = (weight * activ).astype(jnp.bfloat16)
    if not with_grad:
        return grad_both, scaled, None
    inner = jnp.sum(activ * cot_down, axis=1, keepdims=True)
    row_grad = lax.dot_general(
        grad_both, w_in, (((1,), (1,)), ((), ())), preferred_element_type=jnp.float32
    ).astype(jnp.bfloat16)
    inner_table = jnp.where(lanes[None, :] == me, inner, 0.0).astype(jnp.bfloat16)
    return grad_both, scaled, jnp.concatenate([row_grad, inner_table], axis=1)


def outer(rows, columns):
    return lax.dot_general(
        rows, columns, (((0,), (0,)), ((), ())), preferred_element_type=jnp.float32
    ).astype(jnp.bfloat16)


def pick_inner(back, picks):
    return jnp.sum(jnp.where(picks, back.astype(jnp.float32)[:, None, :], 0.0), axis=2).astype(
        jnp.bfloat16
    )


def grouped(tokens, cotangent, expert_ids, combine, gate_up, down_proj):
    width = tokens.shape[1]
    me = lax.axis_index("expert")
    table, picks, lanes = weight_table(expert_ids, combine, lax.axis_size("expert"))
    rows = lax.all_gather(
        jnp.concatenate([tokens, cotangent, table], axis=1), "expert", axis=0, tiled=True
    )
    grad_both, scaled, back = rows_pass(rows, gate_up[0], down_proj[0], me, lanes, True)
    back = lax.psum_scatter(back, "expert", scatter_dimension=0, tiled=True)

    def share(term):
        return lax.psum_scatter(term, "dp", scatter_dimension=0, tiled=True)[None]

    return (
        back[:, :width],
        pick_inner(back[:, width:], picks),
        share(outer(rows[:, :width], grad_both)),
        share(outer(rows[:, width : 2 * width], scaled)),
    )


def gate(passed, stacks=(), after=()):
    count = len(passed)
    arrays = list(passed) + list(after)
    places = [
        (g, j, next(i for i, a in enumerate(arrays) if a is member))
        for g, members in enumerate(stacks)
        for j, member in enumerate(members)
    ]

    def kernel(*refs):
        out = refs[len(arrays) + count :]
        copies = [
            pltpu.make_async_copy(refs[i], out[g].at[j], refs[-1].at[n])
            for n, (g, j, i) in enumerate(places)
        ]
        for copy in copies:
            copy.start()
        for copy in copies:
            copy.wait()

    anywhere = pl.BlockSpec(memory_space=pl.ANY)
    shapes = [jax.ShapeDtypeStruct(a.shape, a.dtype) for a in passed]
    shapes += [jax.ShapeDtypeStruct((len(g),) + g[0].shape, g[0].dtype) for g in stacks]
    return pl.pallas_call(
        kernel,
        out_shape=shapes,
        in_specs=[anywhere] * len(arrays),
        out_specs=[anywhere] * count + [pl.BlockSpec(memory_space=pltpu.VMEM)] * len(stacks),
        scratch_shapes=[pltpu.SemaphoreType.DMA((max(1, len(places)),))],
        input_output_aliases={i: i for i in range(count)},
        compiler_params=pltpu.CompilerParams(vmem_limit_bytes=4 << 20),
    )(*arrays)


def add(terms, after=(), dtype=jnp.bfloat16):
    arrays, picks = zip(*terms)
    anywhere = pl.BlockSpec(memory_space=pl.ANY)
    near = pl.BlockSpec(memory_space=pltpu.VMEM)

    def kernel(*refs):
        parts = [ref if k is None else ref.at[k] for ref, k in zip(refs, picks)]
        total = parts[0][...].astype(jnp.float32)
        for part in parts[1:]:
            total += part[...].astype(jnp.float32)
        refs[-1][...] = total.astype(dtype)

    return pl.pallas_call(
        kernel,
        out_shape=jax.ShapeDtypeStruct(arrays[0].shape[-2:], dtype),
        in_specs=[near] * len(arrays) + [anywhere] * len(after),
        compiler_params=pltpu.CompilerParams(vmem_limit_bytes=6 << 20),
    )(*arrays, *after)


def finish(terms, ids, width, after):
    arrays, picks = zip(*terms)
    top, tok_rows = ids.shape
    anywhere = pl.BlockSpec(memory_space=pl.ANY)
    near = pl.BlockSpec(memory_space=pltpu.VMEM)

    def kernel(ids, *refs):
        parts = [ref if k is None else ref.at[k] for ref, k in zip(refs, picks)]
        out, chosen, rows = refs[-3:]
        total = parts[0][...].astype(jnp.float32)
        for part in parts[1:]:
            total += part[...].astype(jnp.float32)
        out[...] = total[:, :width].astype(jnp.bfloat16)
        table = total[:, width:].T
        line = lax.broadcasted_iota(jnp.int32, table.shape, 0)
        for k in range(top):
            picked = jnp.where(line == ids[k : k + 1, :], table, 0.0)
            rows[k : k + 1, :] = jnp.sum(picked, axis=0, keepdims=True)
        chosen[...] = rows[...].astype(jnp.bfloat16)

    return pl.pallas_call(
        kernel,
        out_shape=[
            jax.ShapeDtypeStruct((tok_rows, width), jnp.bfloat16),
            jax.ShapeDtypeStruct((top, tok_rows), jnp.bfloat16),
        ],
        scratch_shapes=[pltpu.VMEM((top, tok_rows), jnp.float32)],
        in_specs=[near] * (1 + len(arrays)) + [anywhere] * len(after),
        compiler_params=pltpu.CompilerParams(vmem_limit_bytes=6 << 20),
    )(ids, *arrays, *after)


def first_rows(tokens, cotangent, ids, combine, experts):
    top, tok_rows = ids.shape
    width = tokens.shape[1]
    extra = -(-experts // LANES) * LANES

    def kernel(tok, cot, ids, combine, out):
        out[:, :width] = tok[...]
        out[:, width : 2 * width] = cot[...]
        line = lax.broadcasted_iota(jnp.int32, (extra, tok_rows), 0)
        share = combine[...].astype(jnp.float32)
        table = jnp.zeros((extra, tok_rows), jnp.float32)
        for k in range(top):
            table += jnp.where(line == ids[k : k + 1, :], share[k : k + 1, :], 0.0)
        out[:, 2 * width :] = table.T.astype(jnp.bfloat16)

    return pl.pallas_call(
        kernel,
        out_shape=jax.ShapeDtypeStruct((tok_rows, 2 * width + extra), jnp.bfloat16),
        compiler_params=pltpu.CompilerParams(vmem_limit_bytes=4 << 20),
    )(tokens, cotangent, ids, combine)


def keep_near(*arrays):
    def kernel(*refs):
        count = len(arrays)
        copies = [
            pltpu.make_async_copy(refs[i], refs[count + i], refs[-1].at[i]) for i in range(count)
        ]
        for copy in copies:
            copy.start()
        for copy in copies:
            copy.wait()

    return pl.pallas_call(
        kernel,
        out_shape=[pltpu.VMEM(a.shape, a.dtype) for a in arrays],
        in_specs=[pl.BlockSpec(memory_space=pltpu.HBM)] * len(arrays),
        out_specs=[pl.BlockSpec(memory_space=pltpu.VMEM)] * len(arrays),
        scratch_shapes=[pltpu.SemaphoreType.DMA((len(arrays),))],
        compiler_params=pltpu.CompilerParams(vmem_limit_bytes=44 << 20),
    )(*arrays)


def slot_kernel(picks, waits, with_grad, first, last, *refs):
    count = len(picks)
    units = [ref if k is None else ref.at[k] for ref, k in zip(refs[:count], picks)]
    win, wout = refs[count : count + 2]
    refs = refs[count + 2 :]
    if not first:
        old_up, old_down = refs[:2]
        refs = refs[2:]
    refs = refs[waits:]
    new_up, new_down = refs[:2]
    refs = refs[2:]
    if with_grad:
        kept, sent = refs[0], refs[1 : 1 + with_grad]
        sent = [sent[0].at[0], sent[0].at[1]] if with_grad == 1 else sent
        refs = refs[1 + with_grad :]
    else:
        refs[0][...] = jnp.zeros_like(refs[0])
        refs = refs[1:]
    tok, cot, both, scaled, tok_t, cot_t, sems = refs[:7]
    refs = refs[7:]
    if last:
        done_up, done_down = refs[:2]

    width, hidden = wout.shape
    tok_rows, wide = units[0].shape
    rows = count * tok_rows
    back_rows = 4 * tok_rows
    spare = tok.shape[0] - rows
    part = tok_t.shape[0]
    me, mine = lax.axis_index("expert"), lax.axis_index("dp")
    for padded in (tok, cot, both, scaled) if spare else ():
        padded[pl.ds(rows, spare), :] = jnp.zeros((spare, padded.shape[1]), jnp.bfloat16)

    weights = []
    for i in range(0, count, 2):
        span = pl.ds(i * tok_rows, 2 * tok_rows)
        for target, start in ((tok, 0), (cot, width)):
            joined = [units[j][:, pl.ds(start, width)].astype(jnp.float32) for j in (i, i + 1)]
            target[span, :] = jnp.concatenate(joined, axis=0).astype(jnp.bfloat16)
        for j in (i, i + 1):
            table = units[j][:, pl.ds(2 * width, wide - 2 * width)].astype(jnp.float32)
            lane = lax.broadcasted_iota(jnp.int32, table.shape, 1)
            weights.append(jnp.sum(jnp.where(lane == me, table, 0.0), axis=1, keepdims=True))
    weight = jnp.concatenate(weights, axis=0)

    real = pl.ds(0, rows)
    step = 256 if hidden % 256 == 0 else hidden
    inner = jnp.zeros((back_rows, 1), jnp.float32)
    for j in range(hidden // step):
        gates, uppers = pl.ds(j * step, step), pl.ds(hidden + j * step, step)
        gate_x = jnp.dot(tok[real, :], win[:, gates], preferred_element_type=jnp.float32)
        upper = jnp.dot(tok[real, :], win[:, uppers], preferred_element_type=jnp.float32)
        cot_down = jnp.dot(cot[real, :], wout[:, gates], preferred_element_type=jnp.float32)
        sigma = 1.0 / (1.0 + jnp.exp(-gate_x))
        swish = gate_x * sigma
        activ = swish * upper
        grad_act = weight * cot_down
        both[real, gates] = (grad_act * upper * sigma * (1.0 + gate_x * (1.0 - sigma))).astype(
            jnp.bfloat16
        )
        both[real, uppers] = (grad_act * swish).astype(jnp.bfloat16)
        scaled[real, gates] = (weight * activ).astype(jnp.bfloat16)
        if with_grad:
            inner += jnp.sum((activ * cot_down)[:back_rows], axis=1, keepdims=True)

    leave = []
    if with_grad:

        def back(columns, value):
            for i in range(4):
                target = sent[i // 2] if i % 2 else kept.at[i // 2]
                target[:, columns] = value[i * tok_rows : (i + 1) * tok_rows].astype(jnp.bfloat16)

        for start in range(0, width, 512):
            span = pl.ds(start, min(512, width - start))
            term = lax.dot_general(
                both[pl.ds(0, back_rows), :],
                win[span, :],
                (((1,), (1,)), ((), ())),
                preferred_element_type=jnp.float32,
            )
            back(span, term)
        lane = lax.broadcasted_iota(jnp.int32, (back_rows, wide - 2 * width), 1)
        back(pl.ds(width, wide - 2 * width), jnp.where(lane == me, inner, 0.0))

    columns = pl.ds(pl.multiple_of(mine * part, part), part)
    tok_t[...] = tok[:, columns].T
    cot_t[...] = cot[:, columns].T
    sides = [
        (tok_t, both, None if first else old_up, new_up, done_up if last else None),
        (cot_t, scaled, None if first else old_down, new_down, done_down if last else None),
    ]
    place = 0
    for left, right, old, new, done in sides:
        for start in range(0, right.shape[1], step):
            span = pl.ds(start, step)
            term = jnp.dot(left[...], right[:, span], preferred_element_type=jnp.float32)
            if not first:
                term += old[:, span]
            if not last:
                new[:, span] = term
                continue
            done[:, span] = term.astype(jnp.bfloat16)
            leave.append(
                pltpu.make_async_copy(done.at[:, span], new.at[:, span], sems.at[place])
            )
            leave[-1].start()
            place += 1
    for copy in leave:
        copy.wait()


def slot_pass(units, win, wout, sums, with_grad, last, after):
    width, hidden = wout.shape
    arrays, picks = zip(*units)
    tok_rows, wide = arrays[0].shape[-2:]
    rows = len(units) * tok_rows
    padded = -(-rows // LANES) * LANES
    part = width // 2
    first = sums is None
    near, far = pl.BlockSpec(memory_space=pltpu.VMEM), pl.BlockSpec(memory_space=pltpu.HBM)
    grads = [(part, 2 * hidden), (part, hidden)]
    if last:
        shapes, specs = [pltpu.HBM(g, jnp.bfloat16) for g in grads], [far, far]
    else:
        shapes, specs = [pltpu.VMEM(g, jnp.float32) for g in grads], [near, near]
    back = (2, tok_rows, wide - width)
    scratch = [
        pltpu.VMEM((padded, width), jnp.bfloat16),
        pltpu.VMEM((padded, width), jnp.bfloat16),
        pltpu.VMEM((padded, 2 * hidden), jnp.bfloat16),
        pltpu.VMEM((padded, hidden), jnp.bfloat16),
        pltpu.VMEM((part, padded), jnp.bfloat16),
        pltpu.VMEM((part, padded), jnp.bfloat16),
        pltpu.SemaphoreType.DMA((3 * hidden // (256 if hidden % 256 == 0 else hidden),)),
    ]
    if with_grad:
        shapes.append(pltpu.VMEM(back, jnp.bfloat16))
        shapes += [pltpu.VMEM(back[with_grad - 1 :], jnp.bfloat16)] * with_grad
        specs += [near] * (1 + with_grad)
    else:
        shapes.append(pltpu.VMEM((8, LANES), jnp.float32))
        specs.append(near)
    if last:
        scratch += [pltpu.VMEM(g, jnp.bfloat16) for g in grads]
    out = pl.pallas_call(
        functools.partial(slot_kernel, picks, len(after), with_grad, first, last),
        out_shape=shapes,
        in_specs=[near] * (len(units) + (2 if first else 4))
        + [pl.BlockSpec(memory_space=pl.ANY)] * len(after),
        out_specs=specs,
        scratch_shapes=scratch,
        input_output_aliases={} if first or last else {len(units) + 2: 0, len(units) + 3: 1},
        compiler_params=pltpu.CompilerParams(vmem_limit_bytes=(18 if last else 14) << 20),
        cost_estimate=pl.CostEstimate(flops=0, bytes_accessed=0, transcendentals=0),
    )(*arrays, win, wout, *(sums or ()), *after)
    return out[:2], out[2:]


def streamed(tokens, cotangent, expert_ids, combine, gate_up, down_proj):
    width = tokens.shape[1]
    experts = lax.axis_size("expert")
    ids = expert_ids.T

    n_x, n_z = 2, experts // CORES // 2

    def place(z, x, core):
        return (z * n_x + x) * CORES + core

    spots = [(z, x, c) for z in range(n_z) for x in range(n_x) for c in range(CORES)]
    ring = [0] + list(range(1, n_z, 2)) + list(range(2, n_z, 2))[::-1]
    by_z = [
        [
            (place(ring[i], x, c), place(ring[(i + far) % n_z], x, c))
            for i in range(n_z)
            for x in range(n_x)
            for c in range(CORES)
        ]
        for far in range(n_z)
    ]
    over_x = [(place(z, x, c), place(z, 1 - x, c)) for z, x, c in spots]
    over_core = [(place(z, x, c), place(z, x, 1 - c)) for z, x, c in spots]

    def z_hop(a, far=1):
        return lax.ppermute(a, "expert", by_z[far % n_z])

    def x_hop(a):
        return lax.ppermute(a, "expert", over_x)

    def core_hop(a):
        return lax.ppermute(a, "expert", over_core)

    def y_hop(a):
        return lax.ppermute(a, "dp", [(0, 1), (1, 0)])

    sums = None
    win, wout = keep_near(gate_up[0], down_proj[0])

    def run(units, with_grad=False, last=False, after=()):
        nonlocal sums
        sums, rest = slot_pass(units, win, wout, sums, with_grad, last, after)
        return rest

    z0 = first_rows(tokens, cotangent, ids, combine.T, experts)
    z1, x0, y0, z0c = z_hop(z0), x_hop(z0), y_hop(z0), core_hop(z0)
    z1, x0, y0, z0c, pile = gate((z1, x0, y0, z0c), stacks=((x0, z1, y0),), after=(win, wout))

    c1, z2, x1, y1 = core_hop(pile), z_hop(z1), x_hop(z1), y_hop(z1)
    kept0, sent0 = run(
        [(z0, None), (z0c, None), (x0, None), (c1, 0), (y0, None), (c1, 2)], with_grad=1
    )
    z2, x1, y1, sent0, pile = gate((z2, x1, y1, sent0), stacks=((x1, z2, y1),))

    c2, z3, x2, y2, came0 = core_hop(pile), z_hop(z2), x_hop(z2), y_hop(z2), core_hop(sent0)
    kept1, sent1 = run(
        [(z1, None), (c1, 1), (x1, None), (c2, 0), (y1, None), (c2, 2)], with_grad=1
    )
    part0 = add([(kept0, 1), (came0, 1)], after=(kept1,))
    z3, x2, y2, sent1, pile = gate((z3, x2, y2, sent1), stacks=((x2, z3, y2),), after=(part0,))

    c3, x3, d0, y3, came1 = core_hop(pile), z_hop(x2), x_hop(y0), y_hop(z3), core_hop(sent1)
    part1 = add([(kept1, 1), (came1, 1)], after=(pile,))
    kept2, sent2 = run(
        [(z2, None), (c2, 1), (x2, None), (c3, 0), (y2, None), (c3, 2)],
        with_grad=1,
        after=(part1,),
    )
    x3, d0, y3, sent2, part0, part1, pile, pair = gate(
        (x3, d0, y3, sent2, part0, part1), stacks=((x3, y3, d0), (x2, x3)), after=(kept2, x2)
    )

    c4, d1, d23, came2 = core_hop(pile), z_hop(d0), y_hop(pair), core_hop(sent2)
    side1 = x_hop(part1)
    part2 = add([(kept2, 1), (came2, 1)], after=(pile,))
    side2 = x_hop(part2)
    kept3, sent3a, sent3b = run(
        [(z3, None), (c3, 1), (x3, None), (c4, 0), (y3, None), (c4, 1)],
        with_grad=2,
        after=(part2,),
    )
    came3b, came3a = core_hop(sent3b), core_hop(sent3a)
    sum1 = add([(kept1, 0), (came1, 0), (side1, None)], after=(kept3,), dtype=jnp.float32)
    sum2 = add([(kept2, 0), (came2, 0), (side2, None)], after=(sum1,))
    part3 = add([(kept3, 1), (came3b, None)], after=(sum2,))
    (d1,) = gate((d1,), after=(part3,))
    c5, side3 = core_hop(d1), x_hop(part3)
    (mark,) = run([(d0, None), (c4, 2), (d1, None), (c5, None)], after=(d1,))
    sum3 = add([(kept3, 0), (came3a, None), (side3, None)], after=(mark,))
    sum1 = add([(sum1, None), (z_hop(sum2, -1), None)], after=(sum3,))
    (d23,) = gate((d23,), after=(sum1,))

    c6, back1, back3, side0 = core_hop(d23), z_hop(sum1, -1), z_hop(sum3, -3), x_hop(part0)
    (mark,) = run([(d23, 0), (c6, 0), (d23, 1), (c6, 1)], last=True)
    grad_tokens, grad_combine = finish(
        [(kept0, 0), (came0, 0)] + [(a, None) for a in (side0, back1, back3)],
        ids,
        width,
        after=(mark,),
    )
    return grad_tokens, grad_combine.T, sums[0][None], sums[1][None]


def solution(mesh):
    in_specs = (
        P(("expert", "dp"), None),
        P(("expert", "dp"), None),
        P(("expert", "dp"), None),
        P(("expert", "dp"), None),
        P("expert", None, None),
        P("expert", None, None),
    )
    out_specs = (
        P(("expert", "dp"), None),
        P(("expert", "dp"), None),
        P("expert", "dp", None),
        P("expert", "dp", None),
    )

    def run(tokens, *rest):
        small = tokens.size * 2 <= GATHER_BYTES and mesh.shape["dp"] == 2
        shards = streamed if small and mesh.shape["expert"] == 16 else grouped
        return jax.shard_map(
            shards, mesh=mesh, in_specs=in_specs, out_specs=out_specs, check_vma=False
        )(tokens, *rest)

    return run
```

```python
import functools

import jax
import jax.numpy as jnp
from jax import lax
from jax.experimental import pallas as pl
from jax.experimental.pallas import tpu as pltpu
from jax.sharding import PartitionSpec as P

LANES = 128
CORES = 2
GATHER_BYTES = 16 << 20


def weight_table(expert_ids, combine, experts):
    lanes = jnp.arange(-(-experts // LANES) * LANES, dtype=jnp.int32)
    picks = expert_ids[:, :, None] == lanes
    table = jnp.sum(jnp.where(picks, combine.astype(jnp.float32)[:, :, None], 0.0), axis=1)
    return table.astype(jnp.bfloat16), picks, lanes


def rows_pass(rows, w_in, w_out, me, lanes, with_grad):
    width, hidden = w_out.shape
    tok, cot = rows[:, :width], rows[:, width : 2 * width]
    weight = jnp.sum(
        jnp.where(lanes[None, :] == me, rows[:, 2 * width :].astype(jnp.float32), 0.0),
        axis=1,
        keepdims=True,
    )
    both = jnp.dot(tok, w_in, preferred_element_type=jnp.float32)
    gate, upper = both[:, :hidden], both[:, hidden:]
    sigma = jax.nn.sigmoid(gate)
    swish = gate * sigma
    activ = swish * upper
    cot_down = jnp.dot(cot, w_out, preferred_element_type=jnp.float32)
    grad_act = weight * cot_down
    grad_gate = grad_act * upper * sigma * (1.0 + gate * (1.0 - sigma))
    grad_both = jnp.concatenate([grad_gate, grad_act * swish], axis=1).astype(jnp.bfloat16)
    scaled = (weight * activ).astype(jnp.bfloat16)
    if not with_grad:
        return grad_both, scaled, None
    inner = jnp.sum(activ * cot_down, axis=1, keepdims=True)
    row_grad = lax.dot_general(
        grad_both, w_in, (((1,), (1,)), ((), ())), preferred_element_type=jnp.float32
    ).astype(jnp.bfloat16)
    inner_table = jnp.where(lanes[None, :] == me, inner, 0.0).astype(jnp.bfloat16)
    return grad_both, scaled, jnp.concatenate([row_grad, inner_table], axis=1)


def outer(rows, columns):
    return lax.dot_general(
        rows, columns, (((0,), (0,)), ((), ())), preferred_element_type=jnp.float32
    ).astype(jnp.bfloat16)


def pick_inner(back, picks):
    return jnp.sum(jnp.where(picks, back.astype(jnp.float32)[:, None, :], 0.0), axis=2).astype(
        jnp.bfloat16
    )


def grouped(tokens, cotangent, expert_ids, combine, gate_up, down_proj):
    width = tokens.shape[1]
    me = lax.axis_index("expert")
    table, picks, lanes = weight_table(expert_ids, combine, lax.axis_size("expert"))
    rows = lax.all_gather(
        jnp.concatenate([tokens, cotangent, table], axis=1), "expert", axis=0, tiled=True
    )
    grad_both, scaled, back = rows_pass(rows, gate_up[0], down_proj[0], me, lanes, True)
    back = lax.psum_scatter(back, "expert", scatter_dimension=0, tiled=True)

    def share(term):
        return lax.psum_scatter(term, "dp", scatter_dimension=0, tiled=True)[None]

    return (
        back[:, :width],
        pick_inner(back[:, width:], picks),
        share(outer(rows[:, :width], grad_both)),
        share(outer(rows[:, width : 2 * width], scaled)),
    )


def gate(passed, stacks=(), after=()):
    count = len(passed)
    arrays = list(passed) + list(after)
    places = [
        (g, j, next(i for i, a in enumerate(arrays) if a is member))
        for g, members in enumerate(stacks)
        for j, member in enumerate(members)
    ]

    def kernel(*refs):
        out = refs[len(arrays) + count :]
        copies = [
            pltpu.make_async_copy(refs[i], out[g].at[j], refs[-1].at[n])
            for n, (g, j, i) in enumerate(places)
        ]
        for copy in copies:
            copy.start()
        for copy in copies:
            copy.wait()

    anywhere = pl.BlockSpec(memory_space=pl.ANY)
    shapes = [jax.ShapeDtypeStruct(a.shape, a.dtype) for a in passed]
    shapes += [jax.ShapeDtypeStruct((len(g),) + g[0].shape, g[0].dtype) for g in stacks]
    return pl.pallas_call(
        kernel,
        out_shape=shapes,
        in_specs=[anywhere] * len(arrays),
        out_specs=[anywhere] * count + [pl.BlockSpec(memory_space=pltpu.VMEM)] * len(stacks),
        scratch_shapes=[pltpu.SemaphoreType.DMA((max(1, len(places)),))],
        input_output_aliases={i: i for i in range(count)},
        compiler_params=pltpu.CompilerParams(vmem_limit_bytes=4 << 20),
    )(*arrays)


def add(terms, after=(), dtype=jnp.bfloat16):
    arrays, picks = zip(*terms)
    anywhere = pl.BlockSpec(memory_space=pl.ANY)
    near = pl.BlockSpec(memory_space=pltpu.VMEM)

    def kernel(*refs):
        parts = [ref if k is None else ref.at[k] for ref, k in zip(refs, picks)]
        total = parts[0][...].astype(jnp.float32)
        for part in parts[1:]:
            total += part[...].astype(jnp.float32)
        refs[-1][...] = total.astype(dtype)

    return pl.pallas_call(
        kernel,
        out_shape=jax.ShapeDtypeStruct(arrays[0].shape[-2:], dtype),
        in_specs=[near] * len(arrays) + [anywhere] * len(after),
        compiler_params=pltpu.CompilerParams(vmem_limit_bytes=6 << 20),
    )(*arrays, *after)


def finish(terms, ids, width, after):
    arrays, picks = zip(*terms)
    top, tok_rows = ids.shape
    anywhere = pl.BlockSpec(memory_space=pl.ANY)
    near = pl.BlockSpec(memory_space=pltpu.VMEM)

    def kernel(ids, *refs):
        parts = [ref if k is None else ref.at[k] for ref, k in zip(refs, picks)]
        out, chosen, rows = refs[-3:]
        total = parts[0][...].astype(jnp.float32)
        for part in parts[1:]:
            total += part[...].astype(jnp.float32)
        out[...] = total[:, :width].astype(jnp.bfloat16)
        table = total[:, width:].T
        line = lax.broadcasted_iota(jnp.int32, table.shape, 0)
        for k in range(top):
            picked = jnp.where(line == ids[k : k + 1, :], table, 0.0)
            rows[k : k + 1, :] = jnp.sum(picked, axis=0, keepdims=True)
        chosen[...] = rows[...].astype(jnp.bfloat16)

    return pl.pallas_call(
        kernel,
        out_shape=[
            jax.ShapeDtypeStruct((tok_rows, width), jnp.bfloat16),
            jax.ShapeDtypeStruct((top, tok_rows), jnp.bfloat16),
        ],
        scratch_shapes=[pltpu.VMEM((top, tok_rows), jnp.float32)],
        in_specs=[near] * (1 + len(arrays)) + [anywhere] * len(after),
        compiler_params=pltpu.CompilerParams(vmem_limit_bytes=6 << 20),
    )(ids, *arrays, *after)


def first_rows(tokens, cotangent, ids, combine, experts):
    top, tok_rows = ids.shape
    width = tokens.shape[1]
    extra = -(-experts // LANES) * LANES

    def kernel(tok, cot, ids, combine, out):
        out[:, :width] = tok[...]
        out[:, width : 2 * width] = cot[...]
        line = lax.broadcasted_iota(jnp.int32, (extra, tok_rows), 0)
        share = combine[...].astype(jnp.float32)
        table = jnp.zeros((extra, tok_rows), jnp.float32)
        for k in range(top):
            table += jnp.where(line == ids[k : k + 1, :], share[k : k + 1, :], 0.0)
        out[:, 2 * width :] = table.T.astype(jnp.bfloat16)

    return pl.pallas_call(
        kernel,
        out_shape=jax.ShapeDtypeStruct((tok_rows, 2 * width + extra), jnp.bfloat16),
        compiler_params=pltpu.CompilerParams(vmem_limit_bytes=4 << 20),
    )(tokens, cotangent, ids, combine)


def keep_near(*arrays):
    def kernel(*refs):
        count = len(arrays)
        copies = [
            pltpu.make_async_copy(refs[i], refs[count + i], refs[-1].at[i]) for i in range(count)
        ]
        for copy in copies:
            copy.start()
        for copy in copies:
            copy.wait()

    return pl.pallas_call(
        kernel,
        out_shape=[pltpu.VMEM(a.shape, a.dtype) for a in arrays],
        in_specs=[pl.BlockSpec(memory_space=pltpu.HBM)] * len(arrays),
        out_specs=[pl.BlockSpec(memory_space=pltpu.VMEM)] * len(arrays),
        scratch_shapes=[pltpu.SemaphoreType.DMA((len(arrays),))],
        compiler_params=pltpu.CompilerParams(vmem_limit_bytes=44 << 20),
    )(*arrays)


def slot_kernel(picks, waits, with_grad, first, last, *refs):
    count = len(picks)
    units = [ref if k is None else ref.at[k] for ref, k in zip(refs[:count], picks)]
    win, wout = refs[count : count + 2]
    refs = refs[count + 2 :]
    if not first:
        old_up, old_down = refs[:2]
        refs = refs[2:]
    refs = refs[waits:]
    new_up, new_down = refs[:2]
    refs = refs[2:]
    if with_grad:
        kept, sent = refs[0], refs[1 : 1 + with_grad]
        sent = [sent[0].at[0], sent[0].at[1]] if with_grad == 1 else sent
        refs = refs[1 + with_grad :]
    else:
        refs[0][...] = jnp.zeros_like(refs[0])
        refs = refs[1:]
    tok, cot, both, scaled, tok_t, cot_t, sems = refs[:7]
    refs = refs[7:]
    if last:
        done_up, done_down = refs[:2]

    width, hidden = wout.shape
    tok_rows, wide = units[0].shape
    rows = count * tok_rows
    back_rows = 4 * tok_rows
    spare = tok.shape[0] - rows
    part = tok_t.shape[0]
    me, mine = lax.axis_index("expert"), lax.axis_index("dp")
    for padded in (tok, cot, both, scaled) if spare else ():
        padded[pl.ds(rows, spare), :] = jnp.zeros((spare, padded.shape[1]), jnp.bfloat16)

    weights = []
    for i in range(0, count, 2):
        span = pl.ds(i * tok_rows, 2 * tok_rows)
        for target, start in ((tok, 0), (cot, width)):
            joined = [units[j][:, pl.ds(start, width)].astype(jnp.float32) for j in (i, i + 1)]
            target[span, :] = jnp.concatenate(joined, axis=0).astype(jnp.bfloat16)
        for j in (i, i + 1):
            table = units[j][:, pl.ds(2 * width, wide - 2 * width)].astype(jnp.float32)
            lane = lax.broadcasted_iota(jnp.int32, table.shape, 1)
            weights.append(jnp.sum(jnp.where(lane == me, table, 0.0), axis=1, keepdims=True))
    weight = jnp.concatenate(weights, axis=0)

    real = pl.ds(0, rows)
    step = 256 if hidden % 256 == 0 else hidden
    inner = jnp.zeros((back_rows, 1), jnp.float32)
    for j in range(hidden // step):
        gates, uppers = pl.ds(j * step, step), pl.ds(hidden + j * step, step)
        gate_x = jnp.dot(tok[real, :], win[:, gates], preferred_element_type=jnp.float32)
        upper = jnp.dot(tok[real, :], win[:, uppers], preferred_element_type=jnp.float32)
        cot_down = jnp.dot(cot[real, :], wout[:, gates], preferred_element_type=jnp.float32)
        sigma = 1.0 / (1.0 + jnp.exp(-gate_x))
        swish = gate_x * sigma
        activ = swish * upper
        grad_act = weight * cot_down
        both[real, gates] = (grad_act * upper * sigma * (1.0 + gate_x * (1.0 - sigma))).astype(
            jnp.bfloat16
        )
        both[real, uppers] = (grad_act * swish).astype(jnp.bfloat16)
        scaled[real, gates] = (weight * activ).astype(jnp.bfloat16)
        if with_grad:
            inner += jnp.sum((activ * cot_down)[:back_rows], axis=1, keepdims=True)

    leave = []
    if with_grad:

        def back(columns, value):
            for i in range(4):
                target = sent[i // 2] if i % 2 else kept.at[i // 2]
                target[:, columns] = value[i * tok_rows : (i + 1) * tok_rows].astype(jnp.bfloat16)

        for start in range(0, width, 512):
            span = pl.ds(start, min(512, width - start))
            term = lax.dot_general(
                both[pl.ds(0, back_rows), :],
                win[span, :],
                (((1,), (1,)), ((), ())),
                preferred_element_type=jnp.float32,
            )
            back(span, term)
        lane = lax.broadcasted_iota(jnp.int32, (back_rows, wide - 2 * width), 1)
        back(pl.ds(width, wide - 2 * width), jnp.where(lane == me, inner, 0.0))

    columns = pl.ds(pl.multiple_of(mine * part, part), part)
    tok_t[...] = tok[:, columns].T
    cot_t[...] = cot[:, columns].T
    sides = [
        (tok_t, both, None if first else old_up, new_up, done_up if last else None),
        (cot_t, scaled, None if first else old_down, new_down, done_down if last else None),
    ]
    place = 0
    for left, right, old, new, done in sides:
        for start in range(0, right.shape[1], step):
            span = pl.ds(start, step)
            term = jnp.dot(left[...], right[:, span], preferred_element_type=jnp.float32)
            if not first:
                term += old[:, span]
            if not last:
                new[:, span] = term
                continue
            done[:, span] = term.astype(jnp.bfloat16)
            leave.append(
                pltpu.make_async_copy(done.at[:, span], new.at[:, span], sems.at[place])
            )
            leave[-1].start()
            place += 1
    for copy in leave:
        copy.wait()


def slot_pass(units, win, wout, sums, with_grad, last, after):
    width, hidden = wout.shape
    arrays, picks = zip(*units)
    tok_rows, wide = arrays[0].shape[-2:]
    rows = len(units) * tok_rows
    padded = -(-rows // LANES) * LANES
    part = width // 2
    first = sums is None
    near, far = pl.BlockSpec(memory_space=pltpu.VMEM), pl.BlockSpec(memory_space=pltpu.HBM)
    grads = [(part, 2 * hidden), (part, hidden)]
    if last:
        shapes, specs = [pltpu.HBM(g, jnp.bfloat16) for g in grads], [far, far]
    else:
        shapes, specs = [pltpu.VMEM(g, jnp.float32) for g in grads], [near, near]
    back = (2, tok_rows, wide - width)
    scratch = [
        pltpu.VMEM((padded, width), jnp.bfloat16),
        pltpu.VMEM((padded, width), jnp.bfloat16),
        pltpu.VMEM((padded, 2 * hidden), jnp.bfloat16),
        pltpu.VMEM((padded, hidden), jnp.bfloat16),
        pltpu.VMEM((part, padded), jnp.bfloat16),
        pltpu.VMEM((part, padded), jnp.bfloat16),
        pltpu.SemaphoreType.DMA((3 * hidden // (256 if hidden % 256 == 0 else hidden),)),
    ]
    if with_grad:
        shapes.append(pltpu.VMEM(back, jnp.bfloat16))
        shapes += [pltpu.VMEM(back[with_grad - 1 :], jnp.bfloat16)] * with_grad
        specs += [near] * (1 + with_grad)
    else:
        shapes.append(pltpu.VMEM((8, LANES), jnp.float32))
        specs.append(near)
    if last:
        scratch += [pltpu.VMEM(g, jnp.bfloat16) for g in grads]
    out = pl.pallas_call(
        functools.partial(slot_kernel, picks, len(after), with_grad, first, last),
        out_shape=shapes,
        in_specs=[near] * (len(units) + (2 if first else 4))
        + [pl.BlockSpec(memory_space=pl.ANY)] * len(after),
        out_specs=specs,
        scratch_shapes=scratch,
        input_output_aliases={} if first or last else {len(units) + 2: 0, len(units) + 3: 1},
        compiler_params=pltpu.CompilerParams(vmem_limit_bytes=(18 if last else 14) << 20),
        cost_estimate=pl.CostEstimate(flops=0, bytes_accessed=0, transcendentals=0),
    )(*arrays, win, wout, *(sums or ()), *after)
    return out[:2], out[2:]


def streamed(tokens, cotangent, expert_ids, combine, gate_up, down_proj):
    width = tokens.shape[1]
    experts = lax.axis_size("expert")
    ids = expert_ids.T

    n_x, n_z = 2, experts // CORES // 2

    def place(z, x, core):
        return (z * n_x + x) * CORES + core

    spots = [(z, x, c) for z in range(n_z) for x in range(n_x) for c in range(CORES)]
    ring = [0] + list(range(1, n_z, 2)) + list(range(2, n_z, 2))[::-1]
    by_z = [
        [
            (place(ring[i], x, c), place(ring[(i + far) % n_z], x, c))
            for i in range(n_z)
            for x in range(n_x)
            for c in range(CORES)
        ]
        for far in range(n_z)
    ]
    over_x = [(place(z, x, c), place(z, 1 - x, c)) for z, x, c in spots]
    over_core = [(place(z, x, c), place(z, x, 1 - c)) for z, x, c in spots]

    def z_hop(a, far=1):
        return lax.ppermute(a, "expert", by_z[far % n_z])

    def x_hop(a):
        return lax.ppermute(a, "expert", over_x)

    def core_hop(a):
        return lax.ppermute(a, "expert", over_core)

    def y_hop(a):
        return lax.ppermute(a, "dp", [(0, 1), (1, 0)])

    sums = None
    win, wout = keep_near(gate_up[0], down_proj[0])

    def run(units, with_grad=False, last=False, after=()):
        nonlocal sums
        sums, rest = slot_pass(units, win, wout, sums, with_grad, last, after)
        return rest

    z0 = first_rows(tokens, cotangent, ids, combine.T, experts)
    z1, x0, y0, z0c = z_hop(z0), x_hop(z0), y_hop(z0), core_hop(z0)
    z1, x0, y0, z0c, pile = gate((z1, x0, y0, z0c), stacks=((x0, z1, y0),), after=(win, wout))

    c1, z2, x1, y1 = core_hop(pile), z_hop(z1), x_hop(z1), y_hop(z1)
    kept0, sent0 = run(
        [(z0, None), (z0c, None), (x0, None), (c1, 0), (y0, None), (c1, 2)], with_grad=1
    )
    z2, x1, y1, sent0, pile = gate((z2, x1, y1, sent0), stacks=((x1, z2, y1),))

    c2, z3, x2, y2, came0 = core_hop(pile), z_hop(z2), x_hop(z2), y_hop(z2), core_hop(sent0)
    kept1, sent1 = run(
        [(z1, None), (c1, 1), (x1, None), (c2, 0), (y1, None), (c2, 2)], with_grad=1
    )
    part0 = add([(kept0, 1), (came0, 1)], after=(kept1,))
    z3, x2, y2, sent1, pile = gate((z3, x2, y2, sent1), stacks=((x2, z3, y2),), after=(part0,))

    c3, x3, d0, y3, came1 = core_hop(pile), z_hop(x2), x_hop(y0), y_hop(z3), core_hop(sent1)
    part1 = add([(kept1, 1), (came1, 1)], after=(pile,))
    kept2, sent2 = run(
        [(z2, None), (c2, 1), (x2, None), (c3, 0), (y2, None), (c3, 2)],
        with_grad=1,
        after=(part1,),
    )
    x3, d0, y3, sent2, part0, part1, pile, pair = gate(
        (x3, d0, y3, sent2, part0, part1), stacks=((x3, y3, d0), (x2, x3)), after=(kept2, x2)
    )

    c4, d1, d23, came2 = core_hop(pile), z_hop(d0), y_hop(pair), core_hop(sent2)
    side1 = x_hop(part1)
    part2 = add([(kept2, 1), (came2, 1)], after=(pile,))
    side2 = x_hop(part2)
    kept3, sent3a, sent3b = run(
        [(z3, None), (c3, 1), (x3, None), (c4, 0)], with_grad=2, after=(part2,)
    )
    came3b, came3a = core_hop(sent3b), core_hop(sent3a)
    sum1 = add([(kept1, 0), (came1, 0), (side1, None)], after=(kept3,), dtype=jnp.float32)
    sum2 = add([(kept2, 0), (came2, 0), (side2, None)], after=(sum1,))
    part3 = add([(kept3, 1), (came3b, None)], after=(sum2,))
    (d1,) = gate((d1,), after=(part3,))
    c5, side3 = core_hop(d1), x_hop(part3)
    (mark,) = run([(d0, None), (c4, 2), (d1, None), (c5, None)], after=(d1,))
    sum3 = add([(kept3, 0), (came3a, None), (side3, None)], after=(mark,))
    sum1 = add([(sum1, None), (z_hop(sum2, -1), None)], after=(sum3,))
    (d23,) = gate((d23,), after=(sum1,))

    c6, back3, back1, side0 = core_hop(d23), z_hop(sum3, -3), z_hop(sum1, -1), x_hop(part0)
    (mark,) = run(
        [(y3, None), (c4, 1), (d23, 0), (c6, 0), (d23, 1), (c6, 1)], last=True
    )
    grad_tokens, grad_combine = finish(
        [(kept0, 0), (came0, 0)] + [(a, None) for a in (side0, back1, back3)],
        ids,
        width,
        after=(mark,),
    )
    return grad_tokens, grad_combine.T, sums[0][None], sums[1][None]


def solution(mesh):
    in_specs = (
        P(("expert", "dp"), None),
        P(("expert", "dp"), None),
        P(("expert", "dp"), None),
        P(("expert", "dp"), None),
        P("expert", None, None),
        P("expert", None, None),
    )
    out_specs = (
        P(("expert", "dp"), None),
        P(("expert", "dp"), None),
        P("expert", "dp", None),
        P("expert", "dp", None),
    )

    def run(tokens, *rest):
        small = tokens.size * 2 <= GATHER_BYTES and mesh.shape["dp"] == 2
        shards = streamed if small and mesh.shape["expert"] == 16 else grouped
        return jax.shard_map(
            shards, mesh=mesh, in_specs=in_specs, out_specs=out_specs, check_vma=False
        )(tokens, *rest)

    return run
```

```python
import functools

import jax
import jax.numpy as jnp
from jax import lax
from jax.experimental import pallas as pl
from jax.experimental.pallas import tpu as pltpu
from jax.sharding import PartitionSpec as P

LANES = 128
CORES = 2
GATHER_BYTES = 16 << 20


def weight_table(expert_ids, combine, experts):
    lanes = jnp.arange(-(-experts // LANES) * LANES, dtype=jnp.int32)
    picks = expert_ids[:, :, None] == lanes
    table = jnp.sum(jnp.where(picks, combine.astype(jnp.float32)[:, :, None], 0.0), axis=1)
    return table.astype(jnp.bfloat16), picks, lanes


def rows_pass(rows, w_in, w_out, me, lanes, with_grad):
    width, hidden = w_out.shape
    tok, cot = rows[:, :width], rows[:, width : 2 * width]
    weight = jnp.sum(
        jnp.where(lanes[None, :] == me, rows[:, 2 * width :].astype(jnp.float32), 0.0),
        axis=1,
        keepdims=True,
    )
    both = jnp.dot(tok, w_in, preferred_element_type=jnp.float32)
    gate, upper = both[:, :hidden], both[:, hidden:]
    sigma = jax.nn.sigmoid(gate)
    swish = gate * sigma
    activ = swish * upper
    cot_down = jnp.dot(cot, w_out, preferred_element_type=jnp.float32)
    grad_act = weight * cot_down
    grad_gate = grad_act * upper * sigma * (1.0 + gate * (1.0 - sigma))
    grad_both = jnp.concatenate([grad_gate, grad_act * swish], axis=1).astype(jnp.bfloat16)
    scaled = (weight * activ).astype(jnp.bfloat16)
    if not with_grad:
        return grad_both, scaled, None
    inner = jnp.sum(activ * cot_down, axis=1, keepdims=True)
    row_grad = lax.dot_general(
        grad_both, w_in, (((1,), (1,)), ((), ())), preferred_element_type=jnp.float32
    ).astype(jnp.bfloat16)
    inner_table = jnp.where(lanes[None, :] == me, inner, 0.0).astype(jnp.bfloat16)
    return grad_both, scaled, jnp.concatenate([row_grad, inner_table], axis=1)


def outer(rows, columns):
    return lax.dot_general(
        rows, columns, (((0,), (0,)), ((), ())), preferred_element_type=jnp.float32
    ).astype(jnp.bfloat16)


def pick_inner(back, picks):
    return jnp.sum(jnp.where(picks, back.astype(jnp.float32)[:, None, :], 0.0), axis=2).astype(
        jnp.bfloat16
    )


def grouped(tokens, cotangent, expert_ids, combine, gate_up, down_proj):
    width = tokens.shape[1]
    me = lax.axis_index("expert")
    table, picks, lanes = weight_table(expert_ids, combine, lax.axis_size("expert"))
    rows = lax.all_gather(
        jnp.concatenate([tokens, cotangent, table], axis=1), "expert", axis=0, tiled=True
    )
    grad_both, scaled, back = rows_pass(rows, gate_up[0], down_proj[0], me, lanes, True)
    back = lax.psum_scatter(back, "expert", scatter_dimension=0, tiled=True)

    def share(term):
        return lax.psum_scatter(term, "dp", scatter_dimension=0, tiled=True)[None]

    return (
        back[:, :width],
        pick_inner(back[:, width:], picks),
        share(outer(rows[:, :width], grad_both)),
        share(outer(rows[:, width : 2 * width], scaled)),
    )


def gate(passed, stacks=(), after=()):
    count = len(passed)
    arrays = list(passed) + list(after)
    places = [
        (g, j, next(i for i, a in enumerate(arrays) if a is member))
        for g, members in enumerate(stacks)
        for j, member in enumerate(members)
    ]

    def kernel(*refs):
        out = refs[len(arrays) + count :]
        copies = [
            pltpu.make_async_copy(refs[i], out[g].at[j], refs[-1].at[n])
            for n, (g, j, i) in enumerate(places)
        ]
        for copy in copies:
            copy.start()
        for copy in copies:
            copy.wait()

    anywhere = pl.BlockSpec(memory_space=pl.ANY)
    shapes = [jax.ShapeDtypeStruct(a.shape, a.dtype) for a in passed]
    shapes += [jax.ShapeDtypeStruct((len(g),) + g[0].shape, g[0].dtype) for g in stacks]
    return pl.pallas_call(
        kernel,
        out_shape=shapes,
        in_specs=[anywhere] * len(arrays),
        out_specs=[anywhere] * count + [pl.BlockSpec(memory_space=pltpu.VMEM)] * len(stacks),
        scratch_shapes=[pltpu.SemaphoreType.DMA((max(1, len(places)),))],
        input_output_aliases={i: i for i in range(count)},
        compiler_params=pltpu.CompilerParams(vmem_limit_bytes=4 << 20),
    )(*arrays)


def add(terms, after=(), dtype=jnp.bfloat16):
    arrays, picks = zip(*terms)
    anywhere = pl.BlockSpec(memory_space=pl.ANY)
    near = pl.BlockSpec(memory_space=pltpu.VMEM)

    def kernel(*refs):
        parts = [ref if k is None else ref.at[k] for ref, k in zip(refs, picks)]
        total = parts[0][...].astype(jnp.float32)
        for part in parts[1:]:
            total += part[...].astype(jnp.float32)
        refs[-1][...] = total.astype(dtype)

    return pl.pallas_call(
        kernel,
        out_shape=jax.ShapeDtypeStruct(arrays[0].shape[-2:], dtype),
        in_specs=[near] * len(arrays) + [anywhere] * len(after),
        compiler_params=pltpu.CompilerParams(vmem_limit_bytes=6 << 20),
    )(*arrays, *after)


def finish(terms, ids, width, after):
    arrays, picks = zip(*terms)
    top, tok_rows = ids.shape
    anywhere = pl.BlockSpec(memory_space=pl.ANY)
    near = pl.BlockSpec(memory_space=pltpu.VMEM)

    def kernel(ids, *refs):
        parts = [ref if k is None else ref.at[k] for ref, k in zip(refs, picks)]
        out, chosen, rows = refs[-3:]
        total = parts[0][...].astype(jnp.float32)
        for part in parts[1:]:
            total += part[...].astype(jnp.float32)
        out[...] = total[:, :width].astype(jnp.bfloat16)
        table = total[:, width:].T
        line = lax.broadcasted_iota(jnp.int32, table.shape, 0)
        for k in range(top):
            picked = jnp.where(line == ids[k : k + 1, :], table, 0.0)
            rows[k : k + 1, :] = jnp.sum(picked, axis=0, keepdims=True)
        chosen[...] = rows[...].astype(jnp.bfloat16)

    return pl.pallas_call(
        kernel,
        out_shape=[
            jax.ShapeDtypeStruct((tok_rows, width), jnp.bfloat16),
            jax.ShapeDtypeStruct((top, tok_rows), jnp.bfloat16),
        ],
        scratch_shapes=[pltpu.VMEM((top, tok_rows), jnp.float32)],
        in_specs=[near] * (1 + len(arrays)) + [anywhere] * len(after),
        compiler_params=pltpu.CompilerParams(vmem_limit_bytes=6 << 20),
    )(ids, *arrays, *after)


def first_rows(tokens, cotangent, ids, combine, experts):
    top, tok_rows = ids.shape
    width = tokens.shape[1]
    extra = -(-experts // LANES) * LANES

    def kernel(tok, cot, ids, combine, out):
        out[:, :width] = tok[...]
        out[:, width : 2 * width] = cot[...]
        line = lax.broadcasted_iota(jnp.int32, (extra, tok_rows), 0)
        share = combine[...].astype(jnp.float32)
        table = jnp.zeros((extra, tok_rows), jnp.float32)
        for k in range(top):
            table += jnp.where(line == ids[k : k + 1, :], share[k : k + 1, :], 0.0)
        out[:, 2 * width :] = table.T.astype(jnp.bfloat16)

    return pl.pallas_call(
        kernel,
        out_shape=jax.ShapeDtypeStruct((tok_rows, 2 * width + extra), jnp.bfloat16),
        compiler_params=pltpu.CompilerParams(vmem_limit_bytes=60 << 20),
    )(tokens, cotangent, ids, combine)


def keep_near(*arrays):
    def kernel(*refs):
        count = len(arrays)
        copies = [
            pltpu.make_async_copy(refs[i], refs[count + i], refs[-1].at[i]) for i in range(count)
        ]
        for copy in copies:
            copy.start()
        for copy in copies:
            copy.wait()

    return pl.pallas_call(
        kernel,
        out_shape=[pltpu.VMEM(a.shape, a.dtype) for a in arrays],
        in_specs=[pl.BlockSpec(memory_space=pltpu.HBM)] * len(arrays),
        out_specs=[pl.BlockSpec(memory_space=pltpu.VMEM)] * len(arrays),
        scratch_shapes=[pltpu.SemaphoreType.DMA((len(arrays),))],
        compiler_params=pltpu.CompilerParams(vmem_limit_bytes=44 << 20),
    )(*arrays)


def slot_kernel(picks, waits, with_grad, first, last, *refs):
    count = len(picks)
    units = [ref if k is None else ref.at[k] for ref, k in zip(refs[:count], picks)]
    win, wout = refs[count : count + 2]
    refs = refs[count + 2 :]
    if not first:
        old_up, old_down = refs[:2]
        refs = refs[2:]
    refs = refs[waits:]
    new_up, new_down = refs[:2]
    refs = refs[2:]
    if with_grad:
        kept, sent = refs[0], refs[1 : 1 + with_grad]
        sent = [sent[0].at[0], sent[0].at[1]] if with_grad == 1 else sent
        refs = refs[1 + with_grad :]
    else:
        refs[0][...] = jnp.zeros_like(refs[0])
        refs = refs[1:]
    tok, cot, both, scaled, tok_t, cot_t, sems = refs[:7]
    refs = refs[7:]
    if last:
        done_up, done_down = refs[:2]

    width, hidden = wout.shape
    tok_rows, wide = units[0].shape
    rows = count * tok_rows
    back_rows = 4 * tok_rows
    spare = tok.shape[0] - rows
    part = tok_t.shape[0]
    me, mine = lax.axis_index("expert"), lax.axis_index("dp")
    for padded in (tok, cot, both, scaled) if spare else ():
        padded[pl.ds(rows, spare), :] = jnp.zeros((spare, padded.shape[1]), jnp.bfloat16)

    weights = []
    for i in range(0, count, 2):
        span = pl.ds(i * tok_rows, 2 * tok_rows)
        for target, start in ((tok, 0), (cot, width)):
            joined = [units[j][:, pl.ds(start, width)].astype(jnp.float32) for j in (i, i + 1)]
            target[span, :] = jnp.concatenate(joined, axis=0).astype(jnp.bfloat16)
        for j in (i, i + 1):
            table = units[j][:, pl.ds(2 * width, wide - 2 * width)].astype(jnp.float32)
            lane = lax.broadcasted_iota(jnp.int32, table.shape, 1)
            weights.append(jnp.sum(jnp.where(lane == me, table, 0.0), axis=1, keepdims=True))
    weight = jnp.concatenate(weights, axis=0)

    real = pl.ds(0, rows)
    step = 256 if hidden % 256 == 0 else hidden
    inner = jnp.zeros((back_rows, 1), jnp.float32)
    for j in range(hidden // step):
        gates, uppers = pl.ds(j * step, step), pl.ds(hidden + j * step, step)
        gate_x = jnp.dot(tok[real, :], win[:, gates], preferred_element_type=jnp.float32)
        upper = jnp.dot(tok[real, :], win[:, uppers], preferred_element_type=jnp.float32)
        cot_down = jnp.dot(cot[real, :], wout[:, gates], preferred_element_type=jnp.float32)
        sigma = 1.0 / (1.0 + jnp.exp(-gate_x))
        swish = gate_x * sigma
        activ = swish * upper
        grad_act = weight * cot_down
        both[real, gates] = (grad_act * upper * sigma * (1.0 + gate_x * (1.0 - sigma))).astype(
            jnp.bfloat16
        )
        both[real, uppers] = (grad_act * swish).astype(jnp.bfloat16)
        scaled[real, gates] = (weight * activ).astype(jnp.bfloat16)
        if with_grad:
            inner += jnp.sum((activ * cot_down)[:back_rows], axis=1, keepdims=True)

    leave = []
    if with_grad:

        def back(columns, value):
            for i in range(4):
                target = sent[i // 2] if i % 2 else kept.at[i // 2]
                target[:, columns] = value[i * tok_rows : (i + 1) * tok_rows].astype(jnp.bfloat16)

        for start in range(0, width, 512):
            span = pl.ds(start, min(512, width - start))
            term = lax.dot_general(
                both[pl.ds(0, back_rows), :],
                win[span, :],
                (((1,), (1,)), ((), ())),
                preferred_element_type=jnp.float32,
            )
            back(span, term)
        lane = lax.broadcasted_iota(jnp.int32, (back_rows, wide - 2 * width), 1)
        back(pl.ds(width, wide - 2 * width), jnp.where(lane == me, inner, 0.0))

    columns = pl.ds(pl.multiple_of(mine * part, part), part)
    tok_t[...] = tok[:, columns].T
    cot_t[...] = cot[:, columns].T
    sides = [
        (tok_t, both, None if first else old_up, new_up, done_up if last else None),
        (cot_t, scaled, None if first else old_down, new_down, done_down if last else None),
    ]
    place = 0
    for left, right, old, new, done in sides:
        for start in range(0, right.shape[1], step):
            span = pl.ds(start, step)
            term = jnp.dot(left[...], right[:, span], preferred_element_type=jnp.float32)
            if not first:
                term += old[:, span]
            if not last:
                new[:, span] = term
                continue
            done[:, span] = term.astype(jnp.bfloat16)
            leave.append(
                pltpu.make_async_copy(done.at[:, span], new.at[:, span], sems.at[place])
            )
            leave[-1].start()
            place += 1
    for copy in leave:
        copy.wait()


def slot_pass(units, win, wout, sums, with_grad, last, after):
    width, hidden = wout.shape
    arrays, picks = zip(*units)
    tok_rows, wide = arrays[0].shape[-2:]
    rows = len(units) * tok_rows
    padded = -(-rows // LANES) * LANES
    part = width // 2
    first = sums is None
    near, far = pl.BlockSpec(memory_space=pltpu.VMEM), pl.BlockSpec(memory_space=pltpu.HBM)
    grads = [(part, 2 * hidden), (part, hidden)]
    if last:
        shapes, specs = [pltpu.HBM(g, jnp.bfloat16) for g in grads], [far, far]
    else:
        shapes, specs = [pltpu.VMEM(g, jnp.float32) for g in grads], [near, near]
    back = (2, tok_rows, wide - width)
    scratch = [
        pltpu.VMEM((padded, width), jnp.bfloat16),
        pltpu.VMEM((padded, width), jnp.bfloat16),
        pltpu.VMEM((padded, 2 * hidden), jnp.bfloat16),
        pltpu.VMEM((padded, hidden), jnp.bfloat16),
        pltpu.VMEM((part, padded), jnp.bfloat16),
        pltpu.VMEM((part, padded), jnp.bfloat16),
        pltpu.SemaphoreType.DMA((3 * hidden // (256 if hidden % 256 == 0 else hidden),)),
    ]
    if with_grad:
        shapes.append(pltpu.VMEM(back, jnp.bfloat16))
        shapes += [pltpu.VMEM(back[with_grad - 1 :], jnp.bfloat16)] * with_grad
        specs += [near] * (1 + with_grad)
    else:
        shapes.append(pltpu.VMEM((8, LANES), jnp.float32))
        specs.append(near)
    if last:
        scratch += [pltpu.VMEM(g, jnp.bfloat16) for g in grads]
    out = pl.pallas_call(
        functools.partial(slot_kernel, picks, len(after), with_grad, first, last),
        out_shape=shapes,
        in_specs=[near] * (len(units) + (2 if first else 4))
        + [pl.BlockSpec(memory_space=pl.ANY)] * len(after),
        out_specs=specs,
        scratch_shapes=scratch,
        input_output_aliases={} if first or last else {len(units) + 2: 0, len(units) + 3: 1},
        compiler_params=pltpu.CompilerParams(vmem_limit_bytes=(18 if last else 14) << 20),
        cost_estimate=pl.CostEstimate(flops=0, bytes_accessed=0, transcendentals=0),
    )(*arrays, win, wout, *(sums or ()), *after)
    return out[:2], out[2:]


def streamed(tokens, cotangent, expert_ids, combine, gate_up, down_proj):
    width = tokens.shape[1]
    experts = lax.axis_size("expert")
    ids = expert_ids.T

    n_x, n_z = 2, experts // CORES // 2

    def place(z, x, core):
        return (z * n_x + x) * CORES + core

    spots = [(z, x, c) for z in range(n_z) for x in range(n_x) for c in range(CORES)]
    ring = [0] + list(range(1, n_z, 2)) + list(range(2, n_z, 2))[::-1]
    by_z = [
        [
            (place(ring[i], x, c), place(ring[(i + far) % n_z], x, c))
            for i in range(n_z)
            for x in range(n_x)
            for c in range(CORES)
        ]
        for far in range(n_z)
    ]
    over_x = [(place(z, x, c), place(z, 1 - x, c)) for z, x, c in spots]
    over_core = [(place(z, x, c), place(z, x, 1 - c)) for z, x, c in spots]

    def z_hop(a, far=1):
        return lax.ppermute(a, "expert", by_z[far % n_z])

    def x_hop(a):
        return lax.ppermute(a, "expert", over_x)

    def core_hop(a):
        return lax.ppermute(a, "expert", over_core)

    def y_hop(a):
        return lax.ppermute(a, "dp", [(0, 1), (1, 0)])

    sums = None
    win, wout = keep_near(gate_up[0], down_proj[0])

    def run(units, with_grad=False, last=False, after=()):
        nonlocal sums
        sums, rest = slot_pass(units, win, wout, sums, with_grad, last, after)
        return rest

    z0 = first_rows(tokens, cotangent, ids, combine.T, experts)
    z1, x0, y0, z0c = z_hop(z0), x_hop(z0), y_hop(z0), core_hop(z0)
    z1, x0, y0, z0c, pile = gate((z1, x0, y0, z0c), stacks=((x0, z1, y0),), after=(win, wout))

    c1, z2, x1, y1 = core_hop(pile), z_hop(z1), x_hop(z1), y_hop(z1)
    kept0, sent0 = run(
        [(z0, None), (z0c, None), (x0, None), (c1, 0), (y0, None), (c1, 2)], with_grad=1
    )
    z2, x1, y1, sent0, pile = gate((z2, x1, y1, sent0), stacks=((x1, z2, y1),))

    c2, z3, x2, y2, came0 = core_hop(pile), z_hop(z2), x_hop(z2), y_hop(z2), core_hop(sent0)
    kept1, sent1 = run(
        [(z1, None), (c1, 1), (x1, None), (c2, 0), (y1, None), (c2, 2)], with_grad=1
    )
    part0 = add([(kept0, 1), (came0, 1)], after=(kept1,))
    z3, x2, y2, sent1, pile = gate((z3, x2, y2, sent1), stacks=((x2, z3, y2),), after=(part0,))

    c3, x3, d0, y3, came1 = core_hop(pile), z_hop(x2), x_hop(y0), y_hop(z3), core_hop(sent1)
    part1 = add([(kept1, 1), (came1, 1)], after=(pile,))
    kept2, sent2 = run(
        [(z2, None), (c2, 1), (x2, None), (c3, 0), (y2, None), (c3, 2)],
        with_grad=1,
        after=(part1,),
    )
    x3, d0, y3, sent2, part0, part1, pile, pair = gate(
        (x3, d0, y3, sent2, part0, part1), stacks=((x3, y3, d0), (x2, x3)), after=(kept2, x2)
    )

    c4, d1, d23, came2 = core_hop(pile), z_hop(d0), y_hop(pair), core_hop(sent2)
    side1 = x_hop(part1)
    part2 = add([(kept2, 1), (came2, 1)], after=(pile,))
    side2 = x_hop(part2)
    kept3, sent3a, sent3b = run(
        [(z3, None), (c3, 1), (x3, None), (c4, 0)], with_grad=2, after=(part2,)
    )
    came3b, came3a = core_hop(sent3b), core_hop(sent3a)
    sum1 = add([(kept1, 0), (came1, 0), (side1, None)], after=(kept3,), dtype=jnp.float32)
    sum2 = add([(kept2, 0), (came2, 0), (side2, None)], after=(sum1,))
    part3 = add([(kept3, 1), (came3b, None)], after=(sum2,))
    (d1,) = gate((d1,), after=(part3,))
    c5, side3 = core_hop(d1), x_hop(part3)
    (mark,) = run([(d0, None), (c4, 2), (d1, None), (c5, None)], after=(d1,))
    sum3 = add([(kept3, 0), (came3a, None), (side3, None)], after=(mark,))
    sum1 = add([(sum1, None), (z_hop(sum2, -1), None)], after=(sum3,))
    (d23,) = gate((d23,), after=(sum1,))

    c6, back3, back1, side0 = core_hop(d23), z_hop(sum3, -3), z_hop(sum1, -1), x_hop(part0)
    (mark,) = run(
        [(y3, None), (c4, 1), (d23, 0), (c6, 0), (d23, 1), (c6, 1)], last=True
    )
    grad_tokens, grad_combine = finish(
        [(kept0, 0), (came0, 0)] + [(a, None) for a in (side0, back1, back3)],
        ids,
        width,
        after=(mark,),
    )
    return grad_tokens, grad_combine.T, sums[0][None], sums[1][None]


def solution(mesh):
    in_specs = (
        P(("expert", "dp"), None),
        P(("expert", "dp"), None),
        P(("expert", "dp"), None),
        P(("expert", "dp"), None),
        P("expert", None, None),
        P("expert", None, None),
    )
    out_specs = (
        P(("expert", "dp"), None),
        P(("expert", "dp"), None),
        P("expert", "dp", None),
        P("expert", "dp", None),
    )

    def run(tokens, *rest):
        small = tokens.size * 2 <= GATHER_BYTES and mesh.shape["dp"] == 2
        shards = streamed if small and mesh.shape["expert"] == 16 else grouped
        return jax.shard_map(
            shards, mesh=mesh, in_specs=in_specs, out_specs=out_specs, check_vma=False
        )(tokens, *rest)

    return run
```

```python
import functools

import jax
import jax.numpy as jnp
from jax import lax
from jax.experimental import pallas as pl
from jax.experimental.pallas import tpu as pltpu
from jax.sharding import PartitionSpec as P

LANES = 128
CORES = 2
GATHER_BYTES = 16 << 20


def weight_table(expert_ids, combine, experts):
    lanes = jnp.arange(-(-experts // LANES) * LANES, dtype=jnp.int32)
    picks = expert_ids[:, :, None] == lanes
    table = jnp.sum(jnp.where(picks, combine.astype(jnp.float32)[:, :, None], 0.0), axis=1)
    return table.astype(jnp.bfloat16), picks, lanes


def rows_pass(rows, w_in, w_out, me, lanes, with_grad):
    width, hidden = w_out.shape
    tok, cot = rows[:, :width], rows[:, width : 2 * width]
    weight = jnp.sum(
        jnp.where(lanes[None, :] == me, rows[:, 2 * width :].astype(jnp.float32), 0.0),
        axis=1,
        keepdims=True,
    )
    both = jnp.dot(tok, w_in, preferred_element_type=jnp.float32)
    gate, upper = both[:, :hidden], both[:, hidden:]
    sigma = jax.nn.sigmoid(gate)
    swish = gate * sigma
    activ = swish * upper
    cot_down = jnp.dot(cot, w_out, preferred_element_type=jnp.float32)
    grad_act = weight * cot_down
    grad_gate = grad_act * upper * sigma * (1.0 + gate * (1.0 - sigma))
    grad_both = jnp.concatenate([grad_gate, grad_act * swish], axis=1).astype(jnp.bfloat16)
    scaled = (weight * activ).astype(jnp.bfloat16)
    if not with_grad:
        return grad_both, scaled, None
    inner = jnp.sum(activ * cot_down, axis=1, keepdims=True)
    row_grad = lax.dot_general(
        grad_both, w_in, (((1,), (1,)), ((), ())), preferred_element_type=jnp.float32
    ).astype(jnp.bfloat16)
    inner_table = jnp.where(lanes[None, :] == me, inner, 0.0).astype(jnp.bfloat16)
    return grad_both, scaled, jnp.concatenate([row_grad, inner_table], axis=1)


def outer(rows, columns):
    return lax.dot_general(
        rows, columns, (((0,), (0,)), ((), ())), preferred_element_type=jnp.float32
    ).astype(jnp.bfloat16)


def pick_inner(back, picks):
    return jnp.sum(jnp.where(picks, back.astype(jnp.float32)[:, None, :], 0.0), axis=2).astype(
        jnp.bfloat16
    )


def grouped(tokens, cotangent, expert_ids, combine, gate_up, down_proj):
    width = tokens.shape[1]
    me = lax.axis_index("expert")
    table, picks, lanes = weight_table(expert_ids, combine, lax.axis_size("expert"))
    rows = lax.all_gather(
        jnp.concatenate([tokens, cotangent, table], axis=1), "expert", axis=0, tiled=True
    )
    grad_both, scaled, back = rows_pass(rows, gate_up[0], down_proj[0], me, lanes, True)
    back = lax.psum_scatter(back, "expert", scatter_dimension=0, tiled=True)

    def share(term):
        return lax.psum_scatter(term, "dp", scatter_dimension=0, tiled=True)[None]

    return (
        back[:, :width],
        pick_inner(back[:, width:], picks),
        share(outer(rows[:, :width], grad_both)),
        share(outer(rows[:, width : 2 * width], scaled)),
    )


def gate(passed, stacks=(), after=()):
    count = len(passed)
    arrays = list(passed) + list(after)
    places = [
        (g, j, next(i for i, a in enumerate(arrays) if a is member))
        for g, members in enumerate(stacks)
        for j, member in enumerate(members)
    ]

    def kernel(*refs):
        out = refs[len(arrays) + count :]
        copies = [
            pltpu.make_async_copy(refs[i], out[g].at[j], refs[-1].at[n])
            for n, (g, j, i) in enumerate(places)
        ]
        for copy in copies:
            copy.start()
        for copy in copies:
            copy.wait()

    anywhere = pl.BlockSpec(memory_space=pl.ANY)
    shapes = [jax.ShapeDtypeStruct(a.shape, a.dtype) for a in passed]
    shapes += [jax.ShapeDtypeStruct((len(g),) + g[0].shape, g[0].dtype) for g in stacks]
    return pl.pallas_call(
        kernel,
        out_shape=shapes,
        in_specs=[anywhere] * len(arrays),
        out_specs=[anywhere] * count + [pl.BlockSpec(memory_space=pltpu.VMEM)] * len(stacks),
        scratch_shapes=[pltpu.SemaphoreType.DMA((max(1, len(places)),))],
        input_output_aliases={i: i for i in range(count)},
        compiler_params=pltpu.CompilerParams(vmem_limit_bytes=4 << 20),
    )(*arrays)


def add(terms, after=(), dtype=jnp.bfloat16):
    arrays, picks = zip(*terms)
    anywhere = pl.BlockSpec(memory_space=pl.ANY)
    near = pl.BlockSpec(memory_space=pltpu.VMEM)

    def kernel(*refs):
        parts = [ref if k is None else ref.at[k] for ref, k in zip(refs, picks)]
        total = parts[0][...].astype(jnp.float32)
        for part in parts[1:]:
            total += part[...].astype(jnp.float32)
        refs[-1][...] = total.astype(dtype)

    return pl.pallas_call(
        kernel,
        out_shape=jax.ShapeDtypeStruct(arrays[0].shape[-2:], dtype),
        in_specs=[near] * len(arrays) + [anywhere] * len(after),
        compiler_params=pltpu.CompilerParams(vmem_limit_bytes=6 << 20),
    )(*arrays, *after)


def finish(terms, ids, width, after):
    arrays, picks = zip(*terms)
    top, tok_rows = ids.shape
    anywhere = pl.BlockSpec(memory_space=pl.ANY)
    near = pl.BlockSpec(memory_space=pltpu.VMEM)

    def kernel(ids, *refs):
        parts = [ref if k is None else ref.at[k] for ref, k in zip(refs, picks)]
        out, chosen, rows = refs[-3:]
        total = parts[0][...].astype(jnp.float32)
        for part in parts[1:]:
            total += part[...].astype(jnp.float32)
        out[...] = total[:, :width].astype(jnp.bfloat16)
        table = total[:, width:].T
        line = lax.broadcasted_iota(jnp.int32, table.shape, 0)
        for k in range(top):
            picked = jnp.where(line == ids[k : k + 1, :], table, 0.0)
            rows[k : k + 1, :] = jnp.sum(picked, axis=0, keepdims=True)
        chosen[...] = rows[...].astype(jnp.bfloat16)

    return pl.pallas_call(
        kernel,
        out_shape=[
            jax.ShapeDtypeStruct((tok_rows, width), jnp.bfloat16),
            jax.ShapeDtypeStruct((top, tok_rows), jnp.bfloat16),
        ],
        scratch_shapes=[pltpu.VMEM((top, tok_rows), jnp.float32)],
        in_specs=[near] * (1 + len(arrays)) + [anywhere] * len(after),
        compiler_params=pltpu.CompilerParams(vmem_limit_bytes=6 << 20),
    )(ids, *arrays, *after)


def first_rows(tokens, cotangent, ids, combine, experts):
    top, tok_rows = ids.shape
    width = tokens.shape[1]
    extra = -(-experts // LANES) * LANES

    def kernel(tok, cot, ids, combine, out):
        out[:, :width] = tok[...]
        out[:, width : 2 * width] = cot[...]
        line = lax.broadcasted_iota(jnp.int32, (extra, tok_rows), 0)
        share = combine[...].astype(jnp.float32)
        table = jnp.zeros((extra, tok_rows), jnp.float32)
        for k in range(top):
            table += jnp.where(line == ids[k : k + 1, :], share[k : k + 1, :], 0.0)
        out[:, 2 * width :] = table.T.astype(jnp.bfloat16)

    return pl.pallas_call(
        kernel,
        out_shape=jax.ShapeDtypeStruct((tok_rows, 2 * width + extra), jnp.bfloat16),
        compiler_params=pltpu.CompilerParams(vmem_limit_bytes=60 << 20),
    )(tokens, cotangent, ids, combine)


def keep_near(*arrays):
    def kernel(*refs):
        count = len(arrays)
        copies = [
            pltpu.make_async_copy(refs[i], refs[count + i], refs[-1].at[i]) for i in range(count)
        ]
        for copy in copies:
            copy.start()
        for copy in copies:
            copy.wait()

    return pl.pallas_call(
        kernel,
        out_shape=[pltpu.VMEM(a.shape, a.dtype) for a in arrays],
        in_specs=[pl.BlockSpec(memory_space=pltpu.HBM)] * len(arrays),
        out_specs=[pl.BlockSpec(memory_space=pltpu.VMEM)] * len(arrays),
        scratch_shapes=[pltpu.SemaphoreType.DMA((len(arrays),))],
        compiler_params=pltpu.CompilerParams(vmem_limit_bytes=44 << 20),
    )(*arrays)


def slot_kernel(picks, waits, with_grad, first, last, *refs):
    count = len(picks)
    units = [ref if k is None else ref.at[k] for ref, k in zip(refs[:count], picks)]
    win, wout = refs[count : count + 2]
    refs = refs[count + 2 :]
    if not first:
        old_up, old_down = refs[:2]
        refs = refs[2:]
    refs = refs[waits:]
    new_up, new_down = refs[:2]
    refs = refs[2:]
    if with_grad:
        kept, sent = refs[0], refs[1 : 1 + with_grad]
        sent = [sent[0].at[0], sent[0].at[1]] if with_grad == 1 else sent
        refs = refs[1 + with_grad :]
    else:
        refs[0][...] = jnp.zeros_like(refs[0])
        refs = refs[1:]
    tok, cot, both, scaled, tok_t, cot_t, sems = refs[:7]
    refs = refs[7:]
    if last:
        done_up, done_down = refs[:2]

    width, hidden = wout.shape
    tok_rows, wide = units[0].shape
    rows = count * tok_rows
    back_rows = 4 * tok_rows
    spare = tok.shape[0] - rows
    part = tok_t.shape[0]
    me, mine = lax.axis_index("expert"), lax.axis_index("dp")
    for padded in (tok, cot, both, scaled) if spare else ():
        padded[pl.ds(rows, spare), :] = jnp.zeros((spare, padded.shape[1]), jnp.bfloat16)

    weights = []
    for i in range(0, count, 2):
        span = pl.ds(i * tok_rows, 2 * tok_rows)
        for target, start in ((tok, 0), (cot, width)):
            joined = [units[j][:, pl.ds(start, width)].astype(jnp.float32) for j in (i, i + 1)]
            target[span, :] = jnp.concatenate(joined, axis=0).astype(jnp.bfloat16)
        for j in (i, i + 1):
            table = units[j][:, pl.ds(2 * width, wide - 2 * width)].astype(jnp.float32)
            lane = lax.broadcasted_iota(jnp.int32, table.shape, 1)
            weights.append(jnp.sum(jnp.where(lane == me, table, 0.0), axis=1, keepdims=True))
    weight = jnp.concatenate(weights, axis=0)

    real = pl.ds(0, rows)
    step = 256 if hidden % 256 == 0 else hidden
    inner = jnp.zeros((back_rows, 1), jnp.float32)
    for j in range(hidden // step):
        gates, uppers = pl.ds(j * step, step), pl.ds(hidden + j * step, step)
        gate_x = jnp.dot(tok[real, :], win[:, gates], preferred_element_type=jnp.float32)
        upper = jnp.dot(tok[real, :], win[:, uppers], preferred_element_type=jnp.float32)
        cot_down = jnp.dot(cot[real, :], wout[:, gates], preferred_element_type=jnp.float32)
        sigma = 1.0 / (1.0 + jnp.exp(-gate_x))
        swish = gate_x * sigma
        activ = swish * upper
        grad_act = weight * cot_down
        both[real, gates] = (grad_act * upper * sigma * (1.0 + gate_x * (1.0 - sigma))).astype(
            jnp.bfloat16
        )
        both[real, uppers] = (grad_act * swish).astype(jnp.bfloat16)
        scaled[real, gates] = (weight * activ).astype(jnp.bfloat16)
        if with_grad:
            inner += jnp.sum((activ * cot_down)[:back_rows], axis=1, keepdims=True)

    leave = []
    if with_grad:

        def back(columns, value):
            for i in range(4):
                target = sent[i // 2] if i % 2 else kept.at[i // 2]
                target[:, columns] = value[i * tok_rows : (i + 1) * tok_rows].astype(jnp.bfloat16)

        for start in range(0, width, 512):
            span = pl.ds(start, min(512, width - start))
            term = lax.dot_general(
                both[pl.ds(0, back_rows), :],
                win[span, :],
                (((1,), (1,)), ((), ())),
                preferred_element_type=jnp.float32,
            )
            back(span, term)
        lane = lax.broadcasted_iota(jnp.int32, (back_rows, wide - 2 * width), 1)
        back(pl.ds(width, wide - 2 * width), jnp.where(lane == me, inner, 0.0))

    columns = pl.ds(pl.multiple_of(mine * part, part), part)
    tok_t[...] = tok[:, columns].T
    cot_t[...] = cot[:, columns].T
    sides = [
        (tok_t, both, None if first else old_up, new_up, done_up if last else None),
        (cot_t, scaled, None if first else old_down, new_down, done_down if last else None),
    ]
    place = 0
    for left, right, old, new, done in sides:
        for start in range(0, right.shape[1], step):
            span = pl.ds(start, step)
            term = jnp.dot(left[...], right[:, span], preferred_element_type=jnp.float32)
            if not first:
                term += old[:, span]
            if not last:
                new[:, span] = term
                continue
            done[:, span] = term.astype(jnp.bfloat16)
            leave.append(
                pltpu.make_async_copy(done.at[:, span], new.at[:, span], sems.at[place])
            )
            leave[-1].start()
            place += 1
    for copy in leave:
        copy.wait()


def slot_pass(units, win, wout, sums, with_grad, last, after):
    width, hidden = wout.shape
    arrays, picks = zip(*units)
    tok_rows, wide = arrays[0].shape[-2:]
    rows = len(units) * tok_rows
    padded = -(-rows // LANES) * LANES
    part = width // 2
    first = sums is None
    near, far = pl.BlockSpec(memory_space=pltpu.VMEM), pl.BlockSpec(memory_space=pltpu.HBM)
    grads = [(part, 2 * hidden), (part, hidden)]
    if last:
        shapes, specs = [pltpu.HBM(g, jnp.bfloat16) for g in grads], [far, far]
    else:
        shapes, specs = [pltpu.VMEM(g, jnp.float32) for g in grads], [near, near]
    back = (2, tok_rows, wide - width)
    scratch = [
        pltpu.VMEM((padded, width), jnp.bfloat16),
        pltpu.VMEM((padded, width), jnp.bfloat16),
        pltpu.VMEM((padded, 2 * hidden), jnp.bfloat16),
        pltpu.VMEM((padded, hidden), jnp.bfloat16),
        pltpu.VMEM((part, padded), jnp.bfloat16),
        pltpu.VMEM((part, padded), jnp.bfloat16),
        pltpu.SemaphoreType.DMA((3 * hidden // (256 if hidden % 256 == 0 else hidden),)),
    ]
    if with_grad:
        shapes.append(pltpu.VMEM(back, jnp.bfloat16))
        shapes += [pltpu.VMEM(back[with_grad - 1 :], jnp.bfloat16)] * with_grad
        specs += [near] * (1 + with_grad)
    else:
        shapes.append(pltpu.VMEM((8, LANES), jnp.float32))
        specs.append(near)
    if last:
        scratch += [pltpu.VMEM(g, jnp.bfloat16) for g in grads]
    out = pl.pallas_call(
        functools.partial(slot_kernel, picks, len(after), with_grad, first, last),
        out_shape=shapes,
        in_specs=[near] * (len(units) + (2 if first else 4))
        + [pl.BlockSpec(memory_space=pl.ANY)] * len(after),
        out_specs=specs,
        scratch_shapes=scratch,
        input_output_aliases={} if first or last else {len(units) + 2: 0, len(units) + 3: 1},
        compiler_params=pltpu.CompilerParams(vmem_limit_bytes=(18 if last else 14) << 20),
        cost_estimate=pl.CostEstimate(flops=0, bytes_accessed=0, transcendentals=0),
    )(*arrays, win, wout, *(sums or ()), *after)
    return out[:2], out[2:]


def streamed(tokens, cotangent, expert_ids, combine, gate_up, down_proj):
    width = tokens.shape[1]
    experts = lax.axis_size("expert")
    ids = expert_ids.T

    n_x, n_z = 2, experts // CORES // 2

    def place(z, x, core):
        return (z * n_x + x) * CORES + core

    spots = [(z, x, c) for z in range(n_z) for x in range(n_x) for c in range(CORES)]
    ring = [0] + list(range(1, n_z, 2)) + list(range(2, n_z, 2))[::-1]
    by_z = [
        [
            (place(ring[i], x, c), place(ring[(i + far) % n_z], x, c))
            for i in range(n_z)
            for x in range(n_x)
            for c in range(CORES)
        ]
        for far in range(n_z)
    ]
    over_x = [(place(z, x, c), place(z, 1 - x, c)) for z, x, c in spots]
    over_core = [(place(z, x, c), place(z, x, 1 - c)) for z, x, c in spots]

    def z_hop(a, far=1):
        return lax.ppermute(a, "expert", by_z[far % n_z])

    def x_hop(a):
        return lax.ppermute(a, "expert", over_x)

    def core_hop(a):
        return lax.ppermute(a, "expert", over_core)

    def y_hop(a):
        return lax.ppermute(a, "dp", [(0, 1), (1, 0)])

    sums = None
    win, wout = keep_near(gate_up[0], down_proj[0])

    def run(units, with_grad=False, last=False, after=()):
        nonlocal sums
        sums, rest = slot_pass(units, win, wout, sums, with_grad, last, after)
        return rest

    z0 = first_rows(tokens, cotangent, ids, combine.T, experts)
    z1, x0, y0, z0c = z_hop(z0), x_hop(z0), y_hop(z0), core_hop(z0)
    z1, x0, y0, z0c, pile = gate((z1, x0, y0, z0c), stacks=((x0, z1, y0),), after=(win, wout))

    c1, z2, x1, y1 = core_hop(pile), z_hop(z1), x_hop(z1), y_hop(z1)
    kept0, sent0 = run(
        [(z0, None), (z0c, None), (x0, None), (c1, 0), (y0, None), (c1, 2)], with_grad=1
    )
    z2, x1, y1, sent0, pile = gate((z2, x1, y1, sent0), stacks=((x1, z2, y1),))

    c2, y2, x2, z3, came0 = core_hop(pile), y_hop(z2), x_hop(z2), z_hop(z2), core_hop(sent0)
    kept1, sent1 = run(
        [(z1, None), (c1, 1), (x1, None), (c2, 0), (y1, None), (c2, 2)], with_grad=1
    )
    part0 = add([(kept0, 1), (came0, 1)], after=(kept1,))
    y2, x2, z3, sent1, pile = gate((y2, x2, z3, sent1), stacks=((x2, z3, y2),), after=(part0,))

    c3, x3, d0, y3, came1 = core_hop(pile), z_hop(x2), x_hop(y0), y_hop(z3), core_hop(sent1)
    part1 = add([(kept1, 1), (came1, 1)], after=(pile,))
    kept2, sent2 = run(
        [(z2, None), (c2, 1), (x2, None), (c3, 0), (y2, None), (c3, 2)],
        with_grad=1,
        after=(part1,),
    )
    x3, d0, y3, sent2, part0, part1, pile, pair = gate(
        (x3, d0, y3, sent2, part0, part1), stacks=((x3, y3, d0), (x2, x3)), after=(kept2, x2)
    )

    c4, d1, d23, came2 = core_hop(pile), z_hop(d0), y_hop(pair), core_hop(sent2)
    side1 = x_hop(part1)
    part2 = add([(kept2, 1), (came2, 1)], after=(pile,))
    side2 = x_hop(part2)
    kept3, sent3a, sent3b = run(
        [(z3, None), (c3, 1), (x3, None), (c4, 0)], with_grad=2, after=(part2,)
    )
    came3b, came3a = core_hop(sent3b), core_hop(sent3a)
    sum1 = add([(kept1, 0), (came1, 0), (side1, None)], after=(kept3,), dtype=jnp.float32)
    sum2 = add([(kept2, 0), (came2, 0), (side2, None)], after=(sum1,))
    part3 = add([(kept3, 1), (came3b, None)], after=(sum2,))
    (d1,) = gate((d1,), after=(part3,))
    c5, side3 = core_hop(d1), x_hop(part3)
    (mark,) = run([(d0, None), (c4, 2), (d1, None), (c5, None)], after=(d1,))
    sum3 = add([(kept3, 0), (came3a, None), (side3, None)], after=(mark,))
    sum1 = add([(sum1, None), (z_hop(sum2, -1), None)], after=(sum3,))
    (d23,) = gate((d23,), after=(sum1,))

    c6, back3, back1, side0 = core_hop(d23), z_hop(sum3, -3), z_hop(sum1, -1), x_hop(part0)
    (mark,) = run(
        [(y3, None), (c4, 1), (d23, 0), (c6, 0), (d23, 1), (c6, 1)], last=True
    )
    grad_tokens, grad_combine = finish(
        [(kept0, 0), (came0, 0)] + [(a, None) for a in (side0, back1, back3)],
        ids,
        width,
        after=(mark,),
    )
    return grad_tokens, grad_combine.T, sums[0][None], sums[1][None]


def solution(mesh):
    in_specs = (
        P(("expert", "dp"), None),
        P(("expert", "dp"), None),
        P(("expert", "dp"), None),
        P(("expert", "dp"), None),
        P("expert", None, None),
        P("expert", None, None),
    )
    out_specs = (
        P(("expert", "dp"), None),
        P(("expert", "dp"), None),
        P("expert", "dp", None),
        P("expert", "dp", None),
    )

    def run(tokens, *rest):
        small = tokens.size * 2 <= GATHER_BYTES and mesh.shape["dp"] == 2
        shards = streamed if small and mesh.shape["expert"] == 16 else grouped
        return jax.shard_map(
            shards, mesh=mesh, in_specs=in_specs, out_specs=out_specs, check_vma=False
        )(tokens, *rest)

    return run
```
